32 devices in a mesh: groups: 2 (over y), tiles: 4 (over z), split: 2 (over x), depth: 2 (over core).
Axes of the slice: x: 2, y: 2, z: 4, core: 2. Of those that a mesh axis runs over, the one named last changes fastest.
Arguments:
- tile_codes: bfloat16 [2048, 256, 256], P(('groups', 'tiles', 'split', 'depth')), parts along dimension 0, may hold values from -127 to 127, as said below
- tile_scale: float32 [2048], P(('groups', 'tiles', 'split', 'depth')), parts along dimension 0, may hold values from 9.375e-05 to 0.00078125
- tile_row: int32 [2048], P(('groups', 'tiles', 'split', 'depth')), parts along dimension 0, may hold values from 0 to 15
- tile_column: int32 [2048], P(('groups', 'tiles', 'split', 'depth')), parts along dimension 0, may hold values from 0 to 11, as said below
- send_index: int32 [32, 4, 2], P(('groups', 'tiles', 'split', 'depth')), parts along dimension 0, may hold values from 0 to 3
- model_start: float32 [128, 256], P(('groups', 'tiles', 'split', 'depth')), parts along dimension 0, may hold values from -6 to 6
- reg_weight: float32 [128, 256], P(('groups', 'tiles', 'split', 'depth')), parts along dimension 0, may hold values from 0.05 to 1
- observed: float32 [128, 256], P(('groups', 'tiles')), parts along dimension 0, may hold values from -6 to 6
- data_weight: float32 [128, 256], P(('groups', 'tiles')), parts along dimension 0, may hold values from 0.5 to 2
Outputs:
- model: float32 [128, 256], P(('groups', 'tiles', 'split', 'depth')), parts along dimension 0
- residual: float32 [128, 256], P(('groups', 'tiles', 'split', 'depth')), parts along dimension 0
The draws below stay inside these ranges and needn't reach their ends.
There are 2 independent parts, one for each index of `groups`. The reference program is written for one: setup_inputs(seed, part) draws one part's arguments, and reference() takes and returns one part's arrays. A program takes and returns all parts, laid end to end along the dimension named above; each array names one. Nothing has to cross between parts.
Inputs may be any that keep to these rules, and one draw needn't show every extreme that they name: `tile_column`: below 4 a position names a block of the device itself; position c >= 4 names slot (c - 4) % 2 of what map tile (c - 4) // 2 sends from the device with the same split and depth index. Every position is named on every device. `send_index`: entry [d, t, j] is the block of device d's own 4 blocks placed in slot j of what d sends to map tile t. `tile_codes`: each value is an integer.
All inputs are finite; a program needn't handle non-finite values.
Results may differ from the reference program's by a relative error of at most 0.0088.
Values may be sent and summed in bfloat16 or wider, within the bound.
No kernel may reach another device: no remote copies, remote signals or barrier semaphores. Data moves between devices by JAX's collectives and lax.ppermute only.
A program may use at most 64 MiB of HBM per device.

```python
import math
import jax
import jax.numpy as jnp
from jax import lax

B = 256
KT = 64
MB_DEV = 4
ROW_BLOCKS = 16
SLOT = 2
ITERS = 2
DEVS_PART = 16
TILE_ALL = 1024
MBLOCKS = 64
DBLOCKS = 64
NBUF = 12
N_TILES = 4


def draw_tile_codes(key, part):
    key = jax.random.fold_in(key, 11)
    values = jax.random.randint(key, (TILE_ALL, B, B), -127, 128)
    return values.astype(jnp.float32).astype(jnp.bfloat16)


def draw_tile_column(key, part):
    key = jax.random.fold_in(key, 23)
    devices = TILE_ALL // KT
    first_key, rest_key = jax.random.split(key)
    keys = jax.random.split(first_key, devices)
    covered = jax.vmap(lambda single: jax.random.permutation(single, NBUF))(keys).astype(jnp.int32)
    extra = jax.random.randint(rest_key, (devices, KT - NBUF), 0, NBUF).astype(jnp.int32)
    return jnp.concatenate([covered, extra], axis=1).reshape(-1)


def plant(drawn, own_key, smallest, high):
    longest = drawn.shape.index(max(drawn.shape))
    spots = []
    for shift in (0, 1):
        where = [jax.random.randint(jax.random.fold_in(own_key, axis), (), 0, length) for axis, length in enumerate(drawn.shape)]
        where[longest] = (where[longest] + shift) % drawn.shape[longest]
        spots.append(tuple(where))
    return drawn.at[spots[0]].set(smallest).at[spots[1]].set(high)


def level_of(key, shape, shards, low, largest):
    def one(dim, shards_of):
        draws = jax.random.uniform(jax.random.fold_in(jax.random.fold_in(key, 6), dim), (shards_of,), jnp.float32, low / len(shards), largest / len(shards))
        return jnp.repeat(jnp.exp(draws), shape[dim] // shards_of).reshape((-1,) + (1,) * (len(shape) - dim - 1))

    gain = one(*shards[0])
    for cut in shards[1:]:
        gain = gain * one(*cut)
    return gain


def scatter_about(rng, extent, width, most, shards=(), held_as=jnp.bfloat16):
    values = jax.random.normal(rng, extent, jnp.float32) * width
    if len(shards) > 0:
        values = level_of(rng, extent, shards, -0.22, 0.18) * values
    return jnp.clip(values, min=-most, max=most).astype(held_as)


def setup_inputs(seed: int = 0, part: int = 0) -> dict:
    key_list = jax.random.split(jax.random.key(seed), 10)
    own_keys = jax.random.split(jax.random.fold_in(key_list[9], part), 10)
    return {
        "tile_codes": draw_tile_codes(jax.random.fold_in(jax.random.fold_in(key_list[9], part), 71), part),
        "tile_scale": jnp.clip(jnp.exp(math.log(0.00078125) - 2.1202635 * jax.random.uniform(own_keys[1], (TILE_ALL,), jnp.float32) ** level_of(own_keys[1], (TILE_ALL,), ((0, 16),), -0.2, 0.2)), 9.375000081490725e-05, 0.00078125),
        "tile_row": plant(jax.random.randint(own_keys[2], (TILE_ALL,), 0, ROW_BLOCKS), jax.random.fold_in(own_keys[2], 1), 0, ROW_BLOCKS - 1).astype(jnp.int32),
        "tile_column": draw_tile_column(jax.random.fold_in(jax.random.fold_in(key_list[9], part), 71), part),
        "send_index": plant(jax.random.randint(own_keys[4], (DEVS_PART, N_TILES, SLOT), 0, MB_DEV), jax.random.fold_in(own_keys[4], 1), 0, MB_DEV - 1).astype(jnp.int32),
        "model_start": scatter_about(own_keys[5], (MBLOCKS, B), 1.0, 6.0, ((0, 16),), jnp.float32),
        "reg_weight": jnp.clip(jnp.exp(math.log(1.0) - 2.9957323 * jax.random.uniform(own_keys[6], (MBLOCKS, B), jnp.float32) ** level_of(own_keys[6], (MBLOCKS, B), ((0, 16),), -0.2, 0.2)), 0.05, 1.0),
        "observed": scatter_about(own_keys[7], (DBLOCKS, B), 1.0, 6.0, ((0, 4),), jnp.float32),
        "data_weight": jnp.clip(jnp.exp(math.log(2.0) - 1.3862944 * jax.random.uniform(own_keys[8], (DBLOCKS, B), jnp.float32) ** level_of(own_keys[8], (DBLOCKS, B), ((0, 4),), -0.2, 0.2)), 0.5, 2.0),
    }


HIGH = lax.Precision.HIGHEST


def placements(tile_row, tile_column, send_index):
    devices = send_index.shape[0]
    per_owner = devices // N_TILES
    device = jnp.repeat(jnp.arange(devices, dtype=jnp.int32), KT)
    owner = device // per_owner
    within = device % per_owner
    far_pos = jnp.maximum(tile_column - MB_DEV, 0).astype(jnp.int32)
    sender = ((far_pos // SLOT) * per_owner + within).astype(jnp.int32)
    remote = send_index[sender, owner, far_pos % SLOT]
    source = jnp.where(tile_column < MB_DEV, device * MB_DEV + tile_column, sender * MB_DEV + remote).astype(jnp.int32)
    target = (owner * ROW_BLOCKS + tile_row).astype(jnp.int32)
    return source, target


def reference(tile_codes, tile_scale, tile_row, tile_column, send_index, model_start, reg_weight, observed, data_weight):
    devices = send_index.shape[0]
    block_size = tile_codes.shape[1]
    source, target = placements(tile_row, tile_column, send_index)
    codes = tile_codes.reshape(devices, KT, block_size, block_size)
    scales = tile_scale.reshape(devices, KT)
    source_dev = source.reshape(devices, KT)
    target_dev = target.reshape(devices, KT)

    def forward(field):
        rounded = field.astype(jnp.bfloat16)

        def one_device(items):
            codes_dev, scale_dev, index_dev = items
            picked = rounded[index_dev].astype(jnp.float32)
            values = jnp.einsum("kij,kj->ki", codes_dev.astype(jnp.float32), picked, precision=HIGH)
            return values * scale_dev[:, None]

        terms = lax.map(one_device, (codes, scales, source_dev))
        return jax.ops.segment_sum(terms.reshape(-1, block_size), target, num_segments=observed.shape[0])

    def adjoint(weighted):
        def one_device(items):
            codes_dev, scale_dev, index_dev = items
            picked = weighted[index_dev].astype(jnp.float32)
            values = jnp.einsum("kij,ki->kj", codes_dev.astype(jnp.float32), picked, precision=HIGH)
            return values * scale_dev[:, None]

        terms = lax.map(one_device, (codes, scales, target_dev))
        return jax.ops.segment_sum(terms.reshape(-1, block_size), source, num_segments=model_start.shape[0])

    def weigh(predicted, offset):
        return (data_weight * (offset - predicted)).astype(jnp.bfloat16)

    zeros_data = jnp.zeros_like(observed)
    start_data = weigh(forward(model_start), observed)
    residual = adjoint(start_data) - reg_weight * model_start
    direction = residual
    model = model_start
    norm_now = jnp.sum(residual * residual)
    for step in range(ITERS):
        image_data = weigh(forward(direction), zeros_data)
        image = reg_weight * direction - adjoint(image_data)
        alpha = norm_now / jnp.sum(direction * image)
        model = model + alpha * direction
        residual = residual - alpha * image
        norm_next = jnp.sum(residual * residual)
        direction = residual + (norm_next / norm_now) * direction
        norm_now = norm_next
    return model, residual
```

```python
import functools

import jax
import jax.numpy as jnp
from jax import lax
from jax.experimental import pallas as pl
from jax.experimental.pallas import tpu as pltpu
from jax.sharding import PartitionSpec as P

HIGH = lax.Precision.HIGHEST
EXTRA = 8
GROUP = 16
F32 = jnp.float32
BF16 = jnp.bfloat16


def exchange(value, axes, size):
    parts = [value]
    for shift in range(1, size):
        perm = [(i, i ^ shift) for i in range(size)]
        parts.append(lax.ppermute(value, axes, perm))
    return parts


def total_rows(parts):
    total = parts[0][...]
    for part in parts[1:]:
        total = total + part[...]
    return total


def total_blocks(parts, blocks):
    count = len(parts)
    groups = []
    for group in range(count):
        total = None
        for shift in range(count):
            start = (group ^ shift) * blocks
            piece = parts[shift][start : start + blocks, :]
            total = piece if total is None else total + piece
        groups.append(total)
    return jnp.concatenate(groups, axis=0)


def extra_rows(parts, start):
    total = parts[0][start : start + EXTRA, :]
    for part in parts[1:]:
        total = total + part[start : start + EXTRA, :]
    return total


def whole(value):
    return jnp.sum(value, axis=(0, 1), keepdims=True)


def columns(value):
    return jnp.sum(value, axis=0, keepdims=True)


def pack_rows(rows, width):
    filled = list(rows)
    while len(filled) < EXTRA:
        filled.append(jnp.zeros((1, width), F32))
    return jnp.concatenate(filled, axis=0)


def products(codes, picked, adjoint):
    tiles = picked.shape[0]
    dims = (((1,), (0,)), ((), ())) if adjoint else (((1,), (1,)), ((), ()))
    pieces = []
    for first in range(0, tiles, GROUP):
        rows = picked[first : first + GROUP, :]
        index = lax.broadcasted_iota(jnp.int32, (GROUP, codes.shape[1]), 0)
        total = None
        for i in range(GROUP):
            value = lax.dot_general(rows, codes[first + i], dims, preferred_element_type=F32)
            total = value if total is None else jnp.where(index == i, value, total)
        pieces.append(total)
    return jnp.concatenate(pieces, axis=0)


def pick(table, values):
    return lax.dot_general(
        table, values, (((0,), (0,)), ((), ())), preferred_element_type=F32
    ).astype(BF16)


def gather(table, terms):
    return jnp.dot(table, terms, precision=HIGH, preferred_element_type=F32)


def first_kernel(blocks, slots, count, *refs):
    codes, scale, row, column, place = refs[:5]
    parts = refs[5 : 5 + count]
    out, rows_one, rows_scaled, source_one, source_scaled, start, weight = refs[5 + count :]
    tiles = scale.shape[1]
    width = out.shape[1]
    data_rows = out.shape[0]
    here = place[0]
    columns_of = column[...]
    source = jnp.where(columns_of < blocks, columns_of, 0)
    lane = lax.broadcasted_iota(jnp.int32, (1, width), 1)
    for shift in range(count):
        other = jnp.bitwise_xor(here, shift)
        named = parts[shift][2 * blocks : 2 * blocks + 1, :]
        for slot in range(slots):
            mine = jnp.where(lane == here * slots + slot, named, 0.0)
            block = jnp.sum(mine, axis=1, keepdims=True).astype(jnp.int32) + shift * blocks
            source = jnp.where(columns_of == blocks + other * slots + slot, block, source)
    scales = scale[...]
    table = lax.broadcasted_iota(jnp.int32, (data_rows, tiles), 0) == row[...]
    rows_one[...] = jnp.where(table, 1.0, 0.0).astype(BF16)
    rows_scaled[...] = jnp.where(table, scales, 0.0)
    table = lax.broadcasted_iota(jnp.int32, (count * blocks, tiles), 0) == source
    ones = jnp.where(table, 1.0, 0.0).astype(BF16)
    source_one[...] = ones
    source_scaled[...] = jnp.where(table, scales, 0.0)
    field = jnp.concatenate([part[:blocks, :] for part in parts], axis=0)
    start[...] = field
    weight[...] = jnp.concatenate([part[blocks : 2 * blocks, :] for part in parts], axis=0)
    terms = products(codes, pick(ones, field.astype(BF16)), False)
    out[...] = gather(rows_scaled[...], terms)


def start_data_kernel(count, *refs):
    codes, rows_one, source_scaled, observed, data_weight = refs[:5]
    parts = refs[5 : 5 + count]
    out = refs[5 + count]
    total = total_rows(parts)
    data = (data_weight[...] * (observed[...] - total)).astype(BF16)
    terms = products(codes, pick(rows_one[...], data), True)
    out[...] = gather(source_scaled[...], terms)


def start_residual_kernel(blocks, count, *refs):
    codes, source_one, rows_scaled, start, weight = refs[:5]
    parts = refs[5 : 5 + count]
    out, residual = refs[5 + count :]
    weights = weight[...]
    value = total_blocks(parts, blocks) - weights * start[...]
    residual[...] = value
    terms = products(codes, pick(source_one[...], value.astype(BF16)), False)
    data_rows = rows_scaled.shape[0]
    out[:data_rows, :] = gather(rows_scaled[...], terms)
    out[data_rows:, :] = pack_rows(
        [columns(value * value), columns(value * weights * value)], value.shape[1]
    )


def image_data_kernel(count, *refs):
    codes, rows_one, source_scaled, data_weight = refs[:4]
    parts = refs[4 : 4 + count]
    out, predicted, sums = refs[4 + count :]
    data_rows = data_weight.shape[0]
    whole_part = total_rows(parts)
    total = whole_part[:data_rows, :]
    predicted[...] = total
    sums[...] = whole_part[data_rows:, :]
    data = (data_weight[...] * (0.0 - total)).astype(BF16)
    terms = products(codes, pick(rows_one[...], data), True)
    cells = source_scaled.shape[0]
    out[:cells, :] = gather(source_scaled[...], terms)
    out[cells:, :] = pack_rows([columns(total * data.astype(F32))], total.shape[1])


def residual_kernel(blocks, count, *refs):
    codes, source_one, rows_scaled, weight, direction, sums = refs[:6]
    parts = refs[6 : 6 + count]
    out, residual, step = refs[6 + count :]
    cells = source_one.shape[0]
    weights = weight[...]
    along = direction[...]
    image = weights * along - total_blocks(parts, blocks)
    curve = whole(sums[1:2, :]) - whole(extra_rows(parts, cells)[0:1, :])
    alpha = whole(sums[0:1, :]) / curve
    step[...] = jnp.broadcast_to(alpha, step.shape)
    value = residual_of(along, alpha, image)
    residual[...] = value
    terms = products(codes, pick(source_one[...], value.astype(BF16)), False)
    data_rows = rows_scaled.shape[0]
    out[:data_rows, :] = gather(rows_scaled[...], terms)
    weighted = value * weights
    out[data_rows:, :] = pack_rows(
        [columns(value * value), columns(weighted * value), columns(weighted * along)],
        value.shape[1],
    )


def residual_of(residual, alpha, image):
    return residual - alpha * image


def second_data_kernel(count, *refs):
    codes, rows_one, source_scaled, data_weight, predicted, sums = refs[:6]
    parts = refs[6 : 6 + count]
    out, scalars = refs[6 + count :]
    data_rows = data_weight.shape[0]
    whole_part = total_rows(parts)
    norm = whole(whole_part[data_rows : data_rows + 1, :])
    beta = norm / whole(sums[0:1, :])
    curve = whole(
        whole_part[data_rows + 1 : data_rows + 2, :]
        + 2.0 * beta * whole_part[data_rows + 2 : data_rows + 3, :]
        + beta * beta * sums[1:2, :]
    )
    total = whole_part[:data_rows, :] + beta * predicted[...]
    data = (data_weight[...] * (0.0 - total)).astype(BF16)
    terms = products(codes, pick(rows_one[...], data), True)
    cells = source_scaled.shape[0]
    out[:cells, :] = gather(source_scaled[...], terms)
    out[cells:, :] = pack_rows([columns(total * data.astype(F32))], total.shape[1])
    wide = (1, scalars.shape[1])
    scalars[...] = pack_rows(
        [jnp.broadcast_to(value, wide) for value in (norm, beta, curve)], scalars.shape[1]
    )


def last_kernel(blocks, count, *refs):
    weight, start, first, second, step, scalars = refs[:6]
    parts = refs[6 : 6 + count]
    model, residual = refs[6 + count :]
    cells = weight.shape[0]
    norm = scalars[0:1, 0:1]
    beta = scalars[1:2, 0:1]
    curve = scalars[2:3, 0:1]
    along = first[:blocks, :]
    left = second[:blocks, :]
    direction = left + beta * along
    total = None
    for shift in range(count):
        piece = parts[shift][shift * blocks : (shift + 1) * blocks, :]
        total = piece if total is None else total + piece
    image = weight[:blocks, :] * direction - total
    alpha = norm / (curve - whole(extra_rows(parts, cells)[0:1, :]))
    model[...] = start[:blocks, :] + step[0:1, 0:1] * along + alpha * direction
    residual[...] = left - alpha * image


def call(body, outs, *args):
    specs = []
    for arg in args:
        small = arg.ndim == 1
        specs.append(pl.BlockSpec(memory_space=pltpu.SMEM if small else pltpu.VMEM))
    return pl.pallas_call(
        body,
        out_shape=[jax.ShapeDtypeStruct(shape, dtype) for shape, dtype in outs],
        in_specs=specs,
        out_specs=[pl.BlockSpec(memory_space=pltpu.VMEM)] * len(outs),
        compiler_params=pltpu.CompilerParams(vmem_limit_bytes=16 * 1024 * 1024),
    )(*args)


def shards(
    tile_codes,
    tile_scale,
    tile_row,
    tile_column,
    send_index,
    model_start,
    reg_weight,
    observed,
    data_weight,
):
    blocks, width = model_start.shape
    slots = send_index.shape[2]
    data_rows = observed.shape[0]
    tiles = tile_codes.shape[0]
    count = lax.axis_size("tiles")
    sharing = lax.axis_size(("split", "depth"))
    cells = count * blocks
    codes = pltpu.with_memory_space_constraint(tile_codes, pltpu.VMEM)
    place = lax.axis_index("tiles").astype(jnp.int32).reshape(1)

    def across(value):
        return exchange(value, "tiles", count)

    def within(value):
        return exchange(value, ("split", "depth"), sharing)

    named = jnp.pad(send_index.reshape(1, -1).astype(F32), ((0, 0), (0, width - count * slots)))
    begin = across(jnp.concatenate([model_start, reg_weight, named], axis=0))
    part, rows_one, rows_scaled, source_one, source_scaled, start, weight = call(
        functools.partial(first_kernel, blocks, slots, count),
        [
            ((data_rows, width), F32),
            ((data_rows, tiles), BF16),
            ((data_rows, tiles), F32),
            ((cells, tiles), BF16),
            ((cells, tiles), F32),
            ((cells, width), F32),
            ((cells, width), F32),
        ],
        codes,
        tile_scale.reshape(1, -1),
        tile_row.reshape(1, -1),
        tile_column.reshape(1, -1),
        place,
        *begin,
    )
    (part,) = call(
        functools.partial(start_data_kernel, sharing),
        [((cells, width), F32)],
        codes,
        rows_one,
        source_scaled,
        observed,
        data_weight,
        *within(part),
    )
    part, first = call(
        functools.partial(start_residual_kernel, blocks, count),
        [((data_rows + EXTRA, width), F32), ((cells, width), F32)],
        codes,
        source_one,
        rows_scaled,
        start,
        weight,
        *across(part),
    )
    part, predicted, sums = call(
        functools.partial(image_data_kernel, sharing),
        [((cells + EXTRA, width), F32), ((data_rows, width), F32), ((EXTRA, width), F32)],
        codes,
        rows_one,
        source_scaled,
        data_weight,
        *within(part),
    )
    part, second, step = call(
        functools.partial(residual_kernel, blocks, count),
        [((data_rows + EXTRA, width), F32), ((cells, width), F32), ((8, 128), F32)],
        codes,
        source_one,
        rows_scaled,
        weight,
        first,
        sums,
        *across(part),
    )
    part, scalars = call(
        functools.partial(second_data_kernel, sharing),
        [((cells + EXTRA, width), F32), ((EXTRA, width), F32)],
        codes,
        rows_one,
        source_scaled,
        data_weight,
        predicted,
        sums,
        *within(part),
    )
    model, residual = call(
        functools.partial(last_kernel, blocks, count),
        [((blocks, width), F32), ((blocks, width), F32)],
        weight,
        start,
        first,
        second,
        step,
        scalars,
        *across(part),
    )
    return (model, residual)


def solution(mesh):
    both = P(("groups", "tiles", "split", "depth"))
    owned = P(("groups", "tiles", "split", "depth"), None)
    wide = P(("groups", "tiles", "split", "depth"), None, None)
    data = P(("groups", "tiles"), None)
    in_specs = (wide, both, both, both, wide, owned, owned, data, data)
    return jax.shard_map(
        shards, mesh=mesh, in_specs=in_specs, out_specs=(owned, owned), check_vma=False
    )
```

```python
import functools

import jax
import jax.numpy as jnp
from jax import lax
from jax.experimental import pallas as pl
from jax.experimental.pallas import tpu as pltpu
from jax.sharding import PartitionSpec as P

HIGH = lax.Precision.HIGHEST
EXTRA = 8
LIMIT = 16 * 1024 * 1024
GROUP = 16
F32 = jnp.float32
BF16 = jnp.bfloat16


def exchange(values, axes, size):
    parts = [values[0]]
    for shift in range(1, size):
        perm = [(i, i ^ shift) for i in range(size)]
        parts.append(lax.ppermute(values[shift], axes, perm))
    return parts


def total_rows(parts):
    total = parts[0][...]
    for part in parts[1:]:
        total = total + part[...]
    return total


def total_blocks(parts, blocks):
    count = len(parts)
    groups = []
    for group in range(count):
        total = None
        for shift in range(count):
            start = (group ^ shift) * blocks
            piece = parts[shift][start : start + blocks, :]
            total = piece if total is None else total + piece
        groups.append(total)
    return jnp.concatenate(groups, axis=0)


def extra_rows(parts, start):
    total = parts[0][start : start + EXTRA, :]
    for part in parts[1:]:
        total = total + part[start : start + EXTRA, :]
    return total


def whole(value):
    return jnp.sum(value, axis=(0, 1), keepdims=True)


def columns(value):
    return jnp.sum(value, axis=0, keepdims=True)


def pack_rows(rows, width):
    filled = list(rows)
    while len(filled) < EXTRA:
        filled.append(jnp.zeros((1, width), F32))
    return jnp.concatenate(filled, axis=0)


def products(codes, picked, turned=None):
    tiles = picked.shape[0]
    pieces = []
    for first in range(0, tiles, GROUP):
        rows = picked[first : first + GROUP, :]
        index = lax.broadcasted_iota(jnp.int32, (GROUP, codes.shape[1]), 0)
        total = None
        for i in range(GROUP):
            tile = codes[first + i]
            if turned is not None:
                tile = tile.T
                turned[first + i] = tile
            value = jnp.dot(rows, tile, preferred_element_type=F32)
            total = value if total is None else jnp.where(index == i, value, total)
        pieces.append(total)
    return jnp.concatenate(pieces, axis=0)


def pick(table, values):
    return lax.dot_general(
        table, values, (((0,), (0,)), ((), ())), preferred_element_type=F32
    ).astype(BF16)


def gather(table, terms):
    return jnp.dot(table, terms, precision=HIGH, preferred_element_type=F32)


def opening_kernel(codes, start, weight, named, out, sources, weights, names, done):
    copies = [
        pltpu.make_async_copy(start, sources, done.at[0]),
        pltpu.make_async_copy(weight, weights, done.at[1]),
        pltpu.make_async_copy(named, names, done.at[2]),
    ]
    for copy in copies:
        copy.start()
    blocks, width = sources.shape
    slots, count = names.shape
    rest = out.shape[0] - 2 * blocks
    out[2 * blocks :, :] = jnp.zeros((rest, width), F32)
    for copy in copies:
        copy.wait()
    out[:blocks, :] = sources[...]
    out[blocks : 2 * blocks, :] = weights[...]
    out[2 * blocks : 2 * blocks + slots, :count] = names[...].astype(F32)


def first_kernel(blocks, slots, count, *refs):
    codes, scale, row, column, place = refs[:5]
    parts = refs[5 : 5 + count]
    out, turned, rows_one, rows_scaled, source_one, source_scaled, start, weight = refs[5 + count :]
    tiles = scale.shape[1]
    width = out.shape[1]
    data_rows = out.shape[0]
    here = place[0]
    columns_of = column[...]
    source = jnp.where(columns_of < blocks, columns_of, 0)
    lane = lax.broadcasted_iota(jnp.int32, (1, width), 1)
    for shift in range(count):
        other = jnp.bitwise_xor(here, shift)
        for slot in range(slots):
            named = parts[shift][2 * blocks + slot : 2 * blocks + slot + 1, :]
            mine = jnp.where(lane == here, named, 0.0)
            block = jnp.sum(mine, axis=1, keepdims=True).astype(jnp.int32) + shift * blocks
            source = jnp.where(columns_of == blocks + other * slots + slot, block, source)
    scales = scale[...]
    table = lax.broadcasted_iota(jnp.int32, (data_rows, tiles), 0) == row[...]
    rows_one[...] = jnp.where(table, 1.0, 0.0).astype(BF16)
    rows_scaled[...] = jnp.where(table, scales, 0.0)
    table = lax.broadcasted_iota(jnp.int32, (count * blocks, tiles), 0) == source
    ones = jnp.where(table, 1.0, 0.0).astype(BF16)
    source_one[...] = ones
    source_scaled[...] = jnp.where(table, scales, 0.0)
    field = jnp.concatenate([part[:blocks, :] for part in parts], axis=0)
    start[...] = field
    weight[...] = jnp.concatenate([part[blocks : 2 * blocks, :] for part in parts], axis=0)
    terms = products(codes, pick(ones, field.astype(BF16)), turned)
    out[...] = gather(rows_scaled[...], terms)


def start_data_kernel(count, *refs):
    codes, rows_one, source_scaled, observed, data_weight = refs[:5]
    parts = refs[5 : 5 + count]
    out = refs[5 + count]
    total = total_rows(parts)
    data = (data_weight[...] * (observed[...] - total)).astype(BF16)
    terms = products(codes, pick(rows_one[...], data))
    out[...] = gather(source_scaled[...], terms)


def start_residual_kernel(blocks, count, *refs):
    codes, source_one, rows_scaled, start, weight = refs[:5]
    parts = refs[5 : 5 + count]
    out, residual = refs[5 + count :]
    weights = weight[...]
    value = total_blocks(parts, blocks) - weights * start[...]
    residual[...] = value
    terms = products(codes, pick(source_one[...], value.astype(BF16)))
    data_rows = rows_scaled.shape[0]
    out[:data_rows, :] = gather(rows_scaled[...], terms)
    out[data_rows:, :] = pack_rows(
        [columns(value * value), columns(value * weights * value)], value.shape[1]
    )


def image_data_kernel(count, *refs):
    codes, rows_one, source_scaled, data_weight = refs[:4]
    parts = refs[4 : 4 + count]
    out, predicted, sums = refs[4 + count :]
    data_rows = data_weight.shape[0]
    whole_part = total_rows(parts)
    total = whole_part[:data_rows, :]
    predicted[...] = total
    sums[...] = whole_part[data_rows:, :]
    data = (data_weight[...] * (0.0 - total)).astype(BF16)
    terms = products(codes, pick(rows_one[...], data))
    cells = source_scaled.shape[0]
    out[:cells, :] = gather(source_scaled[...], terms)
    out[cells:, :] = pack_rows([columns(total * data.astype(F32))], total.shape[1])


def residual_kernel(blocks, count, *refs):
    codes, source_one, rows_scaled, weight, direction, sums = refs[:6]
    parts = refs[6 : 6 + count]
    out, residual, step = refs[6 + count :]
    cells = source_one.shape[0]
    weights = weight[...]
    along = direction[...]
    image = weights * along - total_blocks(parts, blocks)
    curve = whole(sums[1:2, :]) - whole(extra_rows(parts, cells)[0:1, :])
    alpha = whole(sums[0:1, :]) / curve
    step[...] = jnp.broadcast_to(alpha, step.shape)
    value = residual_of(along, alpha, image)
    residual[...] = value
    terms = products(codes, pick(source_one[...], value.astype(BF16)))
    data_rows = rows_scaled.shape[0]
    out[:data_rows, :] = gather(rows_scaled[...], terms)
    weighted = value * weights
    out[data_rows:, :] = pack_rows(
        [columns(value * value), columns(weighted * value), columns(weighted * along)],
        value.shape[1],
    )


def residual_of(residual, alpha, image):
    return residual - alpha * image


def second_data_kernel(blocks, count, *refs):
    codes, rows_one, source_scaled, data_weight, predicted, sums = refs[:6]
    parts = refs[6 : 6 + count]
    outs, scalars = refs[6 + count : -1], refs[-1]
    data_rows = data_weight.shape[0]
    whole_part = total_rows(parts)
    norm = whole(whole_part[data_rows : data_rows + 1, :])
    beta = norm / whole(sums[0:1, :])
    curve = whole(
        whole_part[data_rows + 1 : data_rows + 2, :]
        + 2.0 * beta * whole_part[data_rows + 2 : data_rows + 3, :]
        + beta * beta * sums[1:2, :]
    )
    total = whole_part[:data_rows, :] + beta * predicted[...]
    data = (data_weight[...] * (0.0 - total)).astype(BF16)
    terms = products(codes, pick(rows_one[...], data))
    cells = gather(source_scaled[...], terms)
    curved = columns(total * data.astype(F32))
    for group, out in enumerate(outs):
        out[:blocks, :] = cells[group * blocks : (group + 1) * blocks, :]
        out[blocks:, :] = jnp.broadcast_to(curved, (out.shape[0] - blocks, total.shape[1]))
    wide = (1, scalars.shape[1])
    scalars[...] = pack_rows(
        [jnp.broadcast_to(value, wide) for value in (norm, beta, curve)], scalars.shape[1]
    )


def last_kernel(blocks, count, *refs):
    weight, start, first, second, step, scalars = refs[:6]
    parts = refs[6 : 6 + count]
    model, residual = refs[6 + count :]
    norm = scalars[0:1, 0:1]
    beta = scalars[1:2, 0:1]
    curve = scalars[2:3, 0:1]
    along = first[:blocks, :]
    left = second[:blocks, :]
    direction = left + beta * along
    whole_part = total_rows(parts)
    image = weight[:blocks, :] * direction - whole_part[:blocks, :]
    alpha = norm / (curve - whole(whole_part[blocks : blocks + 1, :]))
    model[...] = start[:blocks, :] + step[0:1, 0:1] * along + alpha * direction
    residual[...] = left - alpha * image


def call(body, outs, *args):
    specs = []
    for arg in args:
        small = arg.ndim == 1
        specs.append(pl.BlockSpec(memory_space=pltpu.SMEM if small else pltpu.VMEM))
    return pl.pallas_call(
        body,
        out_shape=[jax.ShapeDtypeStruct(shape, dtype) for shape, dtype in outs],
        in_specs=specs,
        out_specs=[pl.BlockSpec(memory_space=pltpu.VMEM)] * len(outs),
        compiler_params=pltpu.CompilerParams(vmem_limit_bytes=LIMIT),
    )(*args)


def shards(
    tile_codes,
    tile_scale,
    tile_row,
    tile_column,
    send_index,
    model_start,
    reg_weight,
    observed,
    data_weight,
):
    blocks, width = model_start.shape
    slots = send_index.shape[2]
    data_rows = observed.shape[0]
    tiles = tile_codes.shape[0]
    count = lax.axis_size("tiles")
    sharing = lax.axis_size(("split", "depth"))
    cells = count * blocks
    codes = tile_codes
    place = lax.axis_index("tiles").astype(jnp.int32).reshape(1)

    def across(values):
        return exchange(values, "tiles", count)

    def within(value):
        return exchange([value] * sharing, ("split", "depth"), sharing)

    opening = pl.pallas_call(
        opening_kernel,
        out_shape=jax.ShapeDtypeStruct((2 * blocks + EXTRA, width), F32),
        in_specs=[pl.BlockSpec(memory_space=pl.ANY)] * 4,
        out_specs=pl.BlockSpec(memory_space=pltpu.VMEM),
        scratch_shapes=[
            pltpu.VMEM((blocks, width), F32),
            pltpu.VMEM((blocks, width), F32),
            pltpu.VMEM((slots, count), jnp.int32),
            pltpu.SemaphoreType.DMA((3,)),
        ],
        compiler_params=pltpu.CompilerParams(vmem_limit_bytes=LIMIT),
    )(
        pltpu.with_memory_space_constraint(tile_codes, pltpu.HBM),
        pltpu.with_memory_space_constraint(model_start, pltpu.HBM),
        pltpu.with_memory_space_constraint(reg_weight, pltpu.HBM),
        pltpu.with_memory_space_constraint(
            jnp.transpose(send_index, (0, 2, 1)).reshape(slots, count), pltpu.HBM
        ),
    )
    begin = across([opening] * count)
    part, turned, rows_one, rows_scaled, source_one, source_scaled, start, weight = call(
        functools.partial(first_kernel, blocks, slots, count),
        [
            ((data_rows, width), F32),
            (tile_codes.shape, BF16),
            ((data_rows, tiles), BF16),
            ((data_rows, tiles), F32),
            ((cells, tiles), BF16),
            ((cells, tiles), F32),
            ((cells, width), F32),
            ((cells, width), F32),
        ],
        codes,
        tile_scale.reshape(1, -1),
        tile_row.reshape(1, -1),
        tile_column.reshape(1, -1),
        place,
        *begin,
    )
    (part,) = call(
        functools.partial(start_data_kernel, sharing),
        [((cells, width), F32)],
        codes,
        rows_one,
        source_scaled,
        observed,
        data_weight,
        *within(part),
    )
    part, first = call(
        functools.partial(start_residual_kernel, blocks, count),
        [((data_rows + EXTRA, width), F32), ((cells, width), F32)],
        turned,
        source_one,
        rows_scaled,
        start,
        weight,
        *across([part] * count),
    )
    part, predicted, sums = call(
        functools.partial(image_data_kernel, sharing),
        [((cells + EXTRA, width), F32), ((data_rows, width), F32), ((EXTRA, width), F32)],
        codes,
        rows_one,
        source_scaled,
        data_weight,
        *within(part),
    )
    part, second, step = call(
        functools.partial(residual_kernel, blocks, count),
        [((data_rows + EXTRA, width), F32), ((cells, width), F32), ((8, 128), F32)],
        turned,
        source_one,
        rows_scaled,
        weight,
        first,
        sums,
        *across([part] * count),
    )
    *part, scalars = call(
        functools.partial(second_data_kernel, blocks, sharing),
        [((blocks + 4, width), F32)] * count + [((EXTRA, width), F32)],
        codes,
        rows_one,
        source_scaled,
        data_weight,
        predicted,
        sums,
        *within(part),
    )
    model, residual = call(
        functools.partial(last_kernel, blocks, count),
        [((blocks, width), F32), ((blocks, width), F32)],
        weight,
        start,
        first,
        second,
        step,
        scalars,
        *across(part),
    )
    return (model, residual)


def solution(mesh):
    both = P(("groups", "tiles", "split", "depth"))
    owned = P(("groups", "tiles", "split", "depth"), None)
    wide = P(("groups", "tiles", "split", "depth"), None, None)
    data = P(("groups", "tiles"), None)
    in_specs = (wide, both, both, both, wide, owned, owned, data, data)
    return jax.shard_map(
        shards, mesh=mesh, in_specs=in_specs, out_specs=(owned, owned), check_vma=False
    )
```

```python
import functools

import jax
import jax.numpy as jnp
from jax import lax
from jax.experimental import pallas as pl
from jax.experimental.pallas import tpu as pltpu
from jax.sharding import PartitionSpec as P

HIGH = lax.Precision.HIGHEST
EXTRA = 8
LIMIT = 16 * 1024 * 1024
GROUP = 16
CHUNK = 8
F32 = jnp.float32
BF16 = jnp.bfloat16


def exchange(values, axes, size):
    parts = [values[0]] + [None] * (size - 1)
    for shift in range(size - 1, 0, -1):
        perm = [(i, i ^ shift) for i in range(size)]
        parts[shift] = lax.ppermute(values[shift], axes, perm)
    return parts


def total_rows(parts):
    total = parts[0][...]
    for part in parts[1:]:
        total = total + part[...]
    return total


def total_blocks(parts, blocks):
    count = len(parts)
    groups = []
    for group in range(count):
        total = None
        for shift in range(count):
            start = (group ^ shift) * blocks
            piece = parts[shift][start : start + blocks, :]
            total = piece if total is None else total + piece
        groups.append(total)
    return jnp.concatenate(groups, axis=0)


def extra_rows(parts, start):
    total = parts[0][start : start + EXTRA, :]
    for part in parts[1:]:
        total = total + part[start : start + EXTRA, :]
    return total


def whole(value):
    return jnp.sum(value, axis=(0, 1), keepdims=True)


def columns(value):
    return jnp.sum(value, axis=0, keepdims=True)


def pack_rows(rows, width):
    filled = list(rows)
    while len(filled) < EXTRA:
        filled.append(jnp.zeros((1, width), F32))
    return jnp.concatenate(filled, axis=0)


def products(tile_of, picked):
    tiles, width = picked.shape
    index = lax.broadcasted_iota(jnp.int32, (GROUP, width), 0)
    pieces = []
    for first in range(0, tiles, GROUP):
        rows = picked[first : first + GROUP, :]
        total = None
        for i in range(GROUP):
            value = jnp.dot(rows, tile_of(first + i), preferred_element_type=F32)
            total = value if total is None else jnp.where(index == i, value, total)
        pieces.append(total)
    return jnp.concatenate(pieces, axis=0)


def kept_tiles(low, high):
    half = low.shape[0]
    return lambda k: low[k] if k < half else high[k - half]


def pick(table, values):
    return jnp.dot(table, values, preferred_element_type=F32).astype(BF16)


def gather(table, scale, terms):
    scaled = scale * terms
    upper = scaled.astype(BF16)
    lower = (scaled - upper.astype(F32)).astype(BF16)
    both = jnp.concatenate([upper, lower], axis=0)
    return jnp.dot(table, both, preferred_element_type=F32)


def loading_kernel(codes, opening, low, low_turned, done):
    half = low.shape[0]
    copies = []
    for chunk in range(half // CHUNK):
        span = pl.ds(chunk * CHUNK, CHUNK)
        copies.append(pltpu.make_async_copy(codes.at[span], low.at[span], done.at[chunk]))
        copies[-1].start()
    for chunk, copy in enumerate(copies):
        copy.wait()
        for k in range(chunk * CHUNK, (chunk + 1) * CHUNK):
            low_turned[k] = low[k].T


def opening_kernel(start, weight, named, out, sources, weights, names, done):
    copies = [
        pltpu.make_async_copy(start, sources, done.at[0]),
        pltpu.make_async_copy(weight, weights, done.at[1]),
        pltpu.make_async_copy(named, names, done.at[2]),
    ]
    for copy in copies:
        copy.start()
    blocks, width = sources.shape
    slots, count = names.shape
    rest = out.shape[0] - 2 * blocks
    out[2 * blocks :, :] = jnp.zeros((rest, width), F32)
    for copy in copies:
        copy.wait()
    out[:blocks, :] = sources[...]
    out[blocks : 2 * blocks, :] = weights[...]
    out[2 * blocks : 2 * blocks + slots, :count] = names[...].astype(F32)


def first_kernel(blocks, slots, count, *refs):
    codes, low_turned, scale, row, column, place = refs[:6]
    parts = refs[6 : 6 + count]
    (out, high, high_turned, rows_pick, rows_pair, source_pick, source_pair, wide_scale) = refs[
        6 + count : 14 + count
    ]
    start, weight, done = refs[14 + count :]
    half = low_turned.shape[0]
    copies = []
    for chunk in range(high.shape[0] // CHUNK):
        copies.append(
            pltpu.make_async_copy(
                codes.at[pl.ds(half + chunk * CHUNK, CHUNK)],
                high.at[pl.ds(chunk * CHUNK, CHUNK)],
                done.at[chunk],
            )
        )
        copies[-1].start()
    tiles = scale.shape[1]
    width = out.shape[1]
    data_rows = out.shape[0]
    here = place[0]
    columns_of = column[...]
    source = jnp.where(columns_of < blocks, columns_of, 0)
    lane = lax.broadcasted_iota(jnp.int32, (1, width), 1)
    for shift in range(count):
        other = jnp.bitwise_xor(here, shift)
        for slot in range(slots):
            named = parts[shift][2 * blocks + slot : 2 * blocks + slot + 1, :]
            mine = jnp.where(lane == here, named, 0.0)
            block = jnp.sum(mine, axis=1, keepdims=True).astype(jnp.int32) + shift * blocks
            source = jnp.where(columns_of == blocks + other * slots + slot, block, source)

    def tables(index, values, picks, pairs):
        hits = lax.broadcasted_iota(jnp.int32, (values, tiles), 0) == index
        ones = jnp.where(hits, 1.0, 0.0)
        turned = ones.T.astype(BF16)
        picks[...] = turned
        pairs[...] = jnp.concatenate([ones, ones], axis=1).astype(BF16)
        return turned

    source_table = tables(source, count * blocks, source_pick, source_pair)
    field = jnp.concatenate([part[:blocks, :] for part in parts], axis=0)
    start[...] = field
    weight[...] = jnp.concatenate([part[blocks : 2 * blocks, :] for part in parts], axis=0)
    tables(row[...], data_rows, rows_pick, rows_pair)
    square = (tiles, tiles)
    same = lax.broadcasted_iota(jnp.int32, square, 0) == lax.broadcasted_iota(jnp.int32, square, 1)
    scales = jnp.dot(
        jnp.where(same, scale[...], 0.0),
        jnp.ones((tiles, width), F32),
        precision=HIGH,
        preferred_element_type=F32,
    )
    wide_scale[...] = scales

    def tile_of(k):
        if k < half:
            return low_turned[k]
        k -= half
        if k % CHUNK == 0:
            copies[k // CHUNK].wait()
        tile = high[k].T
        high_turned[k] = tile
        return tile

    terms = products(tile_of, pick(source_table, field.astype(BF16)))
    out[...] = gather(rows_pair[...], scales, terms)


def start_data_kernel(count, *refs):
    low, high, rows_pick, source_pair, scale, observed, data_weight = refs[:7]
    parts = refs[7 : 7 + count]
    out = refs[7 + count]
    total = total_rows(parts)
    data = (data_weight[...] * (observed[...] - total)).astype(BF16)
    terms = products(kept_tiles(low, high), pick(rows_pick[...], data))
    out[...] = gather(source_pair[...], scale[...], terms)


def start_residual_kernel(blocks, count, *refs):
    low, high, source_pick, rows_pair, scale, start, weight = refs[:7]
    parts = refs[7 : 7 + count]
    out, residual = refs[7 + count :]
    weights = weight[...]
    value = total_blocks(parts, blocks) - weights * start[...]
    residual[...] = value
    terms = products(kept_tiles(low, high), pick(source_pick[...], value.astype(BF16)))
    data_rows = rows_pair.shape[0]
    out[:data_rows, :] = gather(rows_pair[...], scale[...], terms)
    out[data_rows:, :] = pack_rows(
        [columns(value * value), columns(value * weights * value)], value.shape[1]
    )


def image_data_kernel(count, *refs):
    low, high, rows_pick, source_pair, scale, data_weight = refs[:6]
    parts = refs[6 : 6 + count]
    out, predicted, sums = refs[6 + count :]
    data_rows = data_weight.shape[0]
    whole_part = total_rows(parts)
    total = whole_part[:data_rows, :]
    predicted[...] = total
    sums[...] = whole_part[data_rows:, :]
    data = (data_weight[...] * (0.0 - total)).astype(BF16)
    terms = products(kept_tiles(low, high), pick(rows_pick[...], data))
    cells = source_pair.shape[0]
    out[:cells, :] = gather(source_pair[...], scale[...], terms)
    out[cells:, :] = pack_rows([columns(total * data.astype(F32))], total.shape[1])


def residual_kernel(blocks, count, *refs):
    low, high, source_pick, rows_pair, scale, weight, direction, sums = refs[:8]
    parts = refs[8 : 8 + count]
    out, residual, step = refs[8 + count :]
    cells = source_pick.shape[1]
    weights = weight[...]
    along = direction[...]
    image = weights * along - total_blocks(parts, blocks)
    curve = whole(sums[1:2, :]) - whole(extra_rows(parts, cells)[0:1, :])
    alpha = whole(sums[0:1, :]) / curve
    step[...] = jnp.broadcast_to(alpha, step.shape)
    value = residual_of(along, alpha, image)
    residual[...] = value
    terms = products(kept_tiles(low, high), pick(source_pick[...], value.astype(BF16)))
    data_rows = rows_pair.shape[0]
    out[:data_rows, :] = gather(rows_pair[...], scale[...], terms)
    weighted = value * weights
    out[data_rows:, :] = pack_rows(
        [columns(value * value), columns(weighted * value), columns(weighted * along)],
        value.shape[1],
    )


def residual_of(residual, alpha, image):
    return residual - alpha * image


def second_data_kernel(blocks, count, *refs):
    low, high, rows_pick, source_pair, scale, data_weight, predicted, sums = refs[:8]
    parts = refs[8 : 8 + count]
    outs, scalars = refs[8 + count : -1], refs[-1]
    data_rows = data_weight.shape[0]
    whole_part = total_rows(parts)
    norm = whole(whole_part[data_rows : data_rows + 1, :])
    beta = norm / whole(sums[0:1, :])
    curve = whole(
        whole_part[data_rows + 1 : data_rows + 2, :]
        + 2.0 * beta * whole_part[data_rows + 2 : data_rows + 3, :]
        + beta * beta * sums[1:2, :]
    )
    total = whole_part[:data_rows, :] + beta * predicted[...]
    data = (data_weight[...] * (0.0 - total)).astype(BF16)
    terms = products(kept_tiles(low, high), pick(rows_pick[...], data))
    cells = gather(source_pair[...], scale[...], terms)
    curved = columns(total * data.astype(F32))
    for group, out in enumerate(outs):
        out[:blocks, :] = cells[group * blocks : (group + 1) * blocks, :]
        out[blocks:, :] = jnp.broadcast_to(curved, (out.shape[0] - blocks, total.shape[1]))
    wide = (1, scalars.shape[1])
    scalars[...] = pack_rows(
        [jnp.broadcast_to(value, wide) for value in (norm, beta, curve)], scalars.shape[1]
    )


def last_kernel(blocks, count, *refs):
    weight, start, first, second, step, scalars = refs[:6]
    parts = refs[6 : 6 + count]
    model, residual = refs[6 + count :]
    norm = scalars[0:1, 0:1]
    beta = scalars[1:2, 0:1]
    curve = scalars[2:3, 0:1]
    along = first[:blocks, :]
    left = second[:blocks, :]
    direction = left + beta * along
    whole_part = total_rows(parts)
    image = weight[:blocks, :] * direction - whole_part[:blocks, :]
    alpha = norm / (curve - whole(whole_part[blocks : blocks + 1, :]))
    model[...] = start[:blocks, :] + step[0:1, 0:1] * along + alpha * direction
    residual[...] = left - alpha * image


def call(body, outs, *args, scratch=()):
    specs = []
    for arg in args:
        far = getattr(jax.typeof(arg), "memory_space", None) == pltpu.HBM
        space = pl.ANY if far else pltpu.SMEM if arg.ndim == 1 else pltpu.VMEM
        specs.append(pl.BlockSpec(memory_space=space))
    return pl.pallas_call(
        body,
        out_shape=[jax.ShapeDtypeStruct(shape, dtype) for shape, dtype in outs],
        in_specs=specs,
        out_specs=[pl.BlockSpec(memory_space=pltpu.VMEM)] * len(outs),
        scratch_shapes=list(scratch),
        compiler_params=pltpu.CompilerParams(vmem_limit_bytes=LIMIT),
    )(*args)


def shards(
    tile_codes,
    tile_scale,
    tile_row,
    tile_column,
    send_index,
    model_start,
    reg_weight,
    observed,
    data_weight,
):
    blocks, width = model_start.shape
    slots = send_index.shape[2]
    data_rows = observed.shape[0]
    tiles = tile_codes.shape[0]
    count = lax.axis_size("tiles")
    sharing = lax.axis_size(("split", "depth"))
    cells = count * blocks
    half = tiles // 2
    codes = pltpu.with_memory_space_constraint(tile_codes, pltpu.HBM)
    half_shape = (half, width, width)
    place = lax.axis_index("tiles").astype(jnp.int32).reshape(1)

    def across(values):
        return exchange(values, "tiles", count)

    def within(value):
        return exchange([value] * sharing, ("split", "depth"), sharing)

    named = jnp.transpose(send_index, (0, 2, 1)).reshape(slots, count)
    (opening,) = call(
        opening_kernel,
        [((2 * blocks + EXTRA, width), F32)],
        pltpu.with_memory_space_constraint(model_start, pltpu.HBM),
        pltpu.with_memory_space_constraint(reg_weight, pltpu.HBM),
        pltpu.with_memory_space_constraint(named, pltpu.HBM),
        scratch=[
            pltpu.VMEM((blocks, width), F32),
            pltpu.VMEM((blocks, width), F32),
            pltpu.VMEM((slots, count), jnp.int32),
            pltpu.SemaphoreType.DMA((3,)),
        ],
    )
    begin = across([opening] * count)
    low, low_turned = call(
        loading_kernel,
        [(half_shape, BF16)] * 2,
        codes,
        opening,
        scratch=[pltpu.SemaphoreType.DMA((half // CHUNK,))],
    )
    (part, high, high_turned, rows_pick, rows_pair, source_pick, source_pair, scale, start, weight) = call(
        functools.partial(first_kernel, blocks, slots, count),
        [
            ((data_rows, width), F32),
            (half_shape, BF16),
            (half_shape, BF16),
            ((tiles, data_rows), BF16),
            ((data_rows, 2 * tiles), BF16),
            ((tiles, cells), BF16),
            ((cells, 2 * tiles), BF16),
            ((tiles, width), F32),
            ((cells, width), F32),
            ((cells, width), F32),
        ],
        codes,
        low_turned,
        tile_scale.reshape(1, -1),
        tile_row.reshape(1, -1),
        tile_column.reshape(1, -1),
        place,
        *begin,
        scratch=[pltpu.SemaphoreType.DMA((half // CHUNK,))],
    )
    (part,) = call(
        functools.partial(start_data_kernel, sharing),
        [((cells, width), F32)],
        low,
        high,
        rows_pick,
        source_pair,
        scale,
        observed,
        data_weight,
        *within(part),
    )
    part, first = call(
        functools.partial(start_residual_kernel, blocks, count),
        [((data_rows + EXTRA, width), F32), ((cells, width), F32)],
        low_turned,
        high_turned,
        source_pick,
        rows_pair,
        scale,
        start,
        weight,
        *across([part] * count),
    )
    part, predicted, sums = call(
        functools.partial(image_data_kernel, sharing),
        [((cells + EXTRA, width), F32), ((data_rows, width), F32), ((EXTRA, width), F32)],
        low,
        high,
        rows_pick,
        source_pair,
        scale,
        data_weight,
        *within(part),
    )
    part, second, step = call(
        functools.partial(residual_kernel, blocks, count),
        [((data_rows + EXTRA, width), F32), ((cells, width), F32), ((8, 128), F32)],
        low_turned,
        high_turned,
        source_pick,
        rows_pair,
        scale,
        weight,
        first,
        sums,
        *across([part] * count),
    )
    *part, scalars = call(
        functools.partial(second_data_kernel, blocks, sharing),
        [((blocks + 4, width), F32)] * count + [((EXTRA, width), F32)],
        low,
        high,
        rows_pick,
        source_pair,
        scale,
        data_weight,
        predicted,
        sums,
        *within(part),
    )
    model, residual = call(
        functools.partial(last_kernel, blocks, count),
        [((blocks, width), F32), ((blocks, width), F32)],
        weight,
        start,
        first,
        second,
        step,
        scalars,
        *across(part),
    )
    return (model, residual)


def solution(mesh):
    both = P(("groups", "tiles", "split", "depth"))
    owned = P(("groups", "tiles", "split", "depth"), None)
    wide = P(("groups", "tiles", "split", "depth"), None, None)
    data = P(("groups", "tiles"), None)
    in_specs = (wide, both, both, both, wide, owned, owned, data, data)
    return jax.shard_map(
        shards, mesh=mesh, in_specs=in_specs, out_specs=(owned, owned), check_vma=False
    )
```

```python
import functools

import jax
import jax.numpy as jnp
from jax import lax
from jax.experimental import pallas as pl
from jax.experimental.pallas import tpu as pltpu
from jax.sharding import PartitionSpec as P

HIGH = lax.Precision.HIGHEST
EXTRA = 8
LIMIT = 16 * 1024 * 1024
GROUP = 16
CHUNK = 8
F32 = jnp.float32
BF16 = jnp.bfloat16


def exchange(values, axes, size):
    parts = [values[0]] + [None] * (size - 1)
    for shift in range(size - 1, 0, -1):
        perm = [(i, i ^ shift) for i in range(size)]
        parts[shift] = lax.ppermute(values[shift], axes, perm)
    return parts


def doubling(value, axes, size):
    shift = 1
    while True:
        perm = [(i, i ^ shift) for i in range(size)]
        other = lax.ppermute(value, axes, perm)
        shift *= 2
        if shift == size:
            return value, other
        value = value + other


def total_rows(parts):
    total = parts[0][...]
    for part in parts[1:]:
        total = total + part[...]
    return total


def placed(values, here):
    ordered = []
    for place in range(len(values)):
        total = values[0]
        for shift in range(1, len(values)):
            total = jnp.where(jnp.bitwise_xor(here, shift) == place, values[shift], total)
        ordered.append(total)
    return ordered


def own_rows(value, here, blocks):
    total = value[:blocks, :]
    for place in range(1, value.shape[0] // blocks):
        total = jnp.where(here == place, value[place * blocks : (place + 1) * blocks, :], total)
    return total


def whole(value):
    return jnp.sum(value, axis=(0, 1), keepdims=True)


def columns(value):
    return jnp.sum(value, axis=0, keepdims=True)


def pack_rows(rows, width):
    filled = list(rows)
    while len(filled) < EXTRA:
        filled.append(jnp.zeros((1, width), F32))
    return jnp.concatenate(filled, axis=0)


def products(tile_of, picked):
    tiles, width = picked.shape
    index = lax.broadcasted_iota(jnp.int32, (GROUP, width), 0)
    pieces = []
    for first in range(0, tiles, GROUP):
        rows = picked[first : first + GROUP, :]
        total = None
        for i in range(GROUP):
            value = jnp.dot(rows, tile_of(first + i), preferred_element_type=F32)
            total = value if total is None else jnp.where(index == i, value, total)
        pieces.append(total)
    return jnp.concatenate(pieces, axis=0)


def kept_tiles(low, high):
    half = low.shape[0]
    return lambda k: low[k] if k < half else high[k - half]


def pick(table, values):
    return jnp.dot(table, values, preferred_element_type=F32).astype(BF16)


def gather(table, scale, terms):
    scaled = scale * terms
    upper = scaled.astype(BF16)
    lower = (scaled - upper.astype(F32)).astype(BF16)
    both = jnp.concatenate([upper, lower], axis=0)
    return jnp.dot(table, both, preferred_element_type=F32)


def loading_kernel(codes, opening, low, low_turned, done):
    half = low.shape[0]
    copies = []
    for chunk in range(half // CHUNK):
        span = pl.ds(chunk * CHUNK, CHUNK)
        copies.append(pltpu.make_async_copy(codes.at[span], low.at[span], done.at[chunk]))
        copies[-1].start()
    for chunk, copy in enumerate(copies):
        copy.wait()
        for k in range(chunk * CHUNK, (chunk + 1) * CHUNK):
            low_turned[k] = low[k].T


def opening_kernel(start, weight, named, out, sources, weights, names, done):
    copies = [
        pltpu.make_async_copy(start, sources, done.at[0]),
        pltpu.make_async_copy(weight, weights, done.at[1]),
        pltpu.make_async_copy(named, names, done.at[2]),
    ]
    for copy in copies:
        copy.start()
    blocks, width = sources.shape
    slots, count = names.shape
    rest = out.shape[0] - 2 * blocks
    out[2 * blocks :, :] = jnp.zeros((rest, width), F32)
    for copy in copies:
        copy.wait()
    out[:blocks, :] = sources[...]
    out[blocks : 2 * blocks, :] = weights[...]
    out[2 * blocks : 2 * blocks + slots, :count] = names[...].astype(F32)


def first_kernel(blocks, slots, count, *refs):
    codes, low_turned, scale, row, column, place = refs[:6]
    parts = refs[6 : 6 + count]
    (out, high, high_turned, rows_pick, rows_pair, source_pick, source_pair, wide_scale) = refs[
        6 + count : 14 + count
    ]
    start, weight, done = refs[14 + count :]
    half = low_turned.shape[0]
    copies = []
    for chunk in range(high.shape[0] // CHUNK):
        copies.append(
            pltpu.make_async_copy(
                codes.at[pl.ds(half + chunk * CHUNK, CHUNK)],
                high.at[pl.ds(chunk * CHUNK, CHUNK)],
                done.at[chunk],
            )
        )
        copies[-1].start()
    tiles = scale.shape[1]
    width = out.shape[1]
    data_rows = out.shape[0]
    here = place[0]
    columns_of = column[...]
    source = jnp.where(columns_of < blocks, here * blocks + columns_of, 0)
    lane = lax.broadcasted_iota(jnp.int32, (1, width), 1)
    for shift in range(count):
        other = jnp.bitwise_xor(here, shift)
        for slot in range(slots):
            named = parts[shift][2 * blocks + slot : 2 * blocks + slot + 1, :]
            mine = jnp.where(lane == here, named, 0.0)
            block = jnp.sum(mine, axis=1, keepdims=True).astype(jnp.int32) + other * blocks
            source = jnp.where(columns_of == blocks + other * slots + slot, block, source)

    def tables(index, values, picks, pairs):
        hits = lax.broadcasted_iota(jnp.int32, (values, tiles), 0) == index
        ones = jnp.where(hits, 1.0, 0.0)
        turned = ones.T.astype(BF16)
        picks[...] = turned
        pairs[...] = jnp.concatenate([ones, ones], axis=1).astype(BF16)
        return turned

    source_table = tables(source, count * blocks, source_pick, source_pair)
    pairs = placed([part[: 2 * blocks, :] for part in parts], here)
    field = jnp.concatenate([pair[:blocks, :] for pair in pairs], axis=0)
    start[...] = field
    weight[...] = jnp.concatenate([pair[blocks:, :] for pair in pairs], axis=0)
    tables(row[...], data_rows, rows_pick, rows_pair)
    square = (tiles, tiles)
    same = lax.broadcasted_iota(jnp.int32, square, 0) == lax.broadcasted_iota(jnp.int32, square, 1)
    scales = jnp.dot(
        jnp.where(same, scale[...], 0.0),
        jnp.ones((tiles, width), F32),
        precision=HIGH,
        preferred_element_type=F32,
    )
    wide_scale[...] = scales

    def tile_of(k):
        if k < half:
            return low_turned[k]
        k -= half
        if k % CHUNK == 0:
            copies[k // CHUNK].wait()
        tile = high[k].T
        high_turned[k] = tile
        return tile

    terms = products(tile_of, pick(source_table, field.astype(BF16)))
    out[...] = gather(rows_pair[...], scales, terms)


def start_data_kernel(*refs):
    low, high, rows_pick, source_pair, scale, observed, data_weight = refs[:7]
    parts, out = refs[7:-1], refs[-1]
    total = total_rows(parts)
    data = (data_weight[...] * (observed[...] - total)).astype(BF16)
    terms = products(kept_tiles(low, high), pick(rows_pick[...], data))
    out[...] = gather(source_pair[...], scale[...], terms)


def start_residual_kernel(*refs):
    low, high, source_pick, rows_pair, scale, start, weight = refs[:7]
    parts = refs[7:-2]
    out, residual = refs[-2:]
    weights = weight[...]
    value = total_rows(parts) - weights * start[...]
    residual[...] = value
    terms = products(kept_tiles(low, high), pick(source_pick[...], value.astype(BF16)))
    data_rows = rows_pair.shape[0]
    out[:data_rows, :] = gather(rows_pair[...], scale[...], terms)
    out[data_rows:, :] = pack_rows(
        [columns(value * value), columns(value * weights * value)], value.shape[1]
    )


def image_data_kernel(*refs):
    low, high, rows_pick, source_pair, scale, data_weight = refs[:6]
    parts = refs[6:-3]
    out, predicted, sums = refs[-3:]
    data_rows = data_weight.shape[0]
    whole_part = total_rows(parts)
    total = whole_part[:data_rows, :]
    predicted[...] = total
    sums[...] = whole_part[data_rows:, :]
    data = (data_weight[...] * (0.0 - total)).astype(BF16)
    terms = products(kept_tiles(low, high), pick(rows_pick[...], data))
    cells = source_pair.shape[0]
    out[:cells, :] = gather(source_pair[...], scale[...], terms)
    out[cells:, :] = pack_rows([columns(total * data.astype(F32))], total.shape[1])


def residual_kernel(*refs):
    low, high, source_pick, rows_pair, scale, weight, direction, sums = refs[:8]
    parts = refs[8:-3]
    out, residual, step = refs[-3:]
    cells = source_pick.shape[1]
    weights = weight[...]
    along = direction[...]
    total = total_rows(parts)
    image = weights * along - total[:cells, :]
    curve = whole(sums[1:2, :]) - whole(total[cells : cells + 1, :])
    alpha = whole(sums[0:1, :]) / curve
    step[...] = jnp.broadcast_to(alpha, step.shape)
    value = residual_of(along, alpha, image)
    residual[...] = value
    terms = products(kept_tiles(low, high), pick(source_pick[...], value.astype(BF16)))
    data_rows = rows_pair.shape[0]
    out[:data_rows, :] = gather(rows_pair[...], scale[...], terms)
    weighted = value * weights
    out[data_rows:, :] = pack_rows(
        [columns(value * value), columns(weighted * value), columns(weighted * along)],
        value.shape[1],
    )


def residual_of(residual, alpha, image):
    return residual - alpha * image


def second_data_kernel(*refs):
    low, high, rows_pick, source_pair, scale, data_weight, predicted, sums = refs[:8]
    parts = refs[8:-2]
    out, scalars = refs[-2:]
    data_rows = data_weight.shape[0]
    whole_part = total_rows(parts)
    norm = whole(whole_part[data_rows : data_rows + 1, :])
    beta = norm / whole(sums[0:1, :])
    curve = whole(
        whole_part[data_rows + 1 : data_rows + 2, :]
        + 2.0 * beta * whole_part[data_rows + 2 : data_rows + 3, :]
        + beta * beta * sums[1:2, :]
    )
    total = whole_part[:data_rows, :] + beta * predicted[...]
    data = (data_weight[...] * (0.0 - total)).astype(BF16)
    terms = products(kept_tiles(low, high), pick(rows_pick[...], data))
    cells = source_pair.shape[0]
    out[:cells, :] = gather(source_pair[...], scale[...], terms)
    out[cells:, :] = pack_rows([columns(total * data.astype(F32))], total.shape[1])
    wide = (1, scalars.shape[1])
    scalars[...] = pack_rows(
        [jnp.broadcast_to(value, wide) for value in (norm, beta, curve)], scalars.shape[1]
    )


def last_kernel(*refs):
    weight, start, first, second, step, scalars, place = refs[:7]
    parts = refs[7:-2]
    model, residual = refs[-2:]
    blocks = model.shape[0]
    cells = weight.shape[0]
    here = place[0]
    norm = scalars[0:1, 0:1]
    beta = scalars[1:2, 0:1]
    curve = scalars[2:3, 0:1]
    total = total_rows(parts)
    along = own_rows(first[...], here, blocks)
    left = own_rows(second[...], here, blocks)
    direction = left + beta * along
    held = own_rows(weight[...], here, blocks)
    image = held * direction - own_rows(total[:cells, :], here, blocks)
    alpha = norm / (curve - whole(total[cells : cells + 1, :]))
    model[...] = own_rows(start[...], here, blocks) + step[0:1, 0:1] * along + alpha * direction
    residual[...] = left - alpha * image


def call(body, outs, *args, scratch=()):
    specs = []
    for arg in args:
        far = getattr(jax.typeof(arg), "memory_space", None) == pltpu.HBM
        space = pl.ANY if far else pltpu.SMEM if arg.ndim == 1 else pltpu.VMEM
        specs.append(pl.BlockSpec(memory_space=space))
    return pl.pallas_call(
        body,
        out_shape=[jax.ShapeDtypeStruct(shape, dtype) for shape, dtype in outs],
        in_specs=specs,
        out_specs=[pl.BlockSpec(memory_space=pltpu.VMEM)] * len(outs),
        scratch_shapes=list(scratch),
        compiler_params=pltpu.CompilerParams(vmem_limit_bytes=LIMIT),
    )(*args)


def shards(
    tile_codes,
    tile_scale,
    tile_row,
    tile_column,
    send_index,
    model_start,
    reg_weight,
    observed,
    data_weight,
):
    blocks, width = model_start.shape
    slots = send_index.shape[2]
    data_rows = observed.shape[0]
    tiles = tile_codes.shape[0]
    count = lax.axis_size("tiles")
    sharing = lax.axis_size(("split", "depth"))
    cells = count * blocks
    half = tiles // 2
    codes = pltpu.with_memory_space_constraint(tile_codes, pltpu.HBM)
    half_shape = (half, width, width)
    place = lax.axis_index("tiles").astype(jnp.int32).reshape(1)

    def across(value):
        return doubling(value, "tiles", count)

    def within(value):
        return doubling(value, ("split", "depth"), sharing)

    named = jnp.transpose(send_index, (0, 2, 1)).reshape(slots, count)
    (opening,) = call(
        opening_kernel,
        [((2 * blocks + EXTRA, width), F32)],
        pltpu.with_memory_space_constraint(model_start, pltpu.HBM),
        pltpu.with_memory_space_constraint(reg_weight, pltpu.HBM),
        pltpu.with_memory_space_constraint(named, pltpu.HBM),
        scratch=[
            pltpu.VMEM((blocks, width), F32),
            pltpu.VMEM((blocks, width), F32),
            pltpu.VMEM((slots, count), jnp.int32),
            pltpu.SemaphoreType.DMA((3,)),
        ],
    )
    begin = exchange([opening] * count, "tiles", count)
    low, low_turned = call(
        loading_kernel,
        [(half_shape, BF16)] * 2,
        codes,
        opening,
        scratch=[pltpu.SemaphoreType.DMA((half // CHUNK,))],
    )
    (part, high, high_turned, rows_pick, rows_pair, source_pick, source_pair, scale, start, weight) = call(
        functools.partial(first_kernel, blocks, slots, count),
        [
            ((data_rows, width), F32),
            (half_shape, BF16),
            (half_shape, BF16),
            ((tiles, data_rows), BF16),
            ((data_rows, 2 * tiles), BF16),
            ((tiles, cells), BF16),
            ((cells, 2 * tiles), BF16),
            ((tiles, width), F32),
            ((cells, width), F32),
            ((cells, width), F32),
        ],
        codes,
        low_turned,
        tile_scale.reshape(1, -1),
        tile_row.reshape(1, -1),
        tile_column.reshape(1, -1),
        place,
        *begin,
        scratch=[pltpu.SemaphoreType.DMA((half // CHUNK,))],
    )
    (part,) = call(
        start_data_kernel,
        [((cells, width), F32)],
        low,
        high,
        rows_pick,
        source_pair,
        scale,
        observed,
        data_weight,
        *within(part),
    )
    part, first = call(
        start_residual_kernel,
        [((data_rows + EXTRA, width), F32), ((cells, width), F32)],
        low_turned,
        high_turned,
        source_pick,
        rows_pair,
        scale,
        start,
        weight,
        *across(part),
    )
    part, predicted, sums = call(
        image_data_kernel,
        [((cells + EXTRA, width), F32), ((data_rows, width), F32), ((EXTRA, width), F32)],
        low,
        high,
        rows_pick,
        source_pair,
        scale,
        data_weight,
        *within(part),
    )
    part, second, step = call(
        residual_kernel,
        [((data_rows + EXTRA, width), F32), ((cells, width), F32), ((8, 128), F32)],
        low_turned,
        high_turned,
        source_pick,
        rows_pair,
        scale,
        weight,
        first,
        sums,
        *across(part),
    )
    part, scalars = call(
        second_data_kernel,
        [((cells + EXTRA, width), F32), ((EXTRA, width), F32)],
        low,
        high,
        rows_pick,
        source_pair,
        scale,
        data_weight,
        predicted,
        sums,
        *within(part),
    )
    model, residual = call(
        last_kernel,
        [((blocks, width), F32), ((blocks, width), F32)],
        weight,
        start,
        first,
        second,
        step,
        scalars,
        place,
        *across(part),
    )
    return (model, residual)


def solution(mesh):
    both = P(("groups", "tiles", "split", "depth"))
    owned = P(("groups", "tiles", "split", "depth"), None)
    wide = P(("groups", "tiles", "split", "depth"), None, None)
    data = P(("groups", "tiles"), None)
    in_specs = (wide, both, both, both, wide, owned, owned, data, data)
    return jax.shard_map(
        shards, mesh=mesh, in_specs=in_specs, out_specs=(owned, owned), check_vma=False
    )
```

```python
import functools

import jax
import jax.numpy as jnp
from jax import lax
from jax.experimental import pallas as pl
from jax.experimental.pallas import tpu as pltpu
from jax.sharding import PartitionSpec as P

HIGH = lax.Precision.HIGHEST
EXTRA = 8
LIMIT = 16 * 1024 * 1024
GROUP = 16
CHUNK = 8
F32 = jnp.float32
BF16 = jnp.bfloat16


def exchange(values, axes, size):
    parts = [values[0]] + [None] * (size - 1)
    for shift in range(size - 1, 0, -1):
        perm = [(i, i ^ shift) for i in range(size)]
        parts[shift] = lax.ppermute(values[shift], axes, perm)
    return parts


def total_rows(parts):
    total = parts[0][...]
    for part in parts[1:]:
        total = total + part[...]
    return total


def total_blocks(parts, blocks):
    count = len(parts)
    groups = []
    for group in range(count):
        total = None
        for shift in range(count):
            start = (group ^ shift) * blocks
            piece = parts[shift][start : start + blocks, :]
            total = piece if total is None else total + piece
        groups.append(total)
    return jnp.concatenate(groups, axis=0)


def extra_rows(parts, start):
    total = parts[0][start : start + EXTRA, :]
    for part in parts[1:]:
        total = total + part[start : start + EXTRA, :]
    return total


def whole(value):
    return jnp.sum(value, axis=(0, 1), keepdims=True)


def columns(value):
    return jnp.sum(value, axis=0, keepdims=True)


def pack_rows(rows, width):
    filled = list(rows)
    while len(filled) < EXTRA:
        filled.append(jnp.zeros((1, width), F32))
    return jnp.concatenate(filled, axis=0)


def products(tile_of, picked, turn=False):
    tiles, width = picked.shape
    index = lax.broadcasted_iota(jnp.int32, (GROUP, width), 0)
    dims = (((1,), (1 if turn else 0,)), ((), ()))
    pieces = []
    for first in range(0, tiles, GROUP):
        rows = picked[first : first + GROUP, :]
        total = None
        for i in range(GROUP):
            value = lax.dot_general(rows, tile_of(first + i), dims, preferred_element_type=F32)
            total = value if total is None else jnp.where(index == i, value, total)
        pieces.append(total)
    return jnp.concatenate(pieces, axis=0)


def kept_tiles(low, high):
    half = low.shape[0]
    return lambda k: low[k] if k < half else high[k - half]


def pick(table, values):
    return jnp.dot(table, values, preferred_element_type=F32).astype(BF16)


def gather(table, scale, terms):
    scaled = scale * terms
    upper = scaled.astype(BF16)
    lower = (scaled - upper.astype(F32)).astype(BF16)
    both = jnp.concatenate([upper, lower], axis=0)
    return jnp.dot(table, both, preferred_element_type=F32)


def tables(index, values, picks, pairs):
    tiles = index.shape[1]
    hits = lax.broadcasted_iota(jnp.int32, (values, tiles), 0) == index
    ones = jnp.where(hits, 1.0, 0.0)
    picks[...] = ones.T.astype(BF16)
    pairs[...] = jnp.concatenate([ones, ones], axis=1).astype(BF16)


def chunk_copies(codes, first, kept, done):
    copies = []
    for chunk in range(kept.shape[0] // CHUNK):
        source = codes.at[pl.ds(first + chunk * CHUNK, CHUNK)]
        target = kept.at[pl.ds(chunk * CHUNK, CHUNK)]
        copies.append(pltpu.make_async_copy(source, target, done.at[chunk]))
        copies[-1].start()
    return copies


def loading_kernel(
    codes, opening, far_scale, far_row, low, rows_pick, rows_pair, wide_scale, scale, row, done, small
):
    near = [
        pltpu.make_async_copy(far_scale, scale, small.at[0]),
        pltpu.make_async_copy(far_row, row, small.at[1]),
    ]
    for copy in near:
        copy.start()
    copies = chunk_copies(codes, 0, low, done)
    tiles, width = wide_scale.shape
    for copy in near:
        copy.wait()
    tables(row[...], rows_pick.shape[1], rows_pick, rows_pair)
    square = (tiles, tiles)
    same = lax.broadcasted_iota(jnp.int32, square, 0) == lax.broadcasted_iota(jnp.int32, square, 1)
    wide_scale[...] = jnp.dot(
        jnp.where(same, scale[...], 0.0),
        jnp.ones((tiles, width), F32),
        precision=HIGH,
        preferred_element_type=F32,
    )
    for copy in copies:
        copy.wait()


def turning_kernel(first, low, high, part, turned):
    tile_of = kept_tiles(low, high)
    for k in range(turned.shape[0]):
        turned[k] = tile_of(first + k).T


def opening_kernel(start, weight, named, out, sources, weights, names, done):
    copies = [
        pltpu.make_async_copy(start, sources, done.at[0]),
        pltpu.make_async_copy(weight, weights, done.at[1]),
        pltpu.make_async_copy(named, names, done.at[2]),
    ]
    for copy in copies:
        copy.start()
    blocks, width = sources.shape
    slots, count = names.shape
    rest = out.shape[0] - 2 * blocks
    out[2 * blocks :, :] = jnp.zeros((rest, width), F32)
    for copy in copies:
        copy.wait()
    out[:blocks, :] = sources[...]
    out[blocks : 2 * blocks, :] = weights[...]
    out[2 * blocks : 2 * blocks + slots, :count] = names[...].astype(F32)


def first_kernel(blocks, slots, count, *refs):
    codes, low, scale, rows_pair, column, place = refs[:6]
    parts = refs[6 : 6 + count]
    out, high, source_pick, source_pair, start, weight, done = refs[6 + count :]
    loaded = low.shape[0]
    copies = chunk_copies(codes, loaded, high, done)
    width = out.shape[1]
    here = place[0]
    columns_of = column[...]
    source = jnp.where(columns_of < blocks, columns_of, 0)
    lane = lax.broadcasted_iota(jnp.int32, (1, width), 1)
    for shift in range(count):
        other = jnp.bitwise_xor(here, shift)
        for slot in range(slots):
            named = parts[shift][2 * blocks + slot : 2 * blocks + slot + 1, :]
            mine = jnp.where(lane == here, named, 0.0)
            block = jnp.sum(mine, axis=1, keepdims=True).astype(jnp.int32) + shift * blocks
            source = jnp.where(columns_of == blocks + other * slots + slot, block, source)
    tables(source, count * blocks, source_pick, source_pair)
    field = jnp.concatenate([part[:blocks, :] for part in parts], axis=0)
    start[...] = field
    weight[...] = jnp.concatenate([part[blocks : 2 * blocks, :] for part in parts], axis=0)

    def tile_of(k):
        if k < loaded:
            return low[k]
        k -= loaded
        if k % CHUNK == 0:
            copies[k // CHUNK].wait()
        return high[k]

    terms = products(tile_of, pick(source_pick[...], field.astype(BF16)), turn=True)
    out[...] = gather(rows_pair[...], scale[...], terms)


def start_data_kernel(count, *refs):
    low, high, rows_pick, source_pair, scale, observed, data_weight, turned = refs[:8]
    parts = refs[8 : 8 + count]
    out = refs[8 + count]
    total = total_rows(parts)
    data = (data_weight[...] * (observed[...] - total)).astype(BF16)
    terms = products(kept_tiles(low, high), pick(rows_pick[...], data))
    out[...] = gather(source_pair[...], scale[...], terms)


def start_residual_kernel(blocks, count, *refs):
    low, high, source_pick, rows_pair, scale, start, weight = refs[:7]
    parts = refs[7 : 7 + count]
    out, residual = refs[7 + count :]
    weights = weight[...]
    value = total_blocks(parts, blocks) - weights * start[...]
    residual[...] = value
    terms = products(kept_tiles(low, high), pick(source_pick[...], value.astype(BF16)))
    data_rows = rows_pair.shape[0]
    out[:data_rows, :] = gather(rows_pair[...], scale[...], terms)
    out[data_rows:, :] = pack_rows(
        [columns(value * value), columns(value * weights * value)], value.shape[1]
    )


def image_data_kernel(count, *refs):
    low, high, rows_pick, source_pair, scale, data_weight = refs[:6]
    parts = refs[6 : 6 + count]
    out, predicted, sums = refs[6 + count :]
    data_rows = data_weight.shape[0]
    whole_part = total_rows(parts)
    total = whole_part[:data_rows, :]
    predicted[...] = total
    sums[...] = whole_part[data_rows:, :]
    data = (data_weight[...] * (0.0 - total)).astype(BF16)
    terms = products(kept_tiles(low, high), pick(rows_pick[...], data))
    cells = source_pair.shape[0]
    out[:cells, :] = gather(source_pair[...], scale[...], terms)
    out[cells:, :] = pack_rows([columns(total * data.astype(F32))], total.shape[1])


def residual_kernel(blocks, count, *refs):
    low, high, source_pick, rows_pair, scale, weight, direction, sums = refs[:8]
    parts = refs[8 : 8 + count]
    out, residual, step = refs[8 + count :]
    cells = source_pick.shape[1]
    weights = weight[...]
    along = direction[...]
    image = weights * along - total_blocks(parts, blocks)
    curve = whole(sums[1:2, :]) - whole(extra_rows(parts, cells)[0:1, :])
    alpha = whole(sums[0:1, :]) / curve
    step[...] = jnp.broadcast_to(alpha, step.shape)
    value = residual_of(along, alpha, image)
    residual[...] = value
    terms = products(kept_tiles(low, high), pick(source_pick[...], value.astype(BF16)))
    data_rows = rows_pair.shape[0]
    out[:data_rows, :] = gather(rows_pair[...], scale[...], terms)
    weighted = value * weights
    out[data_rows:, :] = pack_rows(
        [columns(value * value), columns(weighted * value), columns(weighted * along)],
        value.shape[1],
    )


def residual_of(residual, alpha, image):
    return residual - alpha * image


def second_data_kernel(blocks, count, *refs):
    low, high, rows_pick, source_pair, scale, data_weight, predicted, sums = refs[:8]
    parts = refs[8 : 8 + count]
    outs, scalars = refs[8 + count : -1], refs[-1]
    data_rows = data_weight.shape[0]
    whole_part = total_rows(parts)
    norm = whole(whole_part[data_rows : data_rows + 1, :])
    beta = norm / whole(sums[0:1, :])
    curve = whole(
        whole_part[data_rows + 1 : data_rows + 2, :]
        + 2.0 * beta * whole_part[data_rows + 2 : data_rows + 3, :]
        + beta * beta * sums[1:2, :]
    )
    total = whole_part[:data_rows, :] + beta * predicted[...]
    data = (data_weight[...] * (0.0 - total)).astype(BF16)
    terms = products(kept_tiles(low, high), pick(rows_pick[...], data))
    cells = gather(source_pair[...], scale[...], terms)
    curved = columns(total * data.astype(F32))
    for group, out in enumerate(outs):
        out[:blocks, :] = cells[group * blocks : (group + 1) * blocks, :]
        out[blocks:, :] = jnp.broadcast_to(curved, (out.shape[0] - blocks, total.shape[1]))
    wide = (1, scalars.shape[1])
    scalars[...] = pack_rows(
        [jnp.broadcast_to(value, wide) for value in (norm, beta, curve)], scalars.shape[1]
    )


def last_kernel(blocks, count, *refs):
    weight, start, first, second, step, scalars = refs[:6]
    parts = refs[6 : 6 + count]
    model, residual = refs[6 + count :]
    norm = scalars[0:1, 0:1]
    beta = scalars[1:2, 0:1]
    curve = scalars[2:3, 0:1]
    along = first[:blocks, :]
    left = second[:blocks, :]
    direction = left + beta * along
    whole_part = total_rows(parts)
    image = weight[:blocks, :] * direction - whole_part[:blocks, :]
    alpha = norm / (curve - whole(whole_part[blocks : blocks + 1, :]))
    model[...] = start[:blocks, :] + step[0:1, 0:1] * along + alpha * direction
    residual[...] = left - alpha * image


def call(body, outs, *args, scratch=()):
    specs = []
    for arg in args:
        far = getattr(jax.typeof(arg), "memory_space", None) == pltpu.HBM
        space = pl.ANY if far else pltpu.SMEM if arg.ndim == 1 else pltpu.VMEM
        specs.append(pl.BlockSpec(memory_space=space))
    return pl.pallas_call(
        body,
        out_shape=[jax.ShapeDtypeStruct(shape, dtype) for shape, dtype in outs],
        in_specs=specs,
        out_specs=[pl.BlockSpec(memory_space=pltpu.VMEM)] * len(outs),
        scratch_shapes=list(scratch),
        compiler_params=pltpu.CompilerParams(vmem_limit_bytes=LIMIT),
    )(*args)


def shards(
    tile_codes,
    tile_scale,
    tile_row,
    tile_column,
    send_index,
    model_start,
    reg_weight,
    observed,
    data_weight,
):
    blocks, width = model_start.shape
    slots = send_index.shape[2]
    data_rows = observed.shape[0]
    tiles = tile_codes.shape[0]
    count = lax.axis_size("tiles")
    sharing = lax.axis_size(("split", "depth"))
    cells = count * blocks
    half = tiles // 2
    loaded = tiles * 3 // 4
    codes = pltpu.with_memory_space_constraint(tile_codes, pltpu.HBM)
    half_shape = (half, width, width)
    place = lax.axis_index("tiles").astype(jnp.int32).reshape(1)

    def across(values):
        return exchange(values, "tiles", count)

    def within(value):
        return exchange([value] * sharing, ("split", "depth"), sharing)

    named = jnp.transpose(send_index, (0, 2, 1)).reshape(slots, count)
    (opening,) = call(
        opening_kernel,
        [((2 * blocks + EXTRA, width), F32)],
        pltpu.with_memory_space_constraint(model_start, pltpu.HBM),
        pltpu.with_memory_space_constraint(reg_weight, pltpu.HBM),
        pltpu.with_memory_space_constraint(named, pltpu.HBM),
        scratch=[
            pltpu.VMEM((blocks, width), F32),
            pltpu.VMEM((blocks, width), F32),
            pltpu.VMEM((slots, count), jnp.int32),
            pltpu.SemaphoreType.DMA((3,)),
        ],
    )
    begin = across([opening] * count)
    low, rows_pick, rows_pair, scale = call(
        loading_kernel,
        [
            ((loaded, width, width), BF16),
            ((tiles, data_rows), BF16),
            ((data_rows, 2 * tiles), BF16),
            ((tiles, width), F32),
        ],
        codes,
        opening,
        pltpu.with_memory_space_constraint(tile_scale.reshape(1, -1), pltpu.HBM),
        pltpu.with_memory_space_constraint(tile_row.reshape(1, -1), pltpu.HBM),
        scratch=[
            pltpu.VMEM((1, tiles), F32),
            pltpu.VMEM((1, tiles), jnp.int32),
            pltpu.SemaphoreType.DMA((loaded // CHUNK,)),
            pltpu.SemaphoreType.DMA((2,)),
        ],
    )
    part, high, source_pick, source_pair, start, weight = call(
        functools.partial(first_kernel, blocks, slots, count),
        [
            ((data_rows, width), F32),
            ((tiles - loaded, width, width), BF16),
            ((tiles, cells), BF16),
            ((cells, 2 * tiles), BF16),
            ((cells, width), F32),
            ((cells, width), F32),
        ],
        codes,
        low,
        scale,
        rows_pair,
        tile_column.reshape(1, -1),
        place,
        *begin,
        scratch=[pltpu.SemaphoreType.DMA(((tiles - loaded) // CHUNK,))],
    )

    def turned_half(first, part):
        (turned,) = call(
            functools.partial(turning_kernel, first), [(half_shape, BF16)], low, high, part
        )
        return turned

    parts = within(part)
    low_turned = turned_half(0, part)
    (part,) = call(
        functools.partial(start_data_kernel, sharing),
        [((cells, width), F32)],
        low,
        high,
        rows_pick,
        source_pair,
        scale,
        observed,
        data_weight,
        low_turned,
        *parts,
    )
    parts = across([part] * count)
    high_turned = turned_half(half, part)
    part, first = call(
        functools.partial(start_residual_kernel, blocks, count),
        [((data_rows + EXTRA, width), F32), ((cells, width), F32)],
        low_turned,
        high_turned,
        source_pick,
        rows_pair,
        scale,
        start,
        weight,
        *parts,
    )
    part, predicted, sums = call(
        functools.partial(image_data_kernel, sharing),
        [((cells + EXTRA, width), F32), ((data_rows, width), F32), ((EXTRA, width), F32)],
        low,
        high,
        rows_pick,
        source_pair,
        scale,
        data_weight,
        *within(part),
    )
    part, second, step = call(
        functools.partial(residual_kernel, blocks, count),
        [((data_rows + EXTRA, width), F32), ((cells, width), F32), ((8, 128), F32)],
        low_turned,
        high_turned,
        source_pick,
        rows_pair,
        scale,
        weight,
        first,
        sums,
        *across([part] * count),
    )
    *part, scalars = call(
        functools.partial(second_data_kernel, blocks, sharing),
        [((blocks + 4, width), F32)] * count + [((EXTRA, width), F32)],
        low,
        high,
        rows_pick,
        source_pair,
        scale,
        data_weight,
        predicted,
        sums,
        *within(part),
    )
    model, residual = call(
        functools.partial(last_kernel, blocks, count),
        [((blocks, width), F32), ((blocks, width), F32)],
        weight,
        start,
        first,
        second,
        step,
        scalars,
        *across(part),
    )
    return (model, residual)


def solution(mesh):
    both = P(("groups", "tiles", "split", "depth"))
    owned = P(("groups", "tiles", "split", "depth"), None)
    wide = P(("groups", "tiles", "split", "depth"), None, None)
    data = P(("groups", "tiles"), None)
    in_specs = (wide, both, both, both, wide, owned, owned, data, data)
    return jax.shard_map(
        shards, mesh=mesh, in_specs=in_specs, out_specs=(owned, owned), check_vma=False
    )
```

```python
import functools

import jax
import jax.numpy as jnp
from jax import lax
from jax.experimental import pallas as pl
from jax.experimental.pallas import tpu as pltpu
from jax.sharding import PartitionSpec as P

HIGH = lax.Precision.HIGHEST
EXTRA = 8
LIMIT = 16 * 1024 * 1024
GROUP = 16
CHUNK = 8
F32 = jnp.float32
BF16 = jnp.bfloat16


def exchange(values, axes, size):
    parts = [values[0]] + [None] * (size - 1)
    for shift in range(size - 1, 0, -1):
        perm = [(i, i ^ shift) for i in range(size)]
        parts[shift] = lax.ppermute(values[shift], axes, perm)
    return parts


def total_rows(parts):
    total = parts[0][...]
    for part in parts[1:]:
        total = total + part[...]
    return total


def total_blocks(parts, blocks):
    count = len(parts)
    groups = []
    for group in range(count):
        total = None
        for shift in range(count):
            start = (group ^ shift) * blocks
            piece = parts[shift][start : start + blocks, :]
            total = piece if total is None else total + piece
        groups.append(total)
    return jnp.concatenate(groups, axis=0)


def extra_rows(parts, start):
    total = parts[0][start : start + EXTRA, :]
    for part in parts[1:]:
        total = total + part[start : start + EXTRA, :]
    return total


def whole(value):
    return jnp.sum(value, axis=(0, 1), keepdims=True)


def columns(value):
    return jnp.sum(value, axis=0, keepdims=True)


def pack_rows(rows, width):
    filled = list(rows)
    while len(filled) < EXTRA:
        filled.append(jnp.zeros((1, width), F32))
    return jnp.concatenate(filled, axis=0)


def products(codes, picked):
    tiles, width = picked.shape
    index = lax.broadcasted_iota(jnp.int32, (GROUP, width), 0)
    pieces = []
    for first in range(0, tiles, GROUP):
        rows = picked[first : first + GROUP, :]
        total = None
        for i in range(GROUP):
            value = jnp.dot(rows, codes[first + i], preferred_element_type=F32)
            total = value if total is None else jnp.where(index == i, value, total)
        pieces.append(total)
    return jnp.concatenate(pieces, axis=0)


def pick(table, values):
    return jnp.dot(table, values, preferred_element_type=F32).astype(BF16)


def gather(table, scale, terms):
    scaled = scale * terms
    upper = scaled.astype(BF16)
    lower = (scaled - upper.astype(F32)).astype(BF16)
    both = jnp.concatenate([upper, lower], axis=0)
    return jnp.dot(table, both, preferred_element_type=F32)


def tables(index, values, picks, pairs):
    tiles = index.shape[1]
    hits = lax.broadcasted_iota(jnp.int32, (values, tiles), 0) == index
    ones = jnp.where(hits, 1.0, 0.0)
    picks[...] = ones.T.astype(BF16)
    pairs[...] = jnp.concatenate([ones, ones], axis=1).astype(BF16)


def turning_kernel(codes, opening, far_scale, far_row, *refs):
    turned, rows_pick, rows_pair, wide_scale, scale, row, done = refs
    copies = [
        pltpu.make_async_copy(far_scale, scale, done.at[0]),
        pltpu.make_async_copy(far_row, row, done.at[1]),
    ]
    for copy in copies:
        copy.start()
    tiles, width = wide_scale.shape
    for k in range(tiles):
        turned[k] = codes[k].T
    for copy in copies:
        copy.wait()
    tables(row[...], rows_pick.shape[1], rows_pick, rows_pair)
    square = (tiles, tiles)
    same = lax.broadcasted_iota(jnp.int32, square, 0) == lax.broadcasted_iota(jnp.int32, square, 1)
    wide_scale[...] = jnp.dot(
        jnp.where(same, scale[...], 0.0),
        jnp.ones((tiles, width), F32),
        precision=HIGH,
        preferred_element_type=F32,
    )


def opening_kernel(start, weight, named, out, sources, weights, names, done):
    copies = [
        pltpu.make_async_copy(start, sources, done.at[0]),
        pltpu.make_async_copy(weight, weights, done.at[1]),
        pltpu.make_async_copy(named, names, done.at[2]),
    ]
    for copy in copies:
        copy.start()
    blocks, width = sources.shape
    slots, count = names.shape
    rest = out.shape[0] - 2 * blocks
    out[2 * blocks :, :] = jnp.zeros((rest, width), F32)
    for copy in copies:
        copy.wait()
    out[:blocks, :] = sources[...]
    out[blocks : 2 * blocks, :] = weights[...]
    out[2 * blocks : 2 * blocks + slots, :count] = names[...].astype(F32)


def first_kernel(blocks, slots, count, *refs):
    turned, scale, rows_pair, column, place = refs[:5]
    parts = refs[5 : 5 + count]
    out, source_pick, source_pair, start, weight = refs[5 + count :]
    width = out.shape[1]
    here = place[0]
    columns_of = column[...]
    source = jnp.where(columns_of < blocks, columns_of, 0)
    lane = lax.broadcasted_iota(jnp.int32, (1, width), 1)
    for shift in range(count):
        other = jnp.bitwise_xor(here, shift)
        for slot in range(slots):
            named = parts[shift][2 * blocks + slot : 2 * blocks + slot + 1, :]
            mine = jnp.where(lane == here, named, 0.0)
            block = jnp.sum(mine, axis=1, keepdims=True).astype(jnp.int32) + shift * blocks
            source = jnp.where(columns_of == blocks + other * slots + slot, block, source)
    tables(source, count * blocks, source_pick, source_pair)
    field = jnp.concatenate([part[:blocks, :] for part in parts], axis=0)
    start[...] = field
    weight[...] = jnp.concatenate([part[blocks : 2 * blocks, :] for part in parts], axis=0)

    terms = products(turned, pick(source_pick[...], field.astype(BF16)))
    out[...] = gather(rows_pair[...], scale[...], terms)


def start_data_kernel(count, *refs):
    codes, rows_pick, source_pair, scale, observed, data_weight = refs[:6]
    parts = refs[6 : 6 + count]
    out = refs[6 + count]
    total = total_rows(parts)
    data = (data_weight[...] * (observed[...] - total)).astype(BF16)
    terms = products(codes, pick(rows_pick[...], data))
    out[...] = gather(source_pair[...], scale[...], terms)


def start_residual_kernel(blocks, count, *refs):
    codes, source_pick, rows_pair, scale, start, weight = refs[:6]
    parts = refs[6 : 6 + count]
    out, residual = refs[6 + count :]
    weights = weight[...]
    value = total_blocks(parts, blocks) - weights * start[...]
    residual[...] = value
    terms = products(codes, pick(source_pick[...], value.astype(BF16)))
    data_rows = rows_pair.shape[0]
    out[:data_rows, :] = gather(rows_pair[...], scale[...], terms)
    out[data_rows:, :] = pack_rows(
        [columns(value * value), columns(value * weights * value)], value.shape[1]
    )


def image_data_kernel(count, *refs):
    codes, rows_pick, source_pair, scale, data_weight = refs[:5]
    parts = refs[5 : 5 + count]
    out, predicted, sums = refs[5 + count :]
    data_rows = data_weight.shape[0]
    whole_part = total_rows(parts)
    total = whole_part[:data_rows, :]
    predicted[...] = total
    sums[...] = whole_part[data_rows:, :]
    data = (data_weight[...] * (0.0 - total)).astype(BF16)
    terms = products(codes, pick(rows_pick[...], data))
    cells = source_pair.shape[0]
    out[:cells, :] = gather(source_pair[...], scale[...], terms)
    out[cells:, :] = pack_rows([columns(total * data.astype(F32))], total.shape[1])


def residual_kernel(blocks, count, *refs):
    codes, source_pick, rows_pair, scale, weight, direction, sums = refs[:7]
    parts = refs[7 : 7 + count]
    out, residual, step = refs[7 + count :]
    cells = source_pick.shape[1]
    weights = weight[...]
    along = direction[...]
    image = weights * along - total_blocks(parts, blocks)
    curve = whole(sums[1:2, :]) - whole(extra_rows(parts, cells)[0:1, :])
    alpha = whole(sums[0:1, :]) / curve
    step[...] = jnp.broadcast_to(alpha, step.shape)
    value = residual_of(along, alpha, image)
    residual[...] = value
    terms = products(codes, pick(source_pick[...], value.astype(BF16)))
    data_rows = rows_pair.shape[0]
    out[:data_rows, :] = gather(rows_pair[...], scale[...], terms)
    weighted = value * weights
    out[data_rows:, :] = pack_rows(
        [columns(value * value), columns(weighted * value), columns(weighted * along)],
        value.shape[1],
    )


def residual_of(residual, alpha, image):
    return residual - alpha * image


def second_data_kernel(blocks, count, *refs):
    codes, rows_pick, source_pair, scale, data_weight, predicted, sums = refs[:7]
    parts = refs[7 : 7 + count]
    outs, scalars = refs[7 + count : -1], refs[-1]
    data_rows = data_weight.shape[0]
    whole_part = total_rows(parts)
    norm = whole(whole_part[data_rows : data_rows + 1, :])
    beta = norm / whole(sums[0:1, :])
    curve = whole(
        whole_part[data_rows + 1 : data_rows + 2, :]
        + 2.0 * beta * whole_part[data_rows + 2 : data_rows + 3, :]
        + beta * beta * sums[1:2, :]
    )
    total = whole_part[:data_rows, :] + beta * predicted[...]
    data = (data_weight[...] * (0.0 - total)).astype(BF16)
    terms = products(codes, pick(rows_pick[...], data))
    cells = gather(source_pair[...], scale[...], terms)
    curved = columns(total * data.astype(F32))
    for group, out in enumerate(outs):
        out[:blocks, :] = cells[group * blocks : (group + 1) * blocks, :]
        out[blocks:, :] = jnp.broadcast_to(curved, (out.shape[0] - blocks, total.shape[1]))
    wide = (1, scalars.shape[1])
    scalars[...] = pack_rows(
        [jnp.broadcast_to(value, wide) for value in (norm, beta, curve)], scalars.shape[1]
    )


def last_kernel(blocks, count, *refs):
    weight, start, first, second, step, scalars = refs[:6]
    parts = refs[6 : 6 + count]
    model, residual = refs[6 + count :]
    norm = scalars[0:1, 0:1]
    beta = scalars[1:2, 0:1]
    curve = scalars[2:3, 0:1]
    along = first[:blocks, :]
    left = second[:blocks, :]
    direction = left + beta * along
    whole_part = total_rows(parts)
    image = weight[:blocks, :] * direction - whole_part[:blocks, :]
    alpha = norm / (curve - whole(whole_part[blocks : blocks + 1, :]))
    model[...] = start[:blocks, :] + step[0:1, 0:1] * along + alpha * direction
    residual[...] = left - alpha * image


def call(body, outs, *args, scratch=(), cost=None):
    specs = []
    for arg in args:
        far = getattr(jax.typeof(arg), "memory_space", None) == pltpu.HBM
        space = pl.ANY if far else pltpu.SMEM if arg.ndim == 1 else pltpu.VMEM
        specs.append(pl.BlockSpec(memory_space=space))
    return pl.pallas_call(
        body,
        out_shape=[jax.ShapeDtypeStruct(shape, dtype) for shape, dtype in outs],
        in_specs=specs,
        out_specs=[pl.BlockSpec(memory_space=pltpu.VMEM)] * len(outs),
        scratch_shapes=list(scratch),
        cost_estimate=cost,
        compiler_params=pltpu.CompilerParams(vmem_limit_bytes=LIMIT),
    )(*args)


def shards(
    tile_codes,
    tile_scale,
    tile_row,
    tile_column,
    send_index,
    model_start,
    reg_weight,
    observed,
    data_weight,
):
    blocks, width = model_start.shape
    slots = send_index.shape[2]
    data_rows = observed.shape[0]
    tiles = tile_codes.shape[0]
    count = lax.axis_size("tiles")
    sharing = lax.axis_size(("split", "depth"))
    cells = count * blocks
    codes = tile_codes
    place = lax.axis_index("tiles").astype(jnp.int32).reshape(1)

    def across(values):
        return exchange(values, "tiles", count)

    def within(value):
        return exchange([value] * sharing, ("split", "depth"), sharing)

    named = jnp.transpose(send_index, (0, 2, 1)).reshape(slots, count)
    (opening,) = call(
        opening_kernel,
        [((2 * blocks + EXTRA, width), F32)],
        pltpu.with_memory_space_constraint(model_start, pltpu.HBM),
        pltpu.with_memory_space_constraint(reg_weight, pltpu.HBM),
        pltpu.with_memory_space_constraint(named, pltpu.HBM),
        scratch=[
            pltpu.VMEM((blocks, width), F32),
            pltpu.VMEM((blocks, width), F32),
            pltpu.VMEM((slots, count), jnp.int32),
            pltpu.SemaphoreType.DMA((3,)),
        ],
        cost=pl.CostEstimate(flops=16 * width * codes.size, transcendentals=0, bytes_accessed=0),
    )
    begin = across([opening] * count)
    turned, rows_pick, rows_pair, scale = call(
        turning_kernel,
        [
            (codes.shape, BF16),
            ((tiles, data_rows), BF16),
            ((data_rows, 2 * tiles), BF16),
            ((tiles, width), F32),
        ],
        codes,
        opening,
        pltpu.with_memory_space_constraint(tile_scale.reshape(1, -1), pltpu.HBM),
        pltpu.with_memory_space_constraint(tile_row.reshape(1, -1), pltpu.HBM),
        scratch=[
            pltpu.VMEM((1, tiles), F32),
            pltpu.VMEM((1, tiles), jnp.int32),
            pltpu.SemaphoreType.DMA((2,)),
        ],
    )
    part, source_pick, source_pair, start, weight = call(
        functools.partial(first_kernel, blocks, slots, count),
        [
            ((data_rows, width), F32),
            ((tiles, cells), BF16),
            ((cells, 2 * tiles), BF16),
            ((cells, width), F32),
            ((cells, width), F32),
        ],
        turned,
        scale,
        rows_pair,
        tile_column.reshape(1, -1),
        place,
        *begin,
    )
    (part,) = call(
        functools.partial(start_data_kernel, sharing),
        [((cells, width), F32)],
        codes,
        rows_pick,
        source_pair,
        scale,
        observed,
        data_weight,
        *within(part),
    )
    part, first = call(
        functools.partial(start_residual_kernel, blocks, count),
        [((data_rows + EXTRA, width), F32), ((cells, width), F32)],
        turned,
        source_pick,
        rows_pair,
        scale,
        start,
        weight,
        *across([part] * count),
    )
    part, predicted, sums = call(
        functools.partial(image_data_kernel, sharing),
        [((cells + EXTRA, width), F32), ((data_rows, width), F32), ((EXTRA, width), F32)],
        codes,
        rows_pick,
        source_pair,
        scale,
        data_weight,
        *within(part),
    )
    part, second, step = call(
        functools.partial(residual_kernel, blocks, count),
        [((data_rows + EXTRA, width), F32), ((cells, width), F32), ((8, 128), F32)],
        turned,
        source_pick,
        rows_pair,
        scale,
        weight,
        first,
        sums,
        *across([part] * count),
    )
    *part, scalars = call(
        functools.partial(second_data_kernel, blocks, sharing),
        [((blocks + 4, width), F32)] * count + [((EXTRA, width), F32)],
        codes,
        rows_pick,
        source_pair,
        scale,
        data_weight,
        predicted,
        sums,
        *within(part),
    )
    model, residual = call(
        functools.partial(last_kernel, blocks, count),
        [((blocks, width), F32), ((blocks, width), F32)],
        weight,
        start,
        first,
        second,
        step,
        scalars,
        *across(part),
    )
    return (model, residual)


def solution(mesh):
    both = P(("groups", "tiles", "split", "depth"))
    owned = P(("groups", "tiles", "split", "depth"), None)
    wide = P(("groups", "tiles", "split", "depth"), None, None)
    data = P(("groups", "tiles"), None)
    in_specs = (wide, both, both, both, wide, owned, owned, data, data)
    return jax.shard_map(
        shards, mesh=mesh, in_specs=in_specs, out_specs=(owned, owned), check_vma=False
    )
```

```python
import functools

import jax
import jax.numpy as jnp
from jax import lax
from jax.experimental import pallas as pl
from jax.experimental.pallas import tpu as pltpu
from jax.sharding import PartitionSpec as P

HIGH = lax.Precision.HIGHEST
EXTRA = 8
LIMIT = 16 * 1024 * 1024
GROUP = 16
CHUNK = 8
F32 = jnp.float32
BF16 = jnp.bfloat16


def exchange(values, axes, size):
    parts = [values[0]] + [None] * (size - 1)
    for shift in range(size - 1, 0, -1):
        perm = [(i, i ^ shift) for i in range(size)]
        parts[shift] = lax.ppermute(values[shift], axes, perm)
    return parts


def total_rows(parts):
    total = parts[0][...]
    for part in parts[1:]:
        total = total + part[...]
    return total


def total_blocks(parts, blocks):
    count = len(parts)
    groups = []
    for group in range(count):
        total = None
        for shift in range(count):
            start = (group ^ shift) * blocks
            piece = parts[shift][start : start + blocks, :]
            total = piece if total is None else total + piece
        groups.append(total)
    return jnp.concatenate(groups, axis=0)


def extra_rows(parts, start):
    total = parts[0][start : start + EXTRA, :]
    for part in parts[1:]:
        total = total + part[start : start + EXTRA, :]
    return total


def whole(value):
    return jnp.sum(value, axis=(0, 1), keepdims=True)


def columns(value):
    return jnp.sum(value, axis=0, keepdims=True)


def pack_rows(rows, width):
    filled = list(rows)
    while len(filled) < EXTRA:
        filled.append(jnp.zeros((1, width), F32))
    return jnp.concatenate(filled, axis=0)


def products(codes, picked):
    tiles, width = picked.shape
    index = lax.broadcasted_iota(jnp.int32, (GROUP, width), 0)
    pieces = []
    for first in range(0, tiles, GROUP):
        rows = picked[first : first + GROUP, :]
        total = None
        for i in range(GROUP):
            value = jnp.dot(rows, codes[first + i], preferred_element_type=F32)
            total = value if total is None else jnp.where(index == i, value, total)
        pieces.append(total)
    return jnp.concatenate(pieces, axis=0)


def pick(table, values):
    return jnp.dot(table, values, preferred_element_type=F32).astype(BF16)


def gather(table, scale, terms):
    scaled = scale * terms
    upper = scaled.astype(BF16)
    lower = (scaled - upper.astype(F32)).astype(BF16)
    both = jnp.concatenate([upper, lower], axis=0)
    return jnp.dot(table, both, preferred_element_type=F32)


def tables(index, values, picks, pairs):
    tiles = index.shape[1]
    hits = lax.broadcasted_iota(jnp.int32, (values, tiles), 0) == index
    ones = jnp.where(hits, 1.0, 0.0)
    picks[...] = ones.T.astype(BF16)
    pairs[...] = jnp.concatenate([ones, ones], axis=1).astype(BF16)


def turning_kernel(codes, opening, far_scale, far_row, *refs):
    turned, rows_pick, rows_pair, wide_scale, scale, row, done = refs
    copies = [
        pltpu.make_async_copy(far_scale, scale, done.at[0]),
        pltpu.make_async_copy(far_row, row, done.at[1]),
    ]
    for copy in copies:
        copy.start()
    tiles, width = wide_scale.shape
    for k in range(tiles):
        turned[k] = codes[k].T
    for copy in copies:
        copy.wait()
    tables(row[...], rows_pick.shape[1], rows_pick, rows_pair)
    square = (tiles, tiles)
    same = lax.broadcasted_iota(jnp.int32, square, 0) == lax.broadcasted_iota(jnp.int32, square, 1)
    wide_scale[...] = jnp.dot(
        jnp.where(same, scale[...], 0.0),
        jnp.ones((tiles, width), F32),
        precision=HIGH,
        preferred_element_type=F32,
    )


def opening_kernel(start, weight, named, out, sources, weights, names, done):
    copies = [
        pltpu.make_async_copy(start, sources, done.at[0]),
        pltpu.make_async_copy(weight, weights, done.at[1]),
        pltpu.make_async_copy(named, names, done.at[2]),
    ]
    for copy in copies:
        copy.start()
    blocks, width = sources.shape
    slots, count = names.shape
    rest = out.shape[0] - 2 * blocks
    out[2 * blocks :, :] = jnp.zeros((rest, width), F32)
    for copy in copies:
        copy.wait()
    out[:blocks, :] = sources[...]
    out[blocks : 2 * blocks, :] = weights[...]
    out[2 * blocks : 2 * blocks + slots, :count] = names[...].astype(F32)


def first_kernel(blocks, slots, count, *refs):
    turned, scale, rows_pair, column, place = refs[:5]
    parts = refs[5 : 5 + count]
    out, source_pick, source_pair, start, weight = refs[5 + count :]
    width = out.shape[1]
    here = place[0]
    columns_of = column[...]
    source = jnp.where(columns_of < blocks, columns_of, 0)
    lane = lax.broadcasted_iota(jnp.int32, (1, width), 1)
    for shift in range(count):
        other = jnp.bitwise_xor(here, shift)
        for slot in range(slots):
            named = parts[shift][2 * blocks + slot : 2 * blocks + slot + 1, :]
            mine = jnp.where(lane == here, named, 0.0)
            block = jnp.sum(mine, axis=1, keepdims=True).astype(jnp.int32) + shift * blocks
            source = jnp.where(columns_of == blocks + other * slots + slot, block, source)
    tables(source, count * blocks, source_pick, source_pair)
    field = jnp.concatenate([part[:blocks, :] for part in parts], axis=0)
    start[...] = field
    weight[...] = jnp.concatenate([part[blocks : 2 * blocks, :] for part in parts], axis=0)

    terms = products(turned, pick(source_pick[...], field.astype(BF16)))
    out[...] = gather(rows_pair[...], scale[...], terms)


def start_data_kernel(count, *refs):
    codes, rows_pick, source_pair, scale, observed, data_weight = refs[:6]
    parts = refs[6 : 6 + count]
    out = refs[6 + count]
    total = total_rows(parts)
    data = (data_weight[...] * (observed[...] - total)).astype(BF16)
    terms = products(codes, pick(rows_pick[...], data))
    out[...] = gather(source_pair[...], scale[...], terms)


def start_residual_kernel(blocks, count, *refs):
    codes, source_pick, rows_pair, scale, start, weight = refs[:6]
    parts = refs[6 : 6 + count]
    out, residual = refs[6 + count :]
    weights = weight[...]
    value = total_blocks(parts, blocks) - weights * start[...]
    residual[...] = value
    terms = products(codes, pick(source_pick[...], value.astype(BF16)))
    data_rows = rows_pair.shape[0]
    out[:data_rows, :] = gather(rows_pair[...], scale[...], terms)
    out[data_rows:, :] = pack_rows(
        [columns(value * value), columns(value * weights * value)], value.shape[1]
    )


def image_data_kernel(count, *refs):
    codes, rows_pick, source_pair, scale, data_weight = refs[:5]
    parts = refs[5 : 5 + count]
    out, predicted, sums = refs[5 + count :]
    data_rows = data_weight.shape[0]
    whole_part = total_rows(parts)
    total = whole_part[:data_rows, :]
    predicted[...] = total
    sums[...] = whole_part[data_rows:, :]
    data = (data_weight[...] * (0.0 - total)).astype(BF16)
    terms = products(codes, pick(rows_pick[...], data))
    cells = source_pair.shape[0]
    out[:cells, :] = gather(source_pair[...], scale[...], terms)
    out[cells:, :] = pack_rows([columns(total * data.astype(F32))], total.shape[1])


def residual_kernel(blocks, count, *refs):
    codes, source_pick, rows_pair, scale, weight, direction, sums = refs[:7]
    parts = refs[7 : 7 + count]
    out, residual, step = refs[7 + count :]
    cells = source_pick.shape[1]
    weights = weight[...]
    along = direction[...]
    image = weights * along - total_blocks(parts, blocks)
    curve = whole(sums[1:2, :]) - whole(extra_rows(parts, cells)[0:1, :])
    alpha = whole(sums[0:1, :]) / curve
    step[...] = jnp.broadcast_to(alpha, step.shape)
    value = residual_of(along, alpha, image)
    residual[...] = value
    terms = products(codes, pick(source_pick[...], value.astype(BF16)))
    data_rows = rows_pair.shape[0]
    out[:data_rows, :] = gather(rows_pair[...], scale[...], terms)
    weighted = value * weights
    out[data_rows:, :] = pack_rows(
        [columns(value * value), columns(weighted * value), columns(weighted * along)],
        value.shape[1],
    )


def residual_of(residual, alpha, image):
    return residual - alpha * image


def second_data_kernel(blocks, count, *refs):
    codes, rows_pick, source_pair, scale, data_weight, predicted, sums = refs[:7]
    parts = refs[7 : 7 + count]
    outs, scalars = refs[7 + count : -1], refs[-1]
    data_rows = data_weight.shape[0]
    whole_part = total_rows(parts)
    norm = whole(whole_part[data_rows : data_rows + 1, :])
    beta = norm / whole(sums[0:1, :])
    curve = whole(
        whole_part[data_rows + 1 : data_rows + 2, :]
        + 2.0 * beta * whole_part[data_rows + 2 : data_rows + 3, :]
        + beta * beta * sums[1:2, :]
    )
    total = whole_part[:data_rows, :] + beta * predicted[...]
    data = (data_weight[...] * (0.0 - total)).astype(BF16)
    terms = products(codes, pick(rows_pick[...], data))
    cells = gather(source_pair[...], scale[...], terms)
    curved = columns(total * data.astype(F32))
    for group, out in enumerate(outs):
        out[:blocks, :] = cells[group * blocks : (group + 1) * blocks, :]
        out[blocks:, :] = jnp.broadcast_to(curved, (out.shape[0] - blocks, total.shape[1]))
    wide = (1, scalars.shape[1])
    scalars[...] = pack_rows(
        [jnp.broadcast_to(value, wide) for value in (norm, beta, curve)], scalars.shape[1]
    )


def last_kernel(blocks, count, *refs):
    weight, start, first, second, step, scalars = refs[:6]
    parts = refs[6 : 6 + count]
    model, residual = refs[6 + count :]
    norm = scalars[0:1, 0:1]
    beta = scalars[1:2, 0:1]
    curve = scalars[2:3, 0:1]
    along = first[:blocks, :]
    left = second[:blocks, :]
    direction = left + beta * along
    whole_part = total_rows(parts)
    image = weight[:blocks, :] * direction - whole_part[:blocks, :]
    alpha = norm / (curve - whole(whole_part[blocks : blocks + 1, :]))
    model[...] = start[:blocks, :] + step[0:1, 0:1] * along + alpha * direction
    residual[...] = left - alpha * image


def call(body, outs, *args, scratch=(), cost=None):
    specs = []
    for arg in args:
        far = getattr(jax.typeof(arg), "memory_space", None) == pltpu.HBM
        space = pl.ANY if far else pltpu.SMEM if arg.ndim == 1 else pltpu.VMEM
        specs.append(pl.BlockSpec(memory_space=space))
    return pl.pallas_call(
        body,
        out_shape=[jax.ShapeDtypeStruct(shape, dtype) for shape, dtype in outs],
        in_specs=specs,
        out_specs=[pl.BlockSpec(memory_space=pltpu.VMEM)] * len(outs),
        scratch_shapes=list(scratch),
        cost_estimate=cost,
        compiler_params=pltpu.CompilerParams(vmem_limit_bytes=LIMIT),
    )(*args)


def shards(
    tile_codes,
    tile_scale,
    tile_row,
    tile_column,
    send_index,
    model_start,
    reg_weight,
    observed,
    data_weight,
):
    blocks, width = model_start.shape
    slots = send_index.shape[2]
    data_rows = observed.shape[0]
    tiles = tile_codes.shape[0]
    count = lax.axis_size("tiles")
    sharing = lax.axis_size(("split", "depth"))
    cells = count * blocks
    codes = tile_codes
    place = lax.axis_index("tiles").astype(jnp.int32).reshape(1)

    def across(values):
        return exchange(values, "tiles", count)

    def within(value):
        return exchange([value] * sharing, ("split", "depth"), sharing)

    named = jnp.transpose(send_index, (0, 2, 1)).reshape(slots, count)
    (opening,) = call(
        opening_kernel,
        [((2 * blocks + EXTRA, width), F32)],
        pltpu.with_memory_space_constraint(model_start, pltpu.HBM),
        pltpu.with_memory_space_constraint(reg_weight, pltpu.HBM),
        pltpu.with_memory_space_constraint(named, pltpu.HBM),
        scratch=[
            pltpu.VMEM((blocks, width), F32),
            pltpu.VMEM((blocks, width), F32),
            pltpu.VMEM((slots, count), jnp.int32),
            pltpu.SemaphoreType.DMA((3,)),
        ],
        cost=pl.CostEstimate(
            flops=2**14 * width * codes.size, transcendentals=codes.size, bytes_accessed=2**14 * codes.size
        ),
    )
    begin = across([opening] * count)
    turned, rows_pick, rows_pair, scale = call(
        turning_kernel,
        [
            (codes.shape, BF16),
            ((tiles, data_rows), BF16),
            ((data_rows, 2 * tiles), BF16),
            ((tiles, width), F32),
        ],
        codes,
        opening,
        pltpu.with_memory_space_constraint(tile_scale.reshape(1, -1), pltpu.HBM),
        pltpu.with_memory_space_constraint(tile_row.reshape(1, -1), pltpu.HBM),
        scratch=[
            pltpu.VMEM((1, tiles), F32),
            pltpu.VMEM((1, tiles), jnp.int32),
            pltpu.SemaphoreType.DMA((2,)),
        ],
    )
    part, source_pick, source_pair, start, weight = call(
        functools.partial(first_kernel, blocks, slots, count),
        [
            ((data_rows, width), F32),
            ((tiles, cells), BF16),
            ((cells, 2 * tiles), BF16),
            ((cells, width), F32),
            ((cells, width), F32),
        ],
        turned,
        scale,
        rows_pair,
        tile_column.reshape(1, -1),
        place,
        *begin,
    )
    (part,) = call(
        functools.partial(start_data_kernel, sharing),
        [((cells, width), F32)],
        codes,
        rows_pick,
        source_pair,
        scale,
        observed,
        data_weight,
        *within(part),
    )
    part, first = call(
        functools.partial(start_residual_kernel, blocks, count),
        [((data_rows + EXTRA, width), F32), ((cells, width), F32)],
        turned,
        source_pick,
        rows_pair,
        scale,
        start,
        weight,
        *across([part] * count),
    )
    part, predicted, sums = call(
        functools.partial(image_data_kernel, sharing),
        [((cells + EXTRA, width), F32), ((data_rows, width), F32), ((EXTRA, width), F32)],
        codes,
        rows_pick,
        source_pair,
        scale,
        data_weight,
        *within(part),
    )
    part, second, step = call(
        functools.partial(residual_kernel, blocks, count),
        [((data_rows + EXTRA, width), F32), ((cells, width), F32), ((8, 128), F32)],
        turned,
        source_pick,
        rows_pair,
        scale,
        weight,
        first,
        sums,
        *across([part] * count),
    )
    *part, scalars = call(
        functools.partial(second_data_kernel, blocks, sharing),
        [((blocks + 4, width), F32)] * count + [((EXTRA, width), F32)],
        codes,
        rows_pick,
        source_pair,
        scale,
        data_weight,
        predicted,
        sums,
        *within(part),
    )
    model, residual = call(
        functools.partial(last_kernel, blocks, count),
        [((blocks, width), F32), ((blocks, width), F32)],
        weight,
        start,
        first,
        second,
        step,
        scalars,
        *across(part),
    )
    return (model, residual)


def solution(mesh):
    both = P(("groups", "tiles", "split", "depth"))
    owned = P(("groups", "tiles", "split", "depth"), None)
    wide = P(("groups", "tiles", "split", "depth"), None, None)
    data = P(("groups", "tiles"), None)
    in_specs = (wide, both, both, both, wide, owned, owned, data, data)
    return jax.shard_map(
        shards, mesh=mesh, in_specs=in_specs, out_specs=(owned, owned), check_vma=False
    )
```

```python
import functools

import jax
import jax.numpy as jnp
from jax import lax
from jax.experimental import pallas as pl
from jax.experimental.pallas import tpu as pltpu
from jax.sharding import PartitionSpec as P

HIGH = lax.Precision.HIGHEST
EXTRA = 8
LIMIT = 16 * 1024 * 1024
GROUP = 16
CHUNK = 4
F32 = jnp.float32
BF16 = jnp.bfloat16


def exchange(values, axes, size):
    parts = [values[0]] + [None] * (size - 1)
    for shift in range(size - 1, 0, -1):
        perm = [(i, i ^ shift) for i in range(size)]
        parts[shift] = lax.ppermute(values[shift], axes, perm)
    return parts


def total_rows(parts):
    total = parts[0][...]
    for part in parts[1:]:
        total = total + part[...]
    return total


def total_blocks(parts, blocks):
    count = len(parts)
    groups = []
    for group in range(count):
        total = None
        for shift in range(count):
            start = (group ^ shift) * blocks
            piece = parts[shift][start : start + blocks, :]
            total = piece if total is None else total + piece
        groups.append(total)
    return jnp.concatenate(groups, axis=0)


def extra_rows(parts, start):
    total = parts[0][start : start + EXTRA, :]
    for part in parts[1:]:
        total = total + part[start : start + EXTRA, :]
    return total


def whole(value):
    return jnp.sum(value, axis=(0, 1), keepdims=True)


def columns(value):
    return jnp.sum(value, axis=0, keepdims=True)


def pack_rows(rows, width):
    filled = list(rows)
    while len(filled) < EXTRA:
        filled.append(jnp.zeros((1, width), F32))
    return jnp.concatenate(filled, axis=0)


def products(codes, picked):
    tiles, width = picked.shape
    index = lax.broadcasted_iota(jnp.int32, (GROUP, width), 0)
    pieces = []
    for first in range(0, tiles, GROUP):
        rows = picked[first : first + GROUP, :]
        total = None
        for i in range(GROUP):
            value = jnp.dot(rows, codes[first + i], preferred_element_type=F32)
            total = value if total is None else jnp.where(index == i, value, total)
        pieces.append(total)
    return jnp.concatenate(pieces, axis=0)


def pick(table, values):
    return jnp.dot(table, values, preferred_element_type=F32).astype(BF16)


def gather(table, scale, terms):
    scaled = scale * terms
    upper = scaled.astype(BF16)
    lower = (scaled - upper.astype(F32)).astype(BF16)
    both = jnp.concatenate([upper, lower], axis=0)
    return jnp.dot(table, both, preferred_element_type=F32)


def tables(index, values, picks, pairs):
    tiles = index.shape[1]
    hits = lax.broadcasted_iota(jnp.int32, (values, tiles), 0) == index
    ones = jnp.where(hits, 1.0, 0.0)
    picks[...] = ones.T.astype(BF16)
    pairs[...] = jnp.concatenate([ones, ones], axis=1).astype(BF16)


def loading_kernel(far_codes, opening, far_scale, far_row, *refs):
    codes, turned, rows_pick, rows_pair, wide_scale, scale, row, done, small = refs
    near = [
        pltpu.make_async_copy(far_scale, scale, small.at[0]),
        pltpu.make_async_copy(far_row, row, small.at[1]),
    ]
    for copy in near:
        copy.start()
    tiles, width = wide_scale.shape
    copies = []
    for chunk in range(tiles // CHUNK):
        span = pl.ds(chunk * CHUNK, CHUNK)
        copies.append(pltpu.make_async_copy(far_codes.at[span], codes.at[span], done.at[chunk]))
        copies[-1].start()
    for copy in near:
        copy.wait()
    tables(row[...], rows_pick.shape[1], rows_pick, rows_pair)
    square = (tiles, tiles)
    same = lax.broadcasted_iota(jnp.int32, square, 0) == lax.broadcasted_iota(jnp.int32, square, 1)
    wide_scale[...] = jnp.dot(
        jnp.where(same, scale[...], 0.0),
        jnp.ones((tiles, width), F32),
        precision=HIGH,
        preferred_element_type=F32,
    )
    for chunk, copy in enumerate(copies):
        copy.wait()
        for k in range(chunk * CHUNK, (chunk + 1) * CHUNK):
            turned[k] = codes[k].T


def opening_kernel(start, weight, named, out, sources, weights, names, done):
    copies = [
        pltpu.make_async_copy(start, sources, done.at[0]),
        pltpu.make_async_copy(weight, weights, done.at[1]),
        pltpu.make_async_copy(named, names, done.at[2]),
    ]
    for copy in copies:
        copy.start()
    blocks, width = sources.shape
    slots, count = names.shape
    rest = out.shape[0] - 2 * blocks
    out[2 * blocks :, :] = jnp.zeros((rest, width), F32)
    for copy in copies:
        copy.wait()
    out[:blocks, :] = sources[...]
    out[blocks : 2 * blocks, :] = weights[...]
    out[2 * blocks : 2 * blocks + slots, :count] = names[...].astype(F32)


def first_kernel(blocks, slots, order, *refs):
    turned, scale, rows_pair, column, place = refs[:5]
    count = len(order)
    parts = [ref for _, ref in sorted(zip(order, refs[5 : 5 + count]), key=lambda pair: pair[0])]
    out, source_pick, source_pair, start, weight = refs[5 + count :]
    width = out.shape[1]
    here = place[0]
    columns_of = column[...]
    source = jnp.where(columns_of < blocks, columns_of, 0)
    lane = lax.broadcasted_iota(jnp.int32, (1, width), 1)
    for shift in range(count):
        other = jnp.bitwise_xor(here, shift)
        for slot in range(slots):
            named = parts[shift][2 * blocks + slot : 2 * blocks + slot + 1, :]
            mine = jnp.where(lane == here, named, 0.0)
            block = jnp.sum(mine, axis=1, keepdims=True).astype(jnp.int32) + shift * blocks
            source = jnp.where(columns_of == blocks + other * slots + slot, block, source)
    tables(source, count * blocks, source_pick, source_pair)
    field = jnp.concatenate([part[:blocks, :] for part in parts], axis=0)
    start[...] = field
    weight[...] = jnp.concatenate([part[blocks : 2 * blocks, :] for part in parts], axis=0)

    terms = products(turned, pick(source_pick[...], field.astype(BF16)))
    out[...] = gather(rows_pair[...], scale[...], terms)


def start_data_kernel(count, *refs):
    codes, rows_pick, source_pair, scale, observed, data_weight = refs[:6]
    parts = refs[6 : 6 + count]
    out = refs[6 + count]
    total = total_rows(parts)
    data = (data_weight[...] * (observed[...] - total)).astype(BF16)
    terms = products(codes, pick(rows_pick[...], data))
    out[...] = gather(source_pair[...], scale[...], terms)


def start_residual_kernel(blocks, count, *refs):
    codes, source_pick, rows_pair, scale, start, weight = refs[:6]
    parts = refs[6 : 6 + count]
    out, residual = refs[6 + count :]
    weights = weight[...]
    value = total_blocks(parts, blocks) - weights * start[...]
    residual[...] = value
    terms = products(codes, pick(source_pick[...], value.astype(BF16)))
    data_rows = rows_pair.shape[0]
    out[:data_rows, :] = gather(rows_pair[...], scale[...], terms)
    out[data_rows:, :] = pack_rows(
        [columns(value * value), columns(value * weights * value)], value.shape[1]
    )


def image_data_kernel(count, *refs):
    codes, rows_pick, source_pair, scale, data_weight = refs[:5]
    parts = refs[5 : 5 + count]
    out, predicted, sums = refs[5 + count :]
    data_rows = data_weight.shape[0]
    whole_part = total_rows(parts)
    total = whole_part[:data_rows, :]
    predicted[...] = total
    sums[...] = whole_part[data_rows:, :]
    data = (data_weight[...] * (0.0 - total)).astype(BF16)
    terms = products(codes, pick(rows_pick[...], data))
    cells = source_pair.shape[0]
    out[:cells, :] = gather(source_pair[...], scale[...], terms)
    out[cells:, :] = pack_rows([columns(total * data.astype(F32))], total.shape[1])


def residual_kernel(blocks, count, *refs):
    codes, source_pick, rows_pair, scale, weight, direction, sums = refs[:7]
    parts = refs[7 : 7 + count]
    out, residual, step = refs[7 + count :]
    cells = source_pick.shape[1]
    weights = weight[...]
    along = direction[...]
    image = weights * along - total_blocks(parts, blocks)
    curve = whole(sums[1:2, :]) - whole(extra_rows(parts, cells)[0:1, :])
    alpha = whole(sums[0:1, :]) / curve
    step[...] = jnp.broadcast_to(alpha, step.shape)
    value = residual_of(along, alpha, image)
    residual[...] = value
    terms = products(codes, pick(source_pick[...], value.astype(BF16)))
    data_rows = rows_pair.shape[0]
    out[:data_rows, :] = gather(rows_pair[...], scale[...], terms)
    weighted = value * weights
    out[data_rows:, :] = pack_rows(
        [columns(value * value), columns(weighted * value), columns(weighted * along)],
        value.shape[1],
    )


def residual_of(residual, alpha, image):
    return residual - alpha * image


def second_data_kernel(blocks, count, *refs):
    codes, rows_pick, source_pair, scale, data_weight, predicted, sums = refs[:7]
    parts = refs[7 : 7 + count]
    outs, scalars = refs[7 + count : -1], refs[-1]
    data_rows = data_weight.shape[0]
    whole_part = total_rows(parts)
    norm = whole(whole_part[data_rows : data_rows + 1, :])
    beta = norm / whole(sums[0:1, :])
    curve = whole(
        whole_part[data_rows + 1 : data_rows + 2, :]
        + 2.0 * beta * whole_part[data_rows + 2 : data_rows + 3, :]
        + beta * beta * sums[1:2, :]
    )
    total = whole_part[:data_rows, :] + beta * predicted[...]
    data = (data_weight[...] * (0.0 - total)).astype(BF16)
    terms = products(codes, pick(rows_pick[...], data))
    cells = gather(source_pair[...], scale[...], terms)
    curved = columns(total * data.astype(F32))
    for group, out in enumerate(outs):
        out[:blocks, :] = cells[group * blocks : (group + 1) * blocks, :]
        out[blocks:, :] = jnp.broadcast_to(curved, (out.shape[0] - blocks, total.shape[1]))
    wide = (1, scalars.shape[1])
    scalars[...] = pack_rows(
        [jnp.broadcast_to(value, wide) for value in (norm, beta, curve)], scalars.shape[1]
    )


def last_kernel(blocks, count, *refs):
    weight, start, first, second, step, scalars = refs[:6]
    parts = refs[6 : 6 + count]
    model, residual = refs[6 + count :]
    norm = scalars[0:1, 0:1]
    beta = scalars[1:2, 0:1]
    curve = scalars[2:3, 0:1]
    along = first[:blocks, :]
    left = second[:blocks, :]
    direction = left + beta * along
    whole_part = total_rows(parts)
    image = weight[:blocks, :] * direction - whole_part[:blocks, :]
    alpha = norm / (curve - whole(whole_part[blocks : blocks + 1, :]))
    model[...] = start[:blocks, :] + step[0:1, 0:1] * along + alpha * direction
    residual[...] = left - alpha * image


def call(body, outs, *args, scratch=()):
    specs = []
    for arg in args:
        far = getattr(jax.typeof(arg), "memory_space", None) == pltpu.HBM
        space = pl.ANY if far else pltpu.SMEM if arg.ndim == 1 else pltpu.VMEM
        specs.append(pl.BlockSpec(memory_space=space))
    return pl.pallas_call(
        body,
        out_shape=[jax.ShapeDtypeStruct(shape, dtype) for shape, dtype in outs],
        in_specs=specs,
        out_specs=[pl.BlockSpec(memory_space=pltpu.VMEM)] * len(outs),
        scratch_shapes=list(scratch),
        compiler_params=pltpu.CompilerParams(vmem_limit_bytes=LIMIT),
    )(*args)


def shards(
    tile_codes,
    tile_scale,
    tile_row,
    tile_column,
    send_index,
    model_start,
    reg_weight,
    observed,
    data_weight,
):
    blocks, width = model_start.shape
    slots = send_index.shape[2]
    data_rows = observed.shape[0]
    tiles = tile_codes.shape[0]
    count = lax.axis_size("tiles")
    sharing = lax.axis_size(("split", "depth"))
    cells = count * blocks
    place = lax.axis_index("tiles").astype(jnp.int32).reshape(1)

    def across(values):
        return exchange(values, "tiles", count)

    def within(value):
        return exchange([value] * sharing, ("split", "depth"), sharing)

    named = jnp.transpose(send_index, (0, 2, 1)).reshape(slots, count)
    (opening,) = call(
        opening_kernel,
        [((2 * blocks + EXTRA, width), F32)],
        pltpu.with_memory_space_constraint(model_start, pltpu.HBM),
        pltpu.with_memory_space_constraint(reg_weight, pltpu.HBM),
        pltpu.with_memory_space_constraint(named, pltpu.HBM),
        scratch=[
            pltpu.VMEM((blocks, width), F32),
            pltpu.VMEM((blocks, width), F32),
            pltpu.VMEM((slots, count), jnp.int32),
            pltpu.SemaphoreType.DMA((3,)),
        ],
    )
    begin = across([opening] * count)
    order = [0] + sorted(range(1, count), key=lambda shift: (shift != 1, -abs(2 * shift - count)))
    codes, turned, rows_pick, rows_pair, scale = call(
        loading_kernel,
        [
            (tile_codes.shape, BF16),
            (tile_codes.shape, BF16),
            ((tiles, data_rows), BF16),
            ((data_rows, 2 * tiles), BF16),
            ((tiles, width), F32),
        ],
        pltpu.with_memory_space_constraint(tile_codes, pltpu.HBM),
        opening,
        pltpu.with_memory_space_constraint(tile_scale.reshape(1, -1), pltpu.HBM),
        pltpu.with_memory_space_constraint(tile_row.reshape(1, -1), pltpu.HBM),
        scratch=[
            pltpu.VMEM((1, tiles), F32),
            pltpu.VMEM((1, tiles), jnp.int32),
            pltpu.SemaphoreType.DMA((tiles // CHUNK,)),
            pltpu.SemaphoreType.DMA((2,)),
        ],
    )
    part, source_pick, source_pair, start, weight = call(
        functools.partial(first_kernel, blocks, slots, order),
        [
            ((data_rows, width), F32),
            ((tiles, cells), BF16),
            ((cells, 2 * tiles), BF16),
            ((cells, width), F32),
            ((cells, width), F32),
        ],
        turned,
        scale,
        rows_pair,
        tile_column.reshape(1, -1),
        place,
        *[begin[shift] for shift in order],
    )
    (part,) = call(
        functools.partial(start_data_kernel, sharing),
        [((cells, width), F32)],
        codes,
        rows_pick,
        source_pair,
        scale,
        observed,
        data_weight,
        *within(part),
    )
    part, first = call(
        functools.partial(start_residual_kernel, blocks, count),
        [((data_rows + EXTRA, width), F32), ((cells, width), F32)],
        turned,
        source_pick,
        rows_pair,
        scale,
        start,
        weight,
        *across([part] * count),
    )
    part, predicted, sums = call(
        functools.partial(image_data_kernel, sharing),
        [((cells + EXTRA, width), F32), ((data_rows, width), F32), ((EXTRA, width), F32)],
        codes,
        rows_pick,
        source_pair,
        scale,
        data_weight,
        *within(part),
    )
    part, second, step = call(
        functools.partial(residual_kernel, blocks, count),
        [((data_rows + EXTRA, width), F32), ((cells, width), F32), ((8, 128), F32)],
        turned,
        source_pick,
        rows_pair,
        scale,
        weight,
        first,
        sums,
        *across([part] * count),
    )
    *part, scalars = call(
        functools.partial(second_data_kernel, blocks, sharing),
        [((blocks + 4, width), F32)] * count + [((EXTRA, width), F32)],
        codes,
        rows_pick,
        source_pair,
        scale,
        data_weight,
        predicted,
        sums,
        *within(part),
    )
    model, residual = call(
        functools.partial(last_kernel, blocks, count),
        [((blocks, width), F32), ((blocks, width), F32)],
        weight,
        start,
        first,
        second,
        step,
        scalars,
        *across(part),
    )
    return (model, residual)


def solution(mesh):
    both = P(("groups", "tiles", "split", "depth"))
    owned = P(("groups", "tiles", "split", "depth"), None)
    wide = P(("groups", "tiles", "split", "depth"), None, None)
    data = P(("groups", "tiles"), None)
    in_specs = (wide, both, both, both, wide, owned, owned, data, data)
    return jax.shard_map(
        shards, mesh=mesh, in_specs=in_specs, out_specs=(owned, owned), check_vma=False
    )
```

```python
import functools

import jax
import jax.numpy as jnp
from jax import lax
from jax.experimental import pallas as pl
from jax.experimental.pallas import tpu as pltpu
from jax.sharding import PartitionSpec as P

HIGH = lax.Precision.HIGHEST
EXTRA = 8
LIMIT = 16 * 1024 * 1024
GROUP = 16
CHUNK = 16
FLIGHT = 2
F32 = jnp.float32
BF16 = jnp.bfloat16


def exchange(values, axes, size):
    parts = [values[0]] + [None] * (size - 1)
    for shift in range(size - 1, 0, -1):
        perm = [(i, i ^ shift) for i in range(size)]
        parts[shift] = lax.ppermute(values[shift], axes, perm)
    return parts


def total_rows(parts):
    total = parts[0][...]
    for part in parts[1:]:
        total = total + part[...]
    return total


def total_blocks(parts, blocks):
    count = len(parts)
    groups = []
    for group in range(count):
        total = None
        for shift in range(count):
            start = (group ^ shift) * blocks
            piece = parts[shift][start : start + blocks, :]
            total = piece if total is None else total + piece
        groups.append(total)
    return jnp.concatenate(groups, axis=0)


def extra_rows(parts, start):
    total = parts[0][start : start + EXTRA, :]
    for part in parts[1:]:
        total = total + part[start : start + EXTRA, :]
    return total


def whole(value):
    return jnp.sum(value, axis=(0, 1), keepdims=True)


def columns(value):
    return jnp.sum(value, axis=0, keepdims=True)


def pack_rows(rows, width):
    filled = list(rows)
    while len(filled) < EXTRA:
        filled.append(jnp.zeros((1, width), F32))
    return jnp.concatenate(filled, axis=0)


def products(tile_of, picked):
    tiles, width = picked.shape
    index = lax.broadcasted_iota(jnp.int32, (GROUP, width), 0)
    pieces = []
    for first in range(0, tiles, GROUP):
        rows = picked[first : first + GROUP, :]
        total = None
        for i in range(GROUP):
            tile, turn = tile_of(first + i)
            dims = (((1,), (1 if turn else 0,)), ((), ()))
            value = lax.dot_general(rows, tile, dims, preferred_element_type=F32)
            total = value if total is None else jnp.where(index == i, value, total)
        pieces.append(total)
    return jnp.concatenate(pieces, axis=0)


def kept_tiles(codes):
    return lambda k: (codes[k], False)


def turned_tiles(early, late, turn=False):
    count = early.shape[0]
    shift = 0 if turn else count
    return lambda k: (early[k], False) if k < count else (late[k - shift], turn)


def pick(table, values):
    return jnp.dot(table, values, preferred_element_type=F32).astype(BF16)


def gather(table, scale, terms):
    scaled = scale * terms
    upper = scaled.astype(BF16)
    lower = (scaled - upper.astype(F32)).astype(BF16)
    both = jnp.concatenate([upper, lower], axis=0)
    return jnp.dot(table, both, preferred_element_type=F32)


def tables(index, values, picks, pairs):
    tiles = index.shape[1]
    hits = lax.broadcasted_iota(jnp.int32, (values, tiles), 0) == index
    ones = jnp.where(hits, 1.0, 0.0)
    picks[...] = ones.T.astype(BF16)
    pairs[...] = jnp.concatenate([ones, ones], axis=1).astype(BF16)


def loading_kernel(far_codes, opening, far_scale, far_row, *refs):
    codes, early, rows_pick, rows_pair, wide_scale, scale, row, done, small = refs
    near = [
        pltpu.make_async_copy(far_scale, scale, small.at[0]),
        pltpu.make_async_copy(far_row, row, small.at[1]),
    ]
    for copy in near:
        copy.start()
    tiles, width = wide_scale.shape
    copies = []
    for chunk in range(tiles // CHUNK):
        span = pl.ds(chunk * CHUNK, CHUNK)
        copies.append(pltpu.make_async_copy(far_codes.at[span], codes.at[span], done.at[chunk]))
    for copy in copies[:FLIGHT]:
        copy.start()
    for copy in near:
        copy.wait()
    tables(row[...], rows_pick.shape[1], rows_pick, rows_pair)
    square = (tiles, tiles)
    same = lax.broadcasted_iota(jnp.int32, square, 0) == lax.broadcasted_iota(jnp.int32, square, 1)
    wide_scale[...] = jnp.dot(
        jnp.where(same, scale[...], 0.0),
        jnp.ones((tiles, width), F32),
        precision=HIGH,
        preferred_element_type=F32,
    )
    for chunk, copy in enumerate(copies):
        copy.wait()
        if chunk + FLIGHT < len(copies):
            copies[chunk + FLIGHT].start()
        for k in range(chunk * CHUNK, min((chunk + 1) * CHUNK, early.shape[0])):
            early[k] = codes[k].T


def turning_kernel(codes, part, late):
    first = codes.shape[0] - late.shape[0]
    for k in range(late.shape[0]):
        late[k] = codes[first + k].T


def opening_kernel(start, weight, named, out, sources, weights, names, done):
    copies = [
        pltpu.make_async_copy(start, sources, done.at[0]),
        pltpu.make_async_copy(weight, weights, done.at[1]),
        pltpu.make_async_copy(named, names, done.at[2]),
    ]
    for copy in copies:
        copy.start()
    blocks, width = sources.shape
    slots, count = names.shape
    rest = out.shape[0] - 2 * blocks
    out[2 * blocks :, :] = jnp.zeros((rest, width), F32)
    for copy in copies:
        copy.wait()
    out[:blocks, :] = sources[...]
    out[blocks : 2 * blocks, :] = weights[...]
    out[2 * blocks : 2 * blocks + slots, :count] = names[...].astype(F32)


def first_kernel(blocks, slots, order, *refs):
    codes, early, scale, rows_pair, column, place = refs[:6]
    count = len(order)
    parts = [ref for _, ref in sorted(zip(order, refs[6 : 6 + count]), key=lambda pair: pair[0])]
    out, source_pick, source_pair, start, weight = refs[6 + count :]
    width = out.shape[1]
    here = place[0]
    columns_of = column[...]
    source = jnp.where(columns_of < blocks, columns_of, 0)
    lane = lax.broadcasted_iota(jnp.int32, (1, width), 1)
    for shift in range(count):
        other = jnp.bitwise_xor(here, shift)
        for slot in range(slots):
            named = parts[shift][2 * blocks + slot : 2 * blocks + slot + 1, :]
            mine = jnp.where(lane == here, named, 0.0)
            block = jnp.sum(mine, axis=1, keepdims=True).astype(jnp.int32) + shift * blocks
            source = jnp.where(columns_of == blocks + other * slots + slot, block, source)
    tables(source, count * blocks, source_pick, source_pair)
    field = jnp.concatenate([part[:blocks, :] for part in parts], axis=0)
    start[...] = field
    weight[...] = jnp.concatenate([part[blocks : 2 * blocks, :] for part in parts], axis=0)

    terms = products(turned_tiles(early, codes, True), pick(source_pick[...], field.astype(BF16)))
    out[...] = gather(rows_pair[...], scale[...], terms)


def start_data_kernel(count, *refs):
    codes, rows_pick, source_pair, scale, observed, data_weight, late = refs[:7]
    parts = refs[7 : 7 + count]
    out = refs[7 + count]
    total = total_rows(parts)
    data = (data_weight[...] * (observed[...] - total)).astype(BF16)
    terms = products(kept_tiles(codes), pick(rows_pick[...], data))
    out[...] = gather(source_pair[...], scale[...], terms)


def start_residual_kernel(blocks, count, *refs):
    early, late, source_pick, rows_pair, scale, start, weight = refs[:7]
    parts = refs[7 : 7 + count]
    out, residual = refs[7 + count :]
    weights = weight[...]
    value = total_blocks(parts, blocks) - weights * start[...]
    residual[...] = value
    terms = products(turned_tiles(early, late), pick(source_pick[...], value.astype(BF16)))
    data_rows = rows_pair.shape[0]
    out[:data_rows, :] = gather(rows_pair[...], scale[...], terms)
    out[data_rows:, :] = pack_rows(
        [columns(value * value), columns(value * weights * value)], value.shape[1]
    )


def image_data_kernel(count, *refs):
    codes, rows_pick, source_pair, scale, data_weight = refs[:5]
    parts = refs[5 : 5 + count]
    out, predicted, sums = refs[5 + count :]
    data_rows = data_weight.shape[0]
    whole_part = total_rows(parts)
    total = whole_part[:data_rows, :]
    predicted[...] = total
    sums[...] = whole_part[data_rows:, :]
    data = (data_weight[...] * (0.0 - total)).astype(BF16)
    terms = products(kept_tiles(codes), pick(rows_pick[...], data))
    cells = source_pair.shape[0]
    out[:cells, :] = gather(source_pair[...], scale[...], terms)
    out[cells:, :] = pack_rows([columns(total * data.astype(F32))], total.shape[1])


def residual_kernel(blocks, count, *refs):
    early, late, source_pick, rows_pair, scale, weight, direction, sums = refs[:8]
    parts = refs[8 : 8 + count]
    out, residual, step = refs[8 + count :]
    cells = source_pick.shape[1]
    weights = weight[...]
    along = direction[...]
    image = weights * along - total_blocks(parts, blocks)
    curve = whole(sums[1:2, :]) - whole(extra_rows(parts, cells)[0:1, :])
    alpha = whole(sums[0:1, :]) / curve
    step[...] = jnp.broadcast_to(alpha, step.shape)
    value = residual_of(along, alpha, image)
    residual[...] = value
    terms = products(turned_tiles(early, late), pick(source_pick[...], value.astype(BF16)))
    data_rows = rows_pair.shape[0]
    out[:data_rows, :] = gather(rows_pair[...], scale[...], terms)
    weighted = value * weights
    out[data_rows:, :] = pack_rows(
        [columns(value * value), columns(weighted * value), columns(weighted * along)],
        value.shape[1],
    )


def residual_of(residual, alpha, image):
    return residual - alpha * image


def second_data_kernel(blocks, count, *refs):
    codes, rows_pick, source_pair, scale, data_weight, predicted, sums = refs[:7]
    parts = refs[7 : 7 + count]
    outs, scalars = refs[7 + count : -1], refs[-1]
    data_rows = data_weight.shape[0]
    whole_part = total_rows(parts)
    norm = whole(whole_part[data_rows : data_rows + 1, :])
    beta = norm / whole(sums[0:1, :])
    curve = whole(
        whole_part[data_rows + 1 : data_rows + 2, :]
        + 2.0 * beta * whole_part[data_rows + 2 : data_rows + 3, :]
        + beta * beta * sums[1:2, :]
    )
    total = whole_part[:data_rows, :] + beta * predicted[...]
    data = (data_weight[...] * (0.0 - total)).astype(BF16)
    terms = products(kept_tiles(codes), pick(rows_pick[...], data))
    cells = gather(source_pair[...], scale[...], terms)
    curved = columns(total * data.astype(F32))
    for group, out in enumerate(outs):
        out[:blocks, :] = cells[group * blocks : (group + 1) * blocks, :]
        out[blocks:, :] = jnp.broadcast_to(curved, (out.shape[0] - blocks, total.shape[1]))
    wide = (1, scalars.shape[1])
    scalars[...] = pack_rows(
        [jnp.broadcast_to(value, wide) for value in (norm, beta, curve)], scalars.shape[1]
    )


def last_kernel(blocks, count, *refs):
    weight, start, first, second, step, scalars = refs[:6]
    parts = refs[6 : 6 + count]
    model, residual = refs[6 + count :]
    norm = scalars[0:1, 0:1]
    beta = scalars[1:2, 0:1]
    curve = scalars[2:3, 0:1]
    along = first[:blocks, :]
    left = second[:blocks, :]
    direction = left + beta * along
    whole_part = total_rows(parts)
    image = weight[:blocks, :] * direction - whole_part[:blocks, :]
    alpha = norm / (curve - whole(whole_part[blocks : blocks + 1, :]))
    model[...] = start[:blocks, :] + step[0:1, 0:1] * along + alpha * direction
    residual[...] = left - alpha * image


def call(body, outs, *args, scratch=()):
    specs = []
    for arg in args:
        far = getattr(jax.typeof(arg), "memory_space", None) == pltpu.HBM
        space = pl.ANY if far else pltpu.SMEM if arg.ndim == 1 else pltpu.VMEM
        specs.append(pl.BlockSpec(memory_space=space))
    return pl.pallas_call(
        body,
        out_shape=[jax.ShapeDtypeStruct(shape, dtype) for shape, dtype in outs],
        in_specs=specs,
        out_specs=[pl.BlockSpec(memory_space=pltpu.VMEM)] * len(outs),
        scratch_shapes=list(scratch),
        compiler_params=pltpu.CompilerParams(vmem_limit_bytes=LIMIT),
    )(*args)


def shards(
    tile_codes,
    tile_scale,
    tile_row,
    tile_column,
    send_index,
    model_start,
    reg_weight,
    observed,
    data_weight,
):
    blocks, width = model_start.shape
    slots = send_index.shape[2]
    data_rows = observed.shape[0]
    tiles = tile_codes.shape[0]
    count = lax.axis_size("tiles")
    sharing = lax.axis_size(("split", "depth"))
    cells = count * blocks
    place = lax.axis_index("tiles").astype(jnp.int32).reshape(1)

    def across(values):
        return exchange(values, "tiles", count)

    def within(value):
        return exchange([value] * sharing, ("split", "depth"), sharing)

    named = jnp.transpose(send_index, (0, 2, 1)).reshape(slots, count)
    (opening,) = call(
        opening_kernel,
        [((2 * blocks + EXTRA, width), F32)],
        pltpu.with_memory_space_constraint(model_start, pltpu.HBM),
        pltpu.with_memory_space_constraint(reg_weight, pltpu.HBM),
        pltpu.with_memory_space_constraint(named, pltpu.HBM),
        scratch=[
            pltpu.VMEM((blocks, width), F32),
            pltpu.VMEM((blocks, width), F32),
            pltpu.VMEM((slots, count), jnp.int32),
            pltpu.SemaphoreType.DMA((3,)),
        ],
    )
    begin = across([opening] * count)
    order = [0] + sorted(range(1, count), key=lambda shift: (shift != 1, -abs(2 * shift - count)))
    codes, early, rows_pick, rows_pair, scale = call(
        loading_kernel,
        [
            (tile_codes.shape, BF16),
            ((tiles - CHUNK, width, width), BF16),
            ((tiles, data_rows), BF16),
            ((data_rows, 2 * tiles), BF16),
            ((tiles, width), F32),
        ],
        pltpu.with_memory_space_constraint(tile_codes, pltpu.HBM),
        opening,
        pltpu.with_memory_space_constraint(tile_scale.reshape(1, -1), pltpu.HBM),
        pltpu.with_memory_space_constraint(tile_row.reshape(1, -1), pltpu.HBM),
        scratch=[
            pltpu.VMEM((1, tiles), F32),
            pltpu.VMEM((1, tiles), jnp.int32),
            pltpu.SemaphoreType.DMA((tiles // CHUNK,)),
            pltpu.SemaphoreType.DMA((2,)),
        ],
    )
    part, source_pick, source_pair, start, weight = call(
        functools.partial(first_kernel, blocks, slots, order),
        [
            ((data_rows, width), F32),
            ((tiles, cells), BF16),
            ((cells, 2 * tiles), BF16),
            ((cells, width), F32),
            ((cells, width), F32),
        ],
        codes,
        early,
        scale,
        rows_pair,
        tile_column.reshape(1, -1),
        place,
        *[begin[shift] for shift in order],
    )
    parts = within(part)
    (late,) = call(turning_kernel, [((CHUNK, width, width), BF16)], codes, part)
    (part,) = call(
        functools.partial(start_data_kernel, sharing),
        [((cells, width), F32)],
        codes,
        rows_pick,
        source_pair,
        scale,
        observed,
        data_weight,
        late,
        *parts,
    )
    part, first = call(
        functools.partial(start_residual_kernel, blocks, count),
        [((data_rows + EXTRA, width), F32), ((cells, width), F32)],
        early,
        late,
        source_pick,
        rows_pair,
        scale,
        start,
        weight,
        *across([part] * count),
    )
    part, predicted, sums = call(
        functools.partial(image_data_kernel, sharing),
        [((cells + EXTRA, width), F32), ((data_rows, width), F32), ((EXTRA, width), F32)],
        codes,
        rows_pick,
        source_pair,
        scale,
        data_weight,
        *within(part),
    )
    part, second, step = call(
        functools.partial(residual_kernel, blocks, count),
        [((data_rows + EXTRA, width), F32), ((cells, width), F32), ((8, 128), F32)],
        early,
        late,
        source_pick,
        rows_pair,
        scale,
        weight,
        first,
        sums,
        *across([part] * count),
    )
    *part, scalars = call(
        functools.partial(second_data_kernel, blocks, sharing),
        [((blocks + 4, width), F32)] * count + [((EXTRA, width), F32)],
        codes,
        rows_pick,
        source_pair,
        scale,
        data_weight,
        predicted,
        sums,
        *within(part),
    )
    model, residual = call(
        functools.partial(last_kernel, blocks, count),
        [((blocks, width), F32), ((blocks, width), F32)],
        weight,
        start,
        first,
        second,
        step,
        scalars,
        *across(part),
    )
    return (model, residual)


def solution(mesh):
    both = P(("groups", "tiles", "split", "depth"))
    owned = P(("groups", "tiles", "split", "depth"), None)
    wide = P(("groups", "tiles", "split", "depth"), None, None)
    data = P(("groups", "tiles"), None)
    in_specs = (wide, both, both, both, wide, owned, owned, data, data)
    return jax.shard_map(
        shards, mesh=mesh, in_specs=in_specs, out_specs=(owned, owned), check_vma=False
    )
```

```python
import functools

import jax
import jax.numpy as jnp
from jax import lax
from jax.experimental import pallas as pl
from jax.experimental.pallas import tpu as pltpu
from jax.sharding import PartitionSpec as P

HIGH = lax.Precision.HIGHEST
EXTRA = 8
LIMIT = 16 * 1024 * 1024
GROUP = 16
CHUNK = 16
F32 = jnp.float32
BF16 = jnp.bfloat16


def exchange(values, axes, size):
    parts = [values[0]] + [None] * (size - 1)
    for shift in range(size - 1, 0, -1):
        perm = [(i, i ^ shift) for i in range(size)]
        parts[shift] = lax.ppermute(values[shift], axes, perm)
    return parts


def by_shift(order, parts):
    return [part for _, part in sorted(zip(order, parts), key=lambda pair: pair[0])]


def total_rows(parts):
    total = parts[0][...]
    for part in parts[1:]:
        total = total + part[...]
    return total


def total_blocks(parts, blocks):
    count = len(parts)
    groups = []
    for group in range(count):
        total = None
        for shift in range(count):
            start = (group ^ shift) * blocks
            piece = parts[shift][start : start + blocks, :]
            total = piece if total is None else total + piece
        groups.append(total)
    return jnp.concatenate(groups, axis=0)


def extra_rows(parts, start):
    total = parts[0][start : start + EXTRA, :]
    for part in parts[1:]:
        total = total + part[start : start + EXTRA, :]
    return total


def whole(value):
    return jnp.sum(value, axis=(0, 1), keepdims=True)


def columns(value):
    return jnp.sum(value, axis=0, keepdims=True)


def pack_rows(rows, width):
    filled = list(rows)
    while len(filled) < EXTRA:
        filled.append(jnp.zeros((1, width), F32))
    return jnp.concatenate(filled, axis=0)


def products(tile_of, picked):
    tiles, width = picked.shape
    index = lax.broadcasted_iota(jnp.int32, (GROUP, width), 0)
    pieces = []
    for first in range(0, tiles, GROUP):
        rows = picked[first : first + GROUP, :]
        total = None
        for i in range(GROUP):
            tile, turn = tile_of(first + i)
            dims = (((1,), (1 if turn else 0,)), ((), ()))
            value = lax.dot_general(rows, tile, dims, preferred_element_type=F32)
            total = value if total is None else jnp.where(index == i, value, total)
        pieces.append(total)
    return jnp.concatenate(pieces, axis=0)


def kept_tiles(codes):
    return lambda k: (codes[k], False)


def turned_tiles(early, late, turn=False):
    count = early.shape[0]
    shift = 0 if turn else count
    return lambda k: (early[k], False) if k < count else (late[k - shift], turn)


def pick(table, values):
    return jnp.dot(table, values, preferred_element_type=F32).astype(BF16)


def gather(table, scale, terms):
    scaled = scale * terms
    upper = scaled.astype(BF16)
    lower = (scaled - upper.astype(F32)).astype(BF16)
    both = jnp.concatenate([upper, lower], axis=0)
    return jnp.dot(table, both, preferred_element_type=F32)


def tables(index, values, picks, pairs):
    tiles = index.shape[1]
    hits = lax.broadcasted_iota(jnp.int32, (values, tiles), 0) == index
    ones = jnp.where(hits, 1.0, 0.0)
    picks[...] = ones.T.astype(BF16)
    pairs[...] = jnp.concatenate([ones, ones], axis=1).astype(BF16)


def loading_kernel(far_codes, opening, far_scale, far_row, *refs):
    codes, early, rows_pick, rows_pair, wide_scale, scale, row, done, small = refs
    near = [
        pltpu.make_async_copy(far_scale, scale, small.at[0]),
        pltpu.make_async_copy(far_row, row, small.at[1]),
    ]
    for copy in near:
        copy.start()
    tiles, width = wide_scale.shape
    copies = []
    for chunk in range(tiles // CHUNK):
        span = pl.ds(chunk * CHUNK, CHUNK)
        copies.append(pltpu.make_async_copy(far_codes.at[span], codes.at[span], done.at[chunk]))
        copies[-1].start()
    for copy in near:
        copy.wait()
    tables(row[...], rows_pick.shape[1], rows_pick, rows_pair)
    square = (tiles, tiles)
    same = lax.broadcasted_iota(jnp.int32, square, 0) == lax.broadcasted_iota(jnp.int32, square, 1)
    wide_scale[...] = jnp.dot(
        jnp.where(same, scale[...], 0.0),
        jnp.ones((tiles, width), F32),
        precision=HIGH,
        preferred_element_type=F32,
    )
    for chunk, copy in enumerate(copies):
        copy.wait()
        for k in range(chunk * CHUNK, min((chunk + 1) * CHUNK, early.shape[0])):
            early[k] = codes[k].T


def turning_kernel(codes, part, late):
    first = codes.shape[0] - late.shape[0]
    for k in range(late.shape[0]):
        late[k] = codes[first + k].T


def opening_kernel(start, weight, named, out, sources, weights, names, done):
    copies = [
        pltpu.make_async_copy(start, sources, done.at[0]),
        pltpu.make_async_copy(weight, weights, done.at[1]),
        pltpu.make_async_copy(named, names, done.at[2]),
    ]
    for copy in copies:
        copy.start()
    blocks, width = sources.shape
    slots, count = names.shape
    rest = out.shape[0] - 2 * blocks
    out[2 * blocks :, :] = jnp.zeros((rest, width), F32)
    for copy in copies:
        copy.wait()
    out[:blocks, :] = sources[...]
    out[blocks : 2 * blocks, :] = weights[...]
    out[2 * blocks : 2 * blocks + slots, :count] = names[...].astype(F32)


def first_kernel(blocks, slots, order, *refs):
    codes, early, scale, rows_pair, column, place = refs[:6]
    count = len(order)
    parts = by_shift(order, refs[6 : 6 + count])
    out, source_pick, source_pair, start, weight = refs[6 + count :]
    width = out.shape[1]
    here = place[0]
    columns_of = column[...]
    source = jnp.where(columns_of < blocks, columns_of, 0)
    lane = lax.broadcasted_iota(jnp.int32, (1, width), 1)
    for shift in range(count):
        other = jnp.bitwise_xor(here, shift)
        for slot in range(slots):
            named = parts[shift][2 * blocks + slot : 2 * blocks + slot + 1, :]
            mine = jnp.where(lane == here, named, 0.0)
            block = jnp.sum(mine, axis=1, keepdims=True).astype(jnp.int32) + shift * blocks
            source = jnp.where(columns_of == blocks + other * slots + slot, block, source)
    tables(source, count * blocks, source_pick, source_pair)
    field = jnp.concatenate([part[:blocks, :] for part in parts], axis=0)
    start[...] = field
    weight[...] = jnp.concatenate([part[blocks : 2 * blocks, :] for part in parts], axis=0)

    terms = products(turned_tiles(early, codes, True), pick(source_pick[...], field.astype(BF16)))
    out[...] = gather(rows_pair[...], scale[...], terms)


def start_data_kernel(count, *refs):
    codes, rows_pick, source_pair, scale, observed, data_weight, late = refs[:7]
    parts = refs[7 : 7 + count]
    out = refs[7 + count]
    total = total_rows(parts)
    data = (data_weight[...] * (observed[...] - total)).astype(BF16)
    terms = products(kept_tiles(codes), pick(rows_pick[...], data))
    out[...] = gather(source_pair[...], scale[...], terms)


def start_residual_kernel(blocks, order, *refs):
    count = len(order)
    early, late, source_pick, rows_pair, scale, start, weight = refs[:7]
    parts = by_shift(order, refs[7 : 7 + count])
    out, residual = refs[7 + count :]
    weights = weight[...]
    value = total_blocks(parts, blocks) - weights * start[...]
    residual[...] = value
    terms = products(turned_tiles(early, late), pick(source_pick[...], value.astype(BF16)))
    data_rows = rows_pair.shape[0]
    out[:data_rows, :] = gather(rows_pair[...], scale[...], terms)
    out[data_rows:, :] = pack_rows(
        [columns(value * value), columns(value * weights * value)], value.shape[1]
    )


def image_data_kernel(count, *refs):
    codes, rows_pick, source_pair, scale, data_weight = refs[:5]
    parts = refs[5 : 5 + count]
    out, predicted, sums = refs[5 + count :]
    data_rows = data_weight.shape[0]
    whole_part = total_rows(parts)
    total = whole_part[:data_rows, :]
    predicted[...] = total
    sums[...] = whole_part[data_rows:, :]
    data = (data_weight[...] * (0.0 - total)).astype(BF16)
    terms = products(kept_tiles(codes), pick(rows_pick[...], data))
    cells = source_pair.shape[0]
    out[:cells, :] = gather(source_pair[...], scale[...], terms)
    out[cells:, :] = pack_rows([columns(total * data.astype(F32))], total.shape[1])


def residual_kernel(blocks, order, *refs):
    count = len(order)
    early, late, source_pick, rows_pair, scale, weight, direction, sums = refs[:8]
    parts = by_shift(order, refs[8 : 8 + count])
    out, residual, step = refs[8 + count :]
    cells = source_pick.shape[1]
    weights = weight[...]
    along = direction[...]
    image = weights * along - total_blocks(parts, blocks)
    curve = whole(sums[1:2, :]) - whole(extra_rows(parts, cells)[0:1, :])
    alpha = whole(sums[0:1, :]) / curve
    step[...] = jnp.broadcast_to(alpha, step.shape)
    value = residual_of(along, alpha, image)
    residual[...] = value
    terms = products(turned_tiles(early, late), pick(source_pick[...], value.astype(BF16)))
    data_rows = rows_pair.shape[0]
    out[:data_rows, :] = gather(rows_pair[...], scale[...], terms)
    weighted = value * weights
    out[data_rows:, :] = pack_rows(
        [columns(value * value), columns(weighted * value), columns(weighted * along)],
        value.shape[1],
    )


def residual_of(residual, alpha, image):
    return residual - alpha * image


def second_data_kernel(blocks, count, *refs):
    codes, rows_pick, source_pair, scale, data_weight, predicted, sums = refs[:7]
    parts = refs[7 : 7 + count]
    outs, scalars = refs[7 + count : -1], refs[-1]
    data_rows = data_weight.shape[0]
    whole_part = total_rows(parts)
    norm = whole(whole_part[data_rows : data_rows + 1, :])
    beta = norm / whole(sums[0:1, :])
    curve = whole(
        whole_part[data_rows + 1 : data_rows + 2, :]
        + 2.0 * beta * whole_part[data_rows + 2 : data_rows + 3, :]
        + beta * beta * sums[1:2, :]
    )
    total = whole_part[:data_rows, :] + beta * predicted[...]
    data = (data_weight[...] * (0.0 - total)).astype(BF16)
    terms = products(kept_tiles(codes), pick(rows_pick[...], data))
    cells = gather(source_pair[...], scale[...], terms)
    curved = columns(total * data.astype(F32))
    for group, out in enumerate(outs):
        out[:blocks, :] = cells[group * blocks : (group + 1) * blocks, :]
        out[blocks:, :] = jnp.broadcast_to(curved, (out.shape[0] - blocks, total.shape[1]))
    wide = (1, scalars.shape[1])
    scalars[...] = pack_rows(
        [jnp.broadcast_to(value, wide) for value in (norm, beta, curve)], scalars.shape[1]
    )


def last_kernel(blocks, count, *refs):
    weight, start, first, second, step, scalars = refs[:6]
    parts = refs[6 : 6 + count]
    model, residual = refs[6 + count :]
    norm = scalars[0:1, 0:1]
    beta = scalars[1:2, 0:1]
    curve = scalars[2:3, 0:1]
    along = first[:blocks, :]
    left = second[:blocks, :]
    direction = left + beta * along
    whole_part = total_rows(parts)
    image = weight[:blocks, :] * direction - whole_part[:blocks, :]
    alpha = norm / (curve - whole(whole_part[blocks : blocks + 1, :]))
    model[...] = start[:blocks, :] + step[0:1, 0:1] * along + alpha * direction
    residual[...] = left - alpha * image


def call(body, outs, *args, scratch=()):
    specs = []
    for arg in args:
        far = getattr(jax.typeof(arg), "memory_space", None) == pltpu.HBM
        space = pl.ANY if far else pltpu.SMEM if arg.ndim == 1 else pltpu.VMEM
        specs.append(pl.BlockSpec(memory_space=space))
    return pl.pallas_call(
        body,
        out_shape=[jax.ShapeDtypeStruct(shape, dtype) for shape, dtype in outs],
        in_specs=specs,
        out_specs=[pl.BlockSpec(memory_space=pltpu.VMEM)] * len(outs),
        scratch_shapes=list(scratch),
        compiler_params=pltpu.CompilerParams(vmem_limit_bytes=LIMIT),
    )(*args)


def shards(
    tile_codes,
    tile_scale,
    tile_row,
    tile_column,
    send_index,
    model_start,
    reg_weight,
    observed,
    data_weight,
):
    blocks, width = model_start.shape
    slots = send_index.shape[2]
    data_rows = observed.shape[0]
    tiles = tile_codes.shape[0]
    count = lax.axis_size("tiles")
    sharing = lax.axis_size(("split", "depth"))
    cells = count * blocks
    place = lax.axis_index("tiles").astype(jnp.int32).reshape(1)

    order = [0] + sorted(range(1, count), key=lambda shift: (shift != 1, -abs(2 * shift - count)))

    def across(values):
        parts = exchange(values, "tiles", count)
        return [parts[shift] for shift in order]

    def within(value):
        return exchange([value] * sharing, ("split", "depth"), sharing)

    named = jnp.transpose(send_index, (0, 2, 1)).reshape(slots, count)
    (opening,) = call(
        opening_kernel,
        [((2 * blocks + EXTRA, width), F32)],
        pltpu.with_memory_space_constraint(model_start, pltpu.HBM),
        pltpu.with_memory_space_constraint(reg_weight, pltpu.HBM),
        pltpu.with_memory_space_constraint(named, pltpu.HBM),
        scratch=[
            pltpu.VMEM((blocks, width), F32),
            pltpu.VMEM((blocks, width), F32),
            pltpu.VMEM((slots, count), jnp.int32),
            pltpu.SemaphoreType.DMA((3,)),
        ],
    )
    begin = across([opening] * count)
    codes, early, rows_pick, rows_pair, scale = call(
        loading_kernel,
        [
            (tile_codes.shape, BF16),
            ((tiles - CHUNK, width, width), BF16),
            ((tiles, data_rows), BF16),
            ((data_rows, 2 * tiles), BF16),
            ((tiles, width), F32),
        ],
        pltpu.with_memory_space_constraint(tile_codes, pltpu.HBM),
        opening,
        pltpu.with_memory_space_constraint(tile_scale.reshape(1, -1), pltpu.HBM),
        pltpu.with_memory_space_constraint(tile_row.reshape(1, -1), pltpu.HBM),
        scratch=[
            pltpu.VMEM((1, tiles), F32),
            pltpu.VMEM((1, tiles), jnp.int32),
            pltpu.SemaphoreType.DMA((tiles // CHUNK,)),
            pltpu.SemaphoreType.DMA((2,)),
        ],
    )
    part, source_pick, source_pair, start, weight = call(
        functools.partial(first_kernel, blocks, slots, order),
        [
            ((data_rows, width), F32),
            ((tiles, cells), BF16),
            ((cells, 2 * tiles), BF16),
            ((cells, width), F32),
            ((cells, width), F32),
        ],
        codes,
        early,
        scale,
        rows_pair,
        tile_column.reshape(1, -1),
        place,
        *begin,
    )
    parts = within(part)
    (late,) = call(turning_kernel, [((CHUNK, width, width), BF16)], codes, part)
    (part,) = call(
        functools.partial(start_data_kernel, sharing),
        [((cells, width), F32)],
        codes,
        rows_pick,
        source_pair,
        scale,
        observed,
        data_weight,
        late,
        *parts,
    )
    part, first = call(
        functools.partial(start_residual_kernel, blocks, order),
        [((data_rows + EXTRA, width), F32), ((cells, width), F32)],
        early,
        late,
        source_pick,
        rows_pair,
        scale,
        start,
        weight,
        *across([part] * count),
    )
    part, predicted, sums = call(
        functools.partial(image_data_kernel, sharing),
        [((cells + EXTRA, width), F32), ((data_rows, width), F32), ((EXTRA, width), F32)],
        codes,
        rows_pick,
        source_pair,
        scale,
        data_weight,
        *within(part),
    )
    part, second, step = call(
        functools.partial(residual_kernel, blocks, order),
        [((data_rows + EXTRA, width), F32), ((cells, width), F32), ((8, 128), F32)],
        early,
        late,
        source_pick,
        rows_pair,
        scale,
        weight,
        first,
        sums,
        *across([part] * count),
    )
    *part, scalars = call(
        functools.partial(second_data_kernel, blocks, sharing),
        [((blocks + 4, width), F32)] * count + [((EXTRA, width), F32)],
        codes,
        rows_pick,
        source_pair,
        scale,
        data_weight,
        predicted,
        sums,
        *within(part),
    )
    model, residual = call(
        functools.partial(last_kernel, blocks, count),
        [((blocks, width), F32), ((blocks, width), F32)],
        weight,
        start,
        first,
        second,
        step,
        scalars,
        *[part[0]] + across(part)[:0:-1],
    )
    return (model, residual)


def solution(mesh):
    both = P(("groups", "tiles", "split", "depth"))
    owned = P(("groups", "tiles", "split", "depth"), None)
    wide = P(("groups", "tiles", "split", "depth"), None, None)
    data = P(("groups", "tiles"), None)
    in_specs = (wide, both, both, both, wide, owned, owned, data, data)
    return jax.shard_map(
        shards, mesh=mesh, in_specs=in_specs, out_specs=(owned, owned), check_vma=False
    )
```

```python
import functools

import jax
import jax.numpy as jnp
from jax import lax
from jax.experimental import pallas as pl
from jax.experimental.pallas import tpu as pltpu
from jax.sharding import PartitionSpec as P

HIGH = lax.Precision.HIGHEST
EXTRA = 8
LIMIT = 16 * 1024 * 1024
GROUP = 16
CHUNK = 16
FLIGHT = 2
F32 = jnp.float32
BF16 = jnp.bfloat16


def exchange(values, axes, size):
    parts = [values[0]] + [None] * (size - 1)
    for shift in range(size - 1, 0, -1):
        perm = [(i, i ^ shift) for i in range(size)]
        parts[shift] = lax.ppermute(values[shift], axes, perm)
    return parts


def by_shift(order, parts):
    return [part for _, part in sorted(zip(order, parts), key=lambda pair: pair[0])]


def total_rows(parts):
    total = parts[0][...]
    for part in parts[1:]:
        total = total + part[...]
    return total


def total_blocks(parts, blocks):
    count = len(parts)
    groups = []
    for group in range(count):
        total = None
        for shift in range(count):
            start = (group ^ shift) * blocks
            piece = parts[shift][start : start + blocks, :]
            total = piece if total is None else total + piece
        groups.append(total)
    return jnp.concatenate(groups, axis=0)


def extra_rows(parts, start):
    total = parts[0][start : start + EXTRA, :]
    for part in parts[1:]:
        total = total + part[start : start + EXTRA, :]
    return total


def whole(value):
    return jnp.sum(value, axis=(0, 1), keepdims=True)


def columns(value):
    return jnp.sum(value, axis=0, keepdims=True)


def pack_rows(rows, width):
    filled = list(rows)
    while len(filled) < EXTRA:
        filled.append(jnp.zeros((1, width), F32))
    return jnp.concatenate(filled, axis=0)


def products(tile_of, picked):
    tiles, width = picked.shape
    index = lax.broadcasted_iota(jnp.int32, (GROUP, width), 0)
    pieces = []
    for first in range(0, tiles, GROUP):
        rows = picked[first : first + GROUP, :]
        total = None
        for i in range(GROUP):
            tile, turn = tile_of(first + i)
            dims = (((1,), (1 if turn else 0,)), ((), ()))
            value = lax.dot_general(rows, tile, dims, preferred_element_type=F32)
            total = value if total is None else jnp.where(index == i, value, total)
        pieces.append(total)
    return jnp.concatenate(pieces, axis=0)


def kept_tiles(codes):
    return lambda k: (codes[k], False)


def turned_tiles(early, late, turn=False):
    count = early.shape[0]
    shift = 0 if turn else count
    return lambda k: (early[k], False) if k < count else (late[k - shift], turn)


def pick(table, values):
    return jnp.dot(table, values, preferred_element_type=F32).astype(BF16)


def gather(table, scale, terms):
    scaled = scale * terms
    upper = scaled.astype(BF16)
    lower = (scaled - upper.astype(F32)).astype(BF16)
    both = jnp.concatenate([upper, lower], axis=0)
    return jnp.dot(table, both, preferred_element_type=F32)


def tables(index, values, picks, pairs):
    tiles = index.shape[1]
    hits = lax.broadcasted_iota(jnp.int32, (values, tiles), 0) == index
    ones = jnp.where(hits, 1.0, 0.0)
    picks[...] = ones.T.astype(BF16)
    pairs[...] = jnp.concatenate([ones, ones], axis=1).astype(BF16)


def loading_kernel(far_codes, opening, far_scale, far_row, *refs):
    codes, early, rows_pick, rows_pair, wide_scale, scale, row, done, small = refs
    near = [
        pltpu.make_async_copy(far_scale, scale, small.at[0]),
        pltpu.make_async_copy(far_row, row, small.at[1]),
    ]
    for copy in near:
        copy.start()
    tiles, width = wide_scale.shape
    copies = []
    for chunk in range(tiles // CHUNK):
        span = pl.ds(chunk * CHUNK, CHUNK)
        copies.append(pltpu.make_async_copy(far_codes.at[span], codes.at[span], done.at[chunk]))
    for copy in copies[:FLIGHT]:
        copy.start()
    for copy in near:
        copy.wait()
    tables(row[...], rows_pick.shape[1], rows_pick, rows_pair)
    square = (tiles, tiles)
    same = lax.broadcasted_iota(jnp.int32, square, 0) == lax.broadcasted_iota(jnp.int32, square, 1)
    wide_scale[...] = jnp.dot(
        jnp.where(same, scale[...], 0.0),
        jnp.ones((tiles, width), F32),
        precision=HIGH,
        preferred_element_type=F32,
    )
    for chunk, copy in enumerate(copies):
        copy.wait()
        if chunk + FLIGHT < len(copies):
            copies[chunk + FLIGHT].start()
        for k in range(chunk * CHUNK, min((chunk + 1) * CHUNK, early.shape[0])):
            early[k] = codes[k].T


def turning_kernel(codes, part, late):
    first = codes.shape[0] - late.shape[0]
    for k in range(late.shape[0]):
        late[k] = codes[first + k].T


def opening_kernel(start, weight, named, out, sources, weights, names, done):
    copies = [
        pltpu.make_async_copy(start, sources, done.at[0]),
        pltpu.make_async_copy(weight, weights, done.at[1]),
        pltpu.make_async_copy(named, names, done.at[2]),
    ]
    for copy in copies:
        copy.start()
    blocks, width = sources.shape
    slots, count = names.shape
    rest = out.shape[0] - 2 * blocks
    out[2 * blocks :, :] = jnp.zeros((rest, width), F32)
    for copy in copies:
        copy.wait()
    out[:blocks, :] = sources[...]
    out[blocks : 2 * blocks, :] = weights[...]
    out[2 * blocks : 2 * blocks + slots, :count] = names[...].astype(F32)


def first_kernel(blocks, slots, order, *refs):
    codes, early, scale, rows_pair, column, place = refs[:6]
    count = len(order)
    parts = by_shift(order, refs[6 : 6 + count])
    out, source_pick, source_pair, start, weight = refs[6 + count :]
    width = out.shape[1]
    here = place[0]
    columns_of = column[...]
    source = jnp.where(columns_of < blocks, columns_of, 0)
    lane = lax.broadcasted_iota(jnp.int32, (1, width), 1)
    for shift in range(count):
        other = jnp.bitwise_xor(here, shift)
        for slot in range(slots):
            named = parts[shift][2 * blocks + slot : 2 * blocks + slot + 1, :]
            mine = jnp.where(lane == here, named, 0.0)
            block = jnp.sum(mine, axis=1, keepdims=True).astype(jnp.int32) + shift * blocks
            source = jnp.where(columns_of == blocks + other * slots + slot, block, source)
    tables(source, count * blocks, source_pick, source_pair)
    field = jnp.concatenate([part[:blocks, :] for part in parts], axis=0)
    start[...] = field
    weight[...] = jnp.concatenate([part[blocks : 2 * blocks, :] for part in parts], axis=0)

    terms = products(turned_tiles(early, codes, True), pick(source_pick[...], field.astype(BF16)))
    out[...] = gather(rows_pair[...], scale[...], terms)


def start_data_kernel(count, *refs):
    codes, rows_pick, source_pair, scale, observed, data_weight, late = refs[:7]
    parts = refs[7 : 7 + count]
    out = refs[7 + count]
    total = total_rows(parts)
    data = (data_weight[...] * (observed[...] - total)).astype(BF16)
    terms = products(kept_tiles(codes), pick(rows_pick[...], data))
    out[...] = gather(source_pair[...], scale[...], terms)


def start_residual_kernel(blocks, order, *refs):
    count = len(order)
    early, late, source_pick, rows_pair, scale, start, weight = refs[:7]
    parts = by_shift(order, refs[7 : 7 + count])
    out, residual = refs[7 + count :]
    weights = weight[...]
    value = total_blocks(parts, blocks) - weights * start[...]
    residual[...] = value
    terms = products(turned_tiles(early, late), pick(source_pick[...], value.astype(BF16)))
    data_rows = rows_pair.shape[0]
    out[:data_rows, :] = gather(rows_pair[...], scale[...], terms)
    out[data_rows:, :] = pack_rows(
        [columns(value * value), columns(value * weights * value)], value.shape[1]
    )


def image_data_kernel(count, *refs):
    codes, rows_pick, source_pair, scale, data_weight = refs[:5]
    parts = refs[5 : 5 + count]
    out, predicted, sums = refs[5 + count :]
    data_rows = data_weight.shape[0]
    whole_part = total_rows(parts)
    total = whole_part[:data_rows, :]
    predicted[...] = total
    sums[...] = whole_part[data_rows:, :]
    data = (data_weight[...] * (0.0 - total)).astype(BF16)
    terms = products(kept_tiles(codes), pick(rows_pick[...], data))
    cells = source_pair.shape[0]
    out[:cells, :] = gather(source_pair[...], scale[...], terms)
    out[cells:, :] = pack_rows([columns(total * data.astype(F32))], total.shape[1])


def residual_kernel(blocks, order, *refs):
    count = len(order)
    early, late, source_pick, rows_pair, scale, weight, direction, sums = refs[:8]
    parts = by_shift(order, refs[8 : 8 + count])
    out, residual, step = refs[8 + count :]
    cells = source_pick.shape[1]
    weights = weight[...]
    along = direction[...]
    image = weights * along - total_blocks(parts, blocks)
    curve = whole(sums[1:2, :]) - whole(extra_rows(parts, cells)[0:1, :])
    alpha = whole(sums[0:1, :]) / curve
    step[...] = jnp.broadcast_to(alpha, step.shape)
    value = residual_of(along, alpha, image)
    residual[...] = value
    terms = products(turned_tiles(early, late), pick(source_pick[...], value.astype(BF16)))
    data_rows = rows_pair.shape[0]
    out[:data_rows, :] = gather(rows_pair[...], scale[...], terms)
    weighted = value * weights
    out[data_rows:, :] = pack_rows(
        [columns(value * value), columns(weighted * value), columns(weighted * along)],
        value.shape[1],
    )


def residual_of(residual, alpha, image):
    return residual - alpha * image


def second_data_kernel(blocks, count, *refs):
    codes, rows_pick, source_pair, scale, data_weight, predicted, sums = refs[:7]
    parts = refs[7 : 7 + count]
    outs, scalars = refs[7 + count : -1], refs[-1]
    data_rows = data_weight.shape[0]
    whole_part = total_rows(parts)
    norm = whole(whole_part[data_rows : data_rows + 1, :])
    beta = norm / whole(sums[0:1, :])
    curve = whole(
        whole_part[data_rows + 1 : data_rows + 2, :]
        + 2.0 * beta * whole_part[data_rows + 2 : data_rows + 3, :]
        + beta * beta * sums[1:2, :]
    )
    total = whole_part[:data_rows, :] + beta * predicted[...]
    data = (data_weight[...] * (0.0 - total)).astype(BF16)
    terms = products(kept_tiles(codes), pick(rows_pick[...], data))
    cells = gather(source_pair[...], scale[...], terms)
    curved = columns(total * data.astype(F32))
    for group, out in enumerate(outs):
        out[:blocks, :] = cells[group * blocks : (group + 1) * blocks, :]
        out[blocks:, :] = jnp.broadcast_to(curved, (out.shape[0] - blocks, total.shape[1]))
    wide = (1, scalars.shape[1])
    scalars[...] = pack_rows(
        [jnp.broadcast_to(value, wide) for value in (norm, beta, curve)], scalars.shape[1]
    )


def last_kernel(blocks, count, *refs):
    weight, start, first, second, step, scalars = refs[:6]
    parts = refs[6 : 6 + count]
    model, residual = refs[6 + count :]
    norm = scalars[0:1, 0:1]
    beta = scalars[1:2, 0:1]
    curve = scalars[2:3, 0:1]
    along = first[:blocks, :]
    left = second[:blocks, :]
    direction = left + beta * along
    whole_part = total_rows(parts)
    image = weight[:blocks, :] * direction - whole_part[:blocks, :]
    alpha = norm / (curve - whole(whole_part[blocks : blocks + 1, :]))
    model[...] = start[:blocks, :] + step[0:1, 0:1] * along + alpha * direction
    residual[...] = left - alpha * image


def call(body, outs, *args, scratch=()):
    specs = []
    for arg in args:
        far = getattr(jax.typeof(arg), "memory_space", None) == pltpu.HBM
        space = pl.ANY if far else pltpu.SMEM if arg.ndim == 1 else pltpu.VMEM
        specs.append(pl.BlockSpec(memory_space=space))
    return pl.pallas_call(
        body,
        out_shape=[jax.ShapeDtypeStruct(shape, dtype) for shape, dtype in outs],
        in_specs=specs,
        out_specs=[pl.BlockSpec(memory_space=pltpu.VMEM)] * len(outs),
        scratch_shapes=list(scratch),
        compiler_params=pltpu.CompilerParams(vmem_limit_bytes=LIMIT),
    )(*args)


def shards(
    tile_codes,
    tile_scale,
    tile_row,
    tile_column,
    send_index,
    model_start,
    reg_weight,
    observed,
    data_weight,
):
    blocks, width = model_start.shape
    slots = send_index.shape[2]
    data_rows = observed.shape[0]
    tiles = tile_codes.shape[0]
    count = lax.axis_size("tiles")
    sharing = lax.axis_size(("split", "depth"))
    cells = count * blocks
    late_tiles = tiles // 2
    place = lax.axis_index("tiles").astype(jnp.int32).reshape(1)

    order = [0] + sorted(range(1, count), key=lambda shift: (shift != 1, -abs(2 * shift - count)))

    def across(values):
        parts = exchange(values, "tiles", count)
        return [parts[shift] for shift in order]

    def within(value):
        return exchange([value] * sharing, ("split", "depth"), sharing)

    named = jnp.transpose(send_index, (0, 2, 1)).reshape(slots, count)
    (opening,) = call(
        opening_kernel,
        [((2 * blocks + EXTRA, width), F32)],
        pltpu.with_memory_space_constraint(model_start, pltpu.HBM),
        pltpu.with_memory_space_constraint(reg_weight, pltpu.HBM),
        pltpu.with_memory_space_constraint(named, pltpu.HBM),
        scratch=[
            pltpu.VMEM((blocks, width), F32),
            pltpu.VMEM((blocks, width), F32),
            pltpu.VMEM((slots, count), jnp.int32),
            pltpu.SemaphoreType.DMA((3,)),
        ],
    )
    begin = across([opening] * count)
    codes, early, rows_pick, rows_pair, scale = call(
        loading_kernel,
        [
            (tile_codes.shape, BF16),
            ((tiles - late_tiles, width, width), BF16),
            ((tiles, data_rows), BF16),
            ((data_rows, 2 * tiles), BF16),
            ((tiles, width), F32),
        ],
        pltpu.with_memory_space_constraint(tile_codes, pltpu.HBM),
        opening,
        pltpu.with_memory_space_constraint(tile_scale.reshape(1, -1), pltpu.HBM),
        pltpu.with_memory_space_constraint(tile_row.reshape(1, -1), pltpu.HBM),
        scratch=[
            pltpu.VMEM((1, tiles), F32),
            pltpu.VMEM((1, tiles), jnp.int32),
            pltpu.SemaphoreType.DMA((tiles // CHUNK,)),
            pltpu.SemaphoreType.DMA((2,)),
        ],
    )
    part, source_pick, source_pair, start, weight = call(
        functools.partial(first_kernel, blocks, slots, order),
        [
            ((data_rows, width), F32),
            ((tiles, cells), BF16),
            ((cells, 2 * tiles), BF16),
            ((cells, width), F32),
            ((cells, width), F32),
        ],
        codes,
        early,
        scale,
        rows_pair,
        tile_column.reshape(1, -1),
        place,
        *begin,
    )
    parts = within(part)
    (late,) = call(turning_kernel, [((late_tiles, width, width), BF16)], codes, part)
    (part,) = call(
        functools.partial(start_data_kernel, sharing),
        [((cells, width), F32)],
        codes,
        rows_pick,
        source_pair,
        scale,
        observed,
        data_weight,
        late,
        *parts,
    )
    part, first = call(
        functools.partial(start_residual_kernel, blocks, order),
        [((data_rows + EXTRA, width), F32), ((cells, width), F32)],
        early,
        late,
        source_pick,
        rows_pair,
        scale,
        start,
        weight,
        *across([part] * count),
    )
    part, predicted, sums = call(
        functools.partial(image_data_kernel, sharing),
        [((cells + EXTRA, width), F32), ((data_rows, width), F32), ((EXTRA, width), F32)],
        codes,
        rows_pick,
        source_pair,
        scale,
        data_weight,
        *within(part),
    )
    part, second, step = call(
        functools.partial(residual_kernel, blocks, order),
        [((data_rows + EXTRA, width), F32), ((cells, width), F32), ((8, 128), F32)],
        early,
        late,
        source_pick,
        rows_pair,
        scale,
        weight,
        first,
        sums,
        *across([part] * count),
    )
    *part, scalars = call(
        functools.partial(second_data_kernel, blocks, sharing),
        [((blocks + 4, width), F32)] * count + [((EXTRA, width), F32)],
        codes,
        rows_pick,
        source_pair,
        scale,
        data_weight,
        predicted,
        sums,
        *within(part),
    )
    model, residual = call(
        functools.partial(last_kernel, blocks, count),
        [((blocks, width), F32), ((blocks, width), F32)],
        weight,
        start,
        first,
        second,
        step,
        scalars,
        *[part[0]] + across(part)[:0:-1],
    )
    return (model, residual)


def solution(mesh):
    both = P(("groups", "tiles", "split", "depth"))
    owned = P(("groups", "tiles", "split", "depth"), None)
    wide = P(("groups", "tiles", "split", "depth"), None, None)
    data = P(("groups", "tiles"), None)
    in_specs = (wide, both, both, both, wide, owned, owned, data, data)
    return jax.shard_map(
        shards, mesh=mesh, in_specs=in_specs, out_specs=(owned, owned), check_vma=False
    )
```

```python
import functools

import jax
import jax.numpy as jnp
from jax import lax
from jax.experimental import pallas as pl
from jax.experimental.pallas import tpu as pltpu
from jax.sharding import PartitionSpec as P

HIGH = lax.Precision.HIGHEST
EXTRA = 8
LIMIT = 16 * 1024 * 1024
GROUP = 16
F32 = jnp.float32
BF16 = jnp.bfloat16


def exchange(values, axes, size):
    parts = [values[0]] + [None] * (size - 1)
    for shift in range(size - 1, 0, -1):
        perm = [(i, i ^ shift) for i in range(size)]
        parts[shift] = lax.ppermute(values[shift], axes, perm)
    return parts


def by_shift(order, parts):
    return [part for _, part in sorted(zip(order, parts), key=lambda pair: pair[0])]


def total_rows(parts):
    total = parts[0][...]
    for part in parts[1:]:
        total = total + part[...]
    return total


def total_blocks(parts, blocks):
    count = len(parts)
    groups = []
    for group in range(count):
        total = None
        for shift in range(count):
            start = (group ^ shift) * blocks
            piece = parts[shift][start : start + blocks, :]
            total = piece if total is None else total + piece
        groups.append(total)
    return jnp.concatenate(groups, axis=0)


def extra_rows(parts, start):
    total = parts[0][start : start + EXTRA, :]
    for part in parts[1:]:
        total = total + part[start : start + EXTRA, :]
    return total


def whole(value):
    return jnp.sum(value, axis=(0, 1), keepdims=True)


def columns(value):
    return jnp.sum(value, axis=0, keepdims=True)


def pack_rows(rows, width):
    filled = list(rows)
    while len(filled) < EXTRA:
        filled.append(jnp.zeros((1, width), F32))
    return jnp.concatenate(filled, axis=0)


def products(tile_of, picked):
    tiles, width = picked.shape
    index = lax.broadcasted_iota(jnp.int32, (GROUP, width), 0)
    pieces = []
    for first in range(0, tiles, GROUP):
        rows = picked[first : first + GROUP, :]
        total = None
        for i in range(GROUP):
            tile, turn = tile_of(first + i)
            dims = (((1,), (1 if turn else 0,)), ((), ()))
            value = lax.dot_general(rows, tile, dims, preferred_element_type=F32)
            total = value if total is None else jnp.where(index == i, value, total)
        pieces.append(total)
    return jnp.concatenate(pieces, axis=0)


def kept_tiles(codes):
    return lambda k: (codes[k], False)


def turned_tiles(early, late, turn=False):
    count = early.shape[0]
    shift = 0 if turn else count
    return lambda k: (early[k], False) if k < count else (late[k - shift], turn)


def pick(table, values):
    return jnp.dot(table, values, preferred_element_type=F32).astype(BF16)


def gather(table, scale, terms):
    scaled = scale * terms
    upper = scaled.astype(BF16)
    lower = (scaled - upper.astype(F32)).astype(BF16)
    both = jnp.concatenate([upper, lower], axis=0)
    return jnp.dot(table, both, preferred_element_type=F32)


def tables(index, values, picks, pairs):
    tiles = index.shape[1]
    hits = lax.broadcasted_iota(jnp.int32, (values, tiles), 0) == index
    ones = jnp.where(hits, 1.0, 0.0)
    picks[...] = ones.T.astype(BF16)
    pairs[...] = jnp.concatenate([ones, ones], axis=1).astype(BF16)


def loading_kernel(far_codes, opening, far_scale, far_row, *refs):
    codes, early, rows_pick, rows_pair, wide_scale, scale, row, done, small = refs
    near = [
        pltpu.make_async_copy(far_scale, scale, small.at[0]),
        pltpu.make_async_copy(far_row, row, small.at[1]),
    ]
    for copy in near:
        copy.start()
    tiles, width = wide_scale.shape
    first = early.shape[0]
    spans = [pl.ds(0, first), pl.ds(first, tiles - first)]
    copies = [
        pltpu.make_async_copy(far_codes.at[span], codes.at[span], done.at[i])
        for i, span in enumerate(spans)
    ]
    copies[0].start()
    for copy in near:
        copy.wait()
    tables(row[...], rows_pick.shape[1], rows_pick, rows_pair)
    square = (tiles, tiles)
    same = lax.broadcasted_iota(jnp.int32, square, 0) == lax.broadcasted_iota(jnp.int32, square, 1)
    wide_scale[...] = jnp.dot(
        jnp.where(same, scale[...], 0.0),
        jnp.ones((tiles, width), F32),
        precision=HIGH,
        preferred_element_type=F32,
    )
    copies[0].wait()
    copies[1].start()
    for k in range(first):
        early[k] = codes[k].T
    copies[1].wait()


def turning_kernel(codes, part, late):
    first = codes.shape[0] - late.shape[0]
    for k in range(late.shape[0]):
        late[k] = codes[first + k].T


def opening_kernel(start, weight, named, out, sources, weights, names, done):
    copies = [
        pltpu.make_async_copy(start, sources, done.at[0]),
        pltpu.make_async_copy(weight, weights, done.at[1]),
        pltpu.make_async_copy(named, names, done.at[2]),
    ]
    for copy in copies:
        copy.start()
    blocks, width = sources.shape
    slots, count = names.shape
    rest = out.shape[0] - 2 * blocks
    out[2 * blocks :, :] = jnp.zeros((rest, width), F32)
    for copy in copies:
        copy.wait()
    out[:blocks, :] = sources[...]
    out[blocks : 2 * blocks, :] = weights[...]
    out[2 * blocks : 2 * blocks + slots, :count] = names[...].astype(F32)


def first_kernel(blocks, slots, order, *refs):
    codes, early, scale, rows_pair, column, place = refs[:6]
    count = len(order)
    parts = by_shift(order, refs[6 : 6 + count])
    out, source_pick, source_pair, start, weight = refs[6 + count :]
    width = out.shape[1]
    here = place[0]
    columns_of = column[...]
    source = jnp.where(columns_of < blocks, columns_of, 0)
    lane = lax.broadcasted_iota(jnp.int32, (1, width), 1)
    for shift in range(count):
        other = jnp.bitwise_xor(here, shift)
        for slot in range(slots):
            named = parts[shift][2 * blocks + slot : 2 * blocks + slot + 1, :]
            mine = jnp.where(lane == here, named, 0.0)
            block = jnp.sum(mine, axis=1, keepdims=True).astype(jnp.int32) + shift * blocks
            source = jnp.where(columns_of == blocks + other * slots + slot, block, source)
    tables(source, count * blocks, source_pick, source_pair)
    field = jnp.concatenate([part[:blocks, :] for part in parts], axis=0)
    start[...] = field
    weight[...] = jnp.concatenate([part[blocks : 2 * blocks, :] for part in parts], axis=0)

    terms = products(turned_tiles(early, codes, True), pick(source_pick[...], field.astype(BF16)))
    out[...] = gather(rows_pair[...], scale[...], terms)


def start_data_kernel(count, *refs):
    codes, rows_pick, source_pair, scale, observed, data_weight, late = refs[:7]
    parts = refs[7 : 7 + count]
    out = refs[7 + count]
    total = total_rows(parts)
    data = (data_weight[...] * (observed[...] - total)).astype(BF16)
    terms = products(kept_tiles(codes), pick(rows_pick[...], data))
    out[...] = gather(source_pair[...], scale[...], terms)


def start_residual_kernel(blocks, order, *refs):
    count = len(order)
    early, late, source_pick, rows_pair, scale, start, weight = refs[:7]
    parts = by_shift(order, refs[7 : 7 + count])
    out, residual = refs[7 + count :]
    weights = weight[...]
    value = total_blocks(parts, blocks) - weights * start[...]
    residual[...] = value
    terms = products(turned_tiles(early, late), pick(source_pick[...], value.astype(BF16)))
    data_rows = rows_pair.shape[0]
    out[:data_rows, :] = gather(rows_pair[...], scale[...], terms)
    out[data_rows:, :] = pack_rows(
        [columns(value * value), columns(value * weights * value)], value.shape[1]
    )


def image_data_kernel(count, *refs):
    codes, rows_pick, source_pair, scale, data_weight = refs[:5]
    parts = refs[5 : 5 + count]
    out, predicted, sums = refs[5 + count :]
    data_rows = data_weight.shape[0]
    whole_part = total_rows(parts)
    total = whole_part[:data_rows, :]
    predicted[...] = total
    sums[...] = whole_part[data_rows:, :]
    data = (data_weight[...] * (0.0 - total)).astype(BF16)
    terms = products(kept_tiles(codes), pick(rows_pick[...], data))
    cells = source_pair.shape[0]
    out[:cells, :] = gather(source_pair[...], scale[...], terms)
    out[cells:, :] = pack_rows([columns(total * data.astype(F32))], total.shape[1])


def residual_kernel(blocks, order, *refs):
    count = len(order)
    early, late, source_pick, rows_pair, scale, weight, direction, sums = refs[:8]
    parts = by_shift(order, refs[8 : 8 + count])
    out, residual, step = refs[8 + count :]
    cells = source_pick.shape[1]
    weights = weight[...]
    along = direction[...]
    image = weights * along - total_blocks(parts, blocks)
    curve = whole(sums[1:2, :]) - whole(extra_rows(parts, cells)[0:1, :])
    alpha = whole(sums[0:1, :]) / curve
    step[...] = jnp.broadcast_to(alpha, step.shape)
    value = residual_of(along, alpha, image)
    residual[...] = value
    terms = products(turned_tiles(early, late), pick(source_pick[...], value.astype(BF16)))
    data_rows = rows_pair.shape[0]
    out[:data_rows, :] = gather(rows_pair[...], scale[...], terms)
    weighted = value * weights
    out[data_rows:, :] = pack_rows(
        [columns(value * value), columns(weighted * value), columns(weighted * along)],
        value.shape[1],
    )


def residual_of(residual, alpha, image):
    return residual - alpha * image


def second_data_kernel(blocks, count, *refs):
    codes, rows_pick, source_pair, scale, data_weight, predicted, sums = refs[:7]
    parts = refs[7 : 7 + count]
    outs, scalars = refs[7 + count : -1], refs[-1]
    data_rows = data_weight.shape[0]
    whole_part = total_rows(parts)
    norm = whole(whole_part[data_rows : data_rows + 1, :])
    beta = norm / whole(sums[0:1, :])
    curve = whole(
        whole_part[data_rows + 1 : data_rows + 2, :]
        + 2.0 * beta * whole_part[data_rows + 2 : data_rows + 3, :]
        + beta * beta * sums[1:2, :]
    )
    total = whole_part[:data_rows, :] + beta * predicted[...]
    data = (data_weight[...] * (0.0 - total)).astype(BF16)
    terms = products(kept_tiles(codes), pick(rows_pick[...], data))
    cells = gather(source_pair[...], scale[...], terms)
    curved = columns(total * data.astype(F32))
    for group, out in enumerate(outs):
        out[:blocks, :] = cells[group * blocks : (group + 1) * blocks, :]
        out[blocks:, :] = jnp.broadcast_to(curved, (out.shape[0] - blocks, total.shape[1]))
    wide = (1, scalars.shape[1])
    scalars[...] = pack_rows(
        [jnp.broadcast_to(value, wide) for value in (norm, beta, curve)], scalars.shape[1]
    )


def last_kernel(blocks, count, *refs):
    weight, start, first, second, step, scalars = refs[:6]
    parts = refs[6 : 6 + count]
    model, residual = refs[6 + count :]
    norm = scalars[0:1, 0:1]
    beta = scalars[1:2, 0:1]
    curve = scalars[2:3, 0:1]
    along = first[:blocks, :]
    left = second[:blocks, :]
    direction = left + beta * along
    whole_part = total_rows(parts)
    image = weight[:blocks, :] * direction - whole_part[:blocks, :]
    alpha = norm / (curve - whole(whole_part[blocks : blocks + 1, :]))
    model[...] = start[:blocks, :] + step[0:1, 0:1] * along + alpha * direction
    residual[...] = left - alpha * image


def call(body, outs, *args, scratch=()):
    specs = []
    for arg in args:
        far = getattr(jax.typeof(arg), "memory_space", None) == pltpu.HBM
        space = pl.ANY if far else pltpu.SMEM if arg.ndim == 1 else pltpu.VMEM
        specs.append(pl.BlockSpec(memory_space=space))
    return pl.pallas_call(
        body,
        out_shape=[jax.ShapeDtypeStruct(shape, dtype) for shape, dtype in outs],
        in_specs=specs,
        out_specs=[pl.BlockSpec(memory_space=pltpu.VMEM)] * len(outs),
        scratch_shapes=list(scratch),
        compiler_params=pltpu.CompilerParams(vmem_limit_bytes=LIMIT),
    )(*args)


def shards(
    tile_codes,
    tile_scale,
    tile_row,
    tile_column,
    send_index,
    model_start,
    reg_weight,
    observed,
    data_weight,
):
    blocks, width = model_start.shape
    slots = send_index.shape[2]
    data_rows = observed.shape[0]
    tiles = tile_codes.shape[0]
    count = lax.axis_size("tiles")
    sharing = lax.axis_size(("split", "depth"))
    cells = count * blocks
    late_tiles = tiles * 3 // 8
    place = lax.axis_index("tiles").astype(jnp.int32).reshape(1)

    order = [0] + sorted(range(1, count), key=lambda shift: (shift != 1, -abs(2 * shift - count)))

    def across(values):
        parts = exchange(values, "tiles", count)
        return [parts[shift] for shift in order]

    def within(value):
        return exchange([value] * sharing, ("split", "depth"), sharing)

    named = jnp.transpose(send_index, (0, 2, 1)).reshape(slots, count)
    (opening,) = call(
        opening_kernel,
        [((2 * blocks + EXTRA, width), F32)],
        pltpu.with_memory_space_constraint(model_start, pltpu.HBM),
        pltpu.with_memory_space_constraint(reg_weight, pltpu.HBM),
        pltpu.with_memory_space_constraint(named, pltpu.HBM),
        scratch=[
            pltpu.VMEM((blocks, width), F32),
            pltpu.VMEM((blocks, width), F32),
            pltpu.VMEM((slots, count), jnp.int32),
            pltpu.SemaphoreType.DMA((3,)),
        ],
    )
    begin = across([opening] * count)
    codes, early, rows_pick, rows_pair, scale = call(
        loading_kernel,
        [
            (tile_codes.shape, BF16),
            ((tiles - late_tiles, width, width), BF16),
            ((tiles, data_rows), BF16),
            ((data_rows, 2 * tiles), BF16),
            ((tiles, width), F32),
        ],
        pltpu.with_memory_space_constraint(tile_codes, pltpu.HBM),
        opening,
        pltpu.with_memory_space_constraint(tile_scale.reshape(1, -1), pltpu.HBM),
        pltpu.with_memory_space_constraint(tile_row.reshape(1, -1), pltpu.HBM),
        scratch=[
            pltpu.VMEM((1, tiles), F32),
            pltpu.VMEM((1, tiles), jnp.int32),
            pltpu.SemaphoreType.DMA((2,)),
            pltpu.SemaphoreType.DMA((2,)),
        ],
    )
    part, source_pick, source_pair, start, weight = call(
        functools.partial(first_kernel, blocks, slots, order),
        [
            ((data_rows, width), F32),
            ((tiles, cells), BF16),
            ((cells, 2 * tiles), BF16),
            ((cells, width), F32),
            ((cells, width), F32),
        ],
        codes,
        early,
        scale,
        rows_pair,
        tile_column.reshape(1, -1),
        place,
        *begin,
    )
    parts = within(part)
    (late,) = call(turning_kernel, [((late_tiles, width, width), BF16)], codes, part)
    (part,) = call(
        functools.partial(start_data_kernel, sharing),
        [((cells, width), F32)],
        codes,
        rows_pick,
        source_pair,
        scale,
        observed,
        data_weight,
        late,
        *parts,
    )
    part, first = call(
        functools.partial(start_residual_kernel, blocks, order),
        [((data_rows + EXTRA, width), F32), ((cells, width), F32)],
        early,
        late,
        source_pick,
        rows_pair,
        scale,
        start,
        weight,
        *across([part] * count),
    )
    part, predicted, sums = call(
        functools.partial(image_data_kernel, sharing),
        [((cells + EXTRA, width), F32), ((data_rows, width), F32), ((EXTRA, width), F32)],
        codes,
        rows_pick,
        source_pair,
        scale,
        data_weight,
        *within(part),
    )
    part, second, step = call(
        functools.partial(residual_kernel, blocks, order),
        [((data_rows + EXTRA, width), F32), ((cells, width), F32), ((8, 128), F32)],
        early,
        late,
        source_pick,
        rows_pair,
        scale,
        weight,
        first,
        sums,
        *across([part] * count),
    )
    *part, scalars = call(
        functools.partial(second_data_kernel, blocks, sharing),
        [((blocks + 4, width), F32)] * count + [((EXTRA, width), F32)],
        codes,
        rows_pick,
        source_pair,
        scale,
        data_weight,
        predicted,
        sums,
        *within(part),
    )
    model, residual = call(
        functools.partial(last_kernel, blocks, count),
        [((blocks, width), F32), ((blocks, width), F32)],
        weight,
        start,
        first,
        second,
        step,
        scalars,
        *[part[0]] + across(part)[:0:-1],
    )
    return (model, residual)


def solution(mesh):
    both = P(("groups", "tiles", "split", "depth"))
    owned = P(("groups", "tiles", "split", "depth"), None)
    wide = P(("groups", "tiles", "split", "depth"), None, None)
    data = P(("groups", "tiles"), None)
    in_specs = (wide, both, both, both, wide, owned, owned, data, data)
    return jax.shard_map(
        shards, mesh=mesh, in_specs=in_specs, out_specs=(owned, owned), check_vma=False
    )
```

```python
import functools

import jax
import jax.numpy as jnp
from jax import lax
from jax.experimental import pallas as pl
from jax.experimental.pallas import tpu as pltpu
from jax.sharding import PartitionSpec as P

HIGH = lax.Precision.HIGHEST
EXTRA = 8
LIMIT = 16 * 1024 * 1024
GROUP = 16
CHUNK = 8
F32 = jnp.float32
BF16 = jnp.bfloat16


def exchange(values, axes, size):
    parts = [values[0]] + [None] * (size - 1)
    for shift in range(size - 1, 0, -1):
        perm = [(i, i ^ shift) for i in range(size)]
        parts[shift] = lax.ppermute(values[shift], axes, perm)
    return parts


def by_shift(order, parts):
    return [part for _, part in sorted(zip(order, parts), key=lambda pair: pair[0])]


def total_rows(parts):
    total = parts[0][...]
    for part in parts[1:]:
        total = total + part[...]
    return total


def total_blocks(parts, blocks):
    count = len(parts)
    groups = []
    for group in range(count):
        total = None
        for shift in range(count):
            start = (group ^ shift) * blocks
            piece = parts[shift][start : start + blocks, :]
            total = piece if total is None else total + piece
        groups.append(total)
    return jnp.concatenate(groups, axis=0)


def extra_rows(parts, start):
    total = parts[0][start : start + EXTRA, :]
    for part in parts[1:]:
        total = total + part[start : start + EXTRA, :]
    return total


def whole(value):
    return jnp.sum(value, axis=(0, 1), keepdims=True)


def columns(value):
    return jnp.sum(value, axis=0, keepdims=True)


def pack_rows(rows, width):
    filled = list(rows)
    while len(filled) < EXTRA:
        filled.append(jnp.zeros((1, width), F32))
    return jnp.concatenate(filled, axis=0)


def products(tile_of, picked):
    tiles, width = picked.shape
    index = lax.broadcasted_iota(jnp.int32, (GROUP, width), 0)
    pieces = []
    for first in range(0, tiles, GROUP):
        rows = picked[first : first + GROUP, :]
        total = None
        for i in range(GROUP):
            tile, turn = tile_of(first + i)
            dims = (((1,), (1 if turn else 0,)), ((), ()))
            value = lax.dot_general(rows, tile, dims, preferred_element_type=F32)
            total = value if total is None else jnp.where(index == i, value, total)
        pieces.append(total)
    return jnp.concatenate(pieces, axis=0)


def kept_tiles(low, high):
    count = low.shape[0]
    return lambda k: (low[k], False) if k < count else (high[k - count], False)


def pick(table, values):
    return jnp.dot(table, values, preferred_element_type=F32).astype(BF16)


def gather(table, scale, terms):
    scaled = scale * terms
    upper = scaled.astype(BF16)
    lower = (scaled - upper.astype(F32)).astype(BF16)
    both = jnp.concatenate([upper, lower], axis=0)
    return jnp.dot(table, both, preferred_element_type=F32)


def tables(index, values, picks, pairs):
    tiles = index.shape[1]
    hits = lax.broadcasted_iota(jnp.int32, (values, tiles), 0) == index
    ones = jnp.where(hits, 1.0, 0.0)
    picks[...] = ones.T.astype(BF16)
    pairs[...] = jnp.concatenate([ones, ones], axis=1).astype(BF16)


def chunk_copies(codes, first, kept, done):
    copies = []
    for chunk in range(kept.shape[0] // CHUNK):
        source = codes.at[pl.ds(first + chunk * CHUNK, CHUNK)]
        target = kept.at[pl.ds(chunk * CHUNK, CHUNK)]
        copies.append(pltpu.make_async_copy(source, target, done.at[chunk]))
        copies[-1].start()
    return copies


def loading_kernel(far_codes, opening, far_scale, far_row, *refs):
    low, early, rows_pick, rows_pair, wide_scale, scale, row, done, small = refs
    near = [
        pltpu.make_async_copy(far_scale, scale, small.at[0]),
        pltpu.make_async_copy(far_row, row, small.at[1]),
    ]
    for copy in near:
        copy.start()
    tiles, width = wide_scale.shape
    copies = chunk_copies(far_codes, 0, low, done)
    for copy in near:
        copy.wait()
    tables(row[...], rows_pick.shape[1], rows_pick, rows_pair)
    square = (tiles, tiles)
    same = lax.broadcasted_iota(jnp.int32, square, 0) == lax.broadcasted_iota(jnp.int32, square, 1)
    wide_scale[...] = jnp.dot(
        jnp.where(same, scale[...], 0.0),
        jnp.ones((tiles, width), F32),
        precision=HIGH,
        preferred_element_type=F32,
    )
    for chunk, copy in enumerate(copies):
        copy.wait()
        for k in range(chunk * CHUNK, min((chunk + 1) * CHUNK, early.shape[0])):
            early[k] = low[k].T


def turning_kernel(low, high, part, late):
    first = low.shape[0] + high.shape[0] - late.shape[0]
    tile_of = kept_tiles(low, high)
    for k in range(late.shape[0]):
        tile, _ = tile_of(first + k)
        late[k] = tile.T


def opening_kernel(start, weight, named, out, sources, weights, names, done):
    copies = [
        pltpu.make_async_copy(start, sources, done.at[0]),
        pltpu.make_async_copy(weight, weights, done.at[1]),
        pltpu.make_async_copy(named, names, done.at[2]),
    ]
    for copy in copies:
        copy.start()
    blocks, width = sources.shape
    slots, count = names.shape
    rest = out.shape[0] - 2 * blocks
    out[2 * blocks :, :] = jnp.zeros((rest, width), F32)
    for copy in copies:
        copy.wait()
    out[:blocks, :] = sources[...]
    out[blocks : 2 * blocks, :] = weights[...]
    out[2 * blocks : 2 * blocks + slots, :count] = names[...].astype(F32)


def first_kernel(blocks, slots, order, *refs):
    far_codes, low, early, scale, rows_pair, column, place = refs[:7]
    count = len(order)
    parts = by_shift(order, refs[7 : 7 + count])
    out, high, source_pick, source_pair, start, weight, done = refs[7 + count :]
    loaded = low.shape[0]
    copies = chunk_copies(far_codes, loaded, high, done)
    width = out.shape[1]
    here = place[0]
    columns_of = column[...]
    source = jnp.where(columns_of < blocks, columns_of, 0)
    lane = lax.broadcasted_iota(jnp.int32, (1, width), 1)
    for shift in range(count):
        other = jnp.bitwise_xor(here, shift)
        for slot in range(slots):
            named = parts[shift][2 * blocks + slot : 2 * blocks + slot + 1, :]
            mine = jnp.where(lane == here, named, 0.0)
            block = jnp.sum(mine, axis=1, keepdims=True).astype(jnp.int32) + shift * blocks
            source = jnp.where(columns_of == blocks + other * slots + slot, block, source)
    tables(source, count * blocks, source_pick, source_pair)
    field = jnp.concatenate([part[:blocks, :] for part in parts], axis=0)
    start[...] = field
    weight[...] = jnp.concatenate([part[blocks : 2 * blocks, :] for part in parts], axis=0)


    def tile_of(k):
        if k < early.shape[0]:
            return early[k], False
        if k < loaded:
            return low[k], True
        if (k - loaded) % CHUNK == 0:
            copies[(k - loaded) // CHUNK].wait()
        return high[k - loaded], True

    terms = products(tile_of, pick(source_pick[...], field.astype(BF16)))
    out[...] = gather(rows_pair[...], scale[...], terms)


def start_data_kernel(count, *refs):
    low, high, rows_pick, source_pair, scale, observed, data_weight, late = refs[:8]
    parts = refs[8 : 8 + count]
    out = refs[8 + count]
    total = total_rows(parts)
    data = (data_weight[...] * (observed[...] - total)).astype(BF16)
    terms = products(kept_tiles(low, high), pick(rows_pick[...], data))
    out[...] = gather(source_pair[...], scale[...], terms)


def start_residual_kernel(blocks, order, *refs):
    count = len(order)
    early, late, source_pick, rows_pair, scale, start, weight = refs[:7]
    parts = by_shift(order, refs[7 : 7 + count])
    out, residual = refs[7 + count :]
    weights = weight[...]
    value = total_blocks(parts, blocks) - weights * start[...]
    residual[...] = value
    terms = products(kept_tiles(early, late), pick(source_pick[...], value.astype(BF16)))
    data_rows = rows_pair.shape[0]
    out[:data_rows, :] = gather(rows_pair[...], scale[...], terms)
    out[data_rows:, :] = pack_rows(
        [columns(value * value), columns(value * weights * value)], value.shape[1]
    )


def image_data_kernel(count, *refs):
    low, high, rows_pick, source_pair, scale, data_weight = refs[:6]
    parts = refs[6 : 6 + count]
    out, predicted, sums = refs[6 + count :]
    data_rows = data_weight.shape[0]
    whole_part = total_rows(parts)
    total = whole_part[:data_rows, :]
    predicted[...] = total
    sums[...] = whole_part[data_rows:, :]
    data = (data_weight[...] * (0.0 - total)).astype(BF16)
    terms = products(kept_tiles(low, high), pick(rows_pick[...], data))
    cells = source_pair.shape[0]
    out[:cells, :] = gather(source_pair[...], scale[...], terms)
    out[cells:, :] = pack_rows([columns(total * data.astype(F32))], total.shape[1])


def residual_kernel(blocks, order, *refs):
    count = len(order)
    early, late, source_pick, rows_pair, scale, weight, direction, sums = refs[:8]
    parts = by_shift(order, refs[8 : 8 + count])
    out, residual, step = refs[8 + count :]
    cells = source_pick.shape[1]
    weights = weight[...]
    along = direction[...]
    image = weights * along - total_blocks(parts, blocks)
    curve = whole(sums[1:2, :]) - whole(extra_rows(parts, cells)[0:1, :])
    alpha = whole(sums[0:1, :]) / curve
    step[...] = jnp.broadcast_to(alpha, step.shape)
    value = residual_of(along, alpha, image)
    residual[...] = value
    terms = products(kept_tiles(early, late), pick(source_pick[...], value.astype(BF16)))
    data_rows = rows_pair.shape[0]
    out[:data_rows, :] = gather(rows_pair[...], scale[...], terms)
    weighted = value * weights
    out[data_rows:, :] = pack_rows(
        [columns(value * value), columns(weighted * value), columns(weighted * along)],
        value.shape[1],
    )


def residual_of(residual, alpha, image):
    return residual - alpha * image


def second_data_kernel(blocks, count, *refs):
    low, high, rows_pick, source_pair, scale, data_weight, predicted, sums = refs[:8]
    parts = refs[8 : 8 + count]
    outs, scalars = refs[8 + count : -1], refs[-1]
    data_rows = data_weight.shape[0]
    whole_part = total_rows(parts)
    norm = whole(whole_part[data_rows : data_rows + 1, :])
    beta = norm / whole(sums[0:1, :])
    curve = whole(
        whole_part[data_rows + 1 : data_rows + 2, :]
        + 2.0 * beta * whole_part[data_rows + 2 : data_rows + 3, :]
        + beta * beta * sums[1:2, :]
    )
    total = whole_part[:data_rows, :] + beta * predicted[...]
    data = (data_weight[...] * (0.0 - total)).astype(BF16)
    terms = products(kept_tiles(low, high), pick(rows_pick[...], data))
    cells = gather(source_pair[...], scale[...], terms)
    curved = columns(total * data.astype(F32))
    for group, out in enumerate(outs):
        out[:blocks, :] = cells[group * blocks : (group + 1) * blocks, :]
        out[blocks:, :] = jnp.broadcast_to(curved, (out.shape[0] - blocks, total.shape[1]))
    wide = (1, scalars.shape[1])
    scalars[...] = pack_rows(
        [jnp.broadcast_to(value, wide) for value in (norm, beta, curve)], scalars.shape[1]
    )


def last_kernel(blocks, count, *refs):
    weight, start, first, second, step, scalars = refs[:6]
    parts = refs[6 : 6 + count]
    model, residual = refs[6 + count :]
    norm = scalars[0:1, 0:1]
    beta = scalars[1:2, 0:1]
    curve = scalars[2:3, 0:1]
    along = first[:blocks, :]
    left = second[:blocks, :]
    direction = left + beta * along
    whole_part = total_rows(parts)
    image = weight[:blocks, :] * direction - whole_part[:blocks, :]
    alpha = norm / (curve - whole(whole_part[blocks : blocks + 1, :]))
    model[...] = start[:blocks, :] + step[0:1, 0:1] * along + alpha * direction
    residual[...] = left - alpha * image


def call(body, outs, *args, scratch=()):
    specs = []
    for arg in args:
        far = getattr(jax.typeof(arg), "memory_space", None) == pltpu.HBM
        space = pl.ANY if far else pltpu.SMEM if arg.ndim == 1 else pltpu.VMEM
        specs.append(pl.BlockSpec(memory_space=space))
    return pl.pallas_call(
        body,
        out_shape=[jax.ShapeDtypeStruct(shape, dtype) for shape, dtype in outs],
        in_specs=specs,
        out_specs=[pl.BlockSpec(memory_space=pltpu.VMEM)] * len(outs),
        scratch_shapes=list(scratch),
        compiler_params=pltpu.CompilerParams(vmem_limit_bytes=LIMIT),
    )(*args)


def shards(
    tile_codes,
    tile_scale,
    tile_row,
    tile_column,
    send_index,
    model_start,
    reg_weight,
    observed,
    data_weight,
):
    blocks, width = model_start.shape
    slots = send_index.shape[2]
    data_rows = observed.shape[0]
    tiles = tile_codes.shape[0]
    count = lax.axis_size("tiles")
    sharing = lax.axis_size(("split", "depth"))
    cells = count * blocks
    late_tiles = tiles // 2
    loaded = tiles * 5 // 8
    codes = pltpu.with_memory_space_constraint(tile_codes, pltpu.HBM)
    place = lax.axis_index("tiles").astype(jnp.int32).reshape(1)

    order = [0] + sorted(range(1, count), key=lambda shift: (shift != 1, -abs(2 * shift - count)))

    def across(values):
        parts = exchange(values, "tiles", count)
        return [parts[shift] for shift in order]

    def within(value):
        return exchange([value] * sharing, ("split", "depth"), sharing)

    named = jnp.transpose(send_index, (0, 2, 1)).reshape(slots, count)
    (opening,) = call(
        opening_kernel,
        [((2 * blocks + EXTRA, width), F32)],
        pltpu.with_memory_space_constraint(model_start, pltpu.HBM),
        pltpu.with_memory_space_constraint(reg_weight, pltpu.HBM),
        pltpu.with_memory_space_constraint(named, pltpu.HBM),
        scratch=[
            pltpu.VMEM((blocks, width), F32),
            pltpu.VMEM((blocks, width), F32),
            pltpu.VMEM((slots, count), jnp.int32),
            pltpu.SemaphoreType.DMA((3,)),
        ],
    )
    begin = across([opening] * count)
    low, early, rows_pick, rows_pair, scale = call(
        loading_kernel,
        [
            ((loaded, width, width), BF16),
            ((tiles - late_tiles, width, width), BF16),
            ((tiles, data_rows), BF16),
            ((data_rows, 2 * tiles), BF16),
            ((tiles, width), F32),
        ],
        codes,
        opening,
        pltpu.with_memory_space_constraint(tile_scale.reshape(1, -1), pltpu.HBM),
        pltpu.with_memory_space_constraint(tile_row.reshape(1, -1), pltpu.HBM),
        scratch=[
            pltpu.VMEM((1, tiles), F32),
            pltpu.VMEM((1, tiles), jnp.int32),
            pltpu.SemaphoreType.DMA((loaded // CHUNK,)),
            pltpu.SemaphoreType.DMA((2,)),
        ],
    )
    part, high, source_pick, source_pair, start, weight = call(
        functools.partial(first_kernel, blocks, slots, order),
        [
            ((data_rows, width), F32),
            ((tiles - loaded, width, width), BF16),
            ((tiles, cells), BF16),
            ((cells, 2 * tiles), BF16),
            ((cells, width), F32),
            ((cells, width), F32),
        ],
        codes,
        low,
        early,
        scale,
        rows_pair,
        tile_column.reshape(1, -1),
        place,
        *begin,
        scratch=[pltpu.SemaphoreType.DMA(((tiles - loaded) // CHUNK,))],
    )
    parts = within(part)
    (late,) = call(turning_kernel, [((late_tiles, width, width), BF16)], low, high, part)
    (part,) = call(
        functools.partial(start_data_kernel, sharing),
        [((cells, width), F32)],
        low,
        high,
        rows_pick,
        source_pair,
        scale,
        observed,
        data_weight,
        late,
        *parts,
    )
    part, first = call(
        functools.partial(start_residual_kernel, blocks, order),
        [((data_rows + EXTRA, width), F32), ((cells, width), F32)],
        early,
        late,
        source_pick,
        rows_pair,
        scale,
        start,
        weight,
        *across([part] * count),
    )
    part, predicted, sums = call(
        functools.partial(image_data_kernel, sharing),
        [((cells + EXTRA, width), F32), ((data_rows, width), F32), ((EXTRA, width), F32)],
        low,
        high,
        rows_pick,
        source_pair,
        scale,
        data_weight,
        *within(part),
    )
    part, second, step = call(
        functools.partial(residual_kernel, blocks, order),
        [((data_rows + EXTRA, width), F32), ((cells, width), F32), ((8, 128), F32)],
        early,
        late,
        source_pick,
        rows_pair,
        scale,
        weight,
        first,
        sums,
        *across([part] * count),
    )
    *part, scalars = call(
        functools.partial(second_data_kernel, blocks, sharing),
        [((blocks + 4, width), F32)] * count + [((EXTRA, width), F32)],
        low,
        high,
        rows_pick,
        source_pair,
        scale,
        data_weight,
        predicted,
        sums,
        *within(part),
    )
    model, residual = call(
        functools.partial(last_kernel, blocks, count),
        [((blocks, width), F32), ((blocks, width), F32)],
        weight,
        start,
        first,
        second,
        step,
        scalars,
        *[part[0]] + across(part)[:0:-1],
    )
    return (model, residual)


def solution(mesh):
    both = P(("groups", "tiles", "split", "depth"))
    owned = P(("groups", "tiles", "split", "depth"), None)
    wide = P(("groups", "tiles", "split", "depth"), None, None)
    data = P(("groups", "tiles"), None)
    in_specs = (wide, both, both, both, wide, owned, owned, data, data)
    return jax.shard_map(
        shards, mesh=mesh, in_specs=in_specs, out_specs=(owned, owned), check_vma=False
    )
```

```python
import functools

import jax
import jax.numpy as jnp
from jax import lax
from jax.experimental import pallas as pl
from jax.experimental.pallas import tpu as pltpu
from jax.sharding import PartitionSpec as P

HIGH = lax.Precision.HIGHEST
EXTRA = 8
LIMIT = 16 * 1024 * 1024
GROUP = 16
CHUNK = 8
F32 = jnp.float32
BF16 = jnp.bfloat16


def exchange(values, axes, size):
    parts = [values[0]] + [None] * (size - 1)
    for shift in range(size - 1, 0, -1):
        perm = [(i, i ^ shift) for i in range(size)]
        parts[shift] = lax.ppermute(values[shift], axes, perm)
    return parts


def by_shift(order, parts):
    return [part for _, part in sorted(zip(order, parts), key=lambda pair: pair[0])]


def total_rows(parts):
    total = parts[0][...]
    for part in parts[1:]:
        total = total + part[...]
    return total


def total_blocks(parts, blocks):
    count = len(parts)
    groups = []
    for group in range(count):
        total = None
        for shift in range(count):
            start = (group ^ shift) * blocks
            piece = parts[shift][start : start + blocks, :]
            total = piece if total is None else total + piece
        groups.append(total)
    return jnp.concatenate(groups, axis=0)


def extra_rows(parts, start):
    total = parts[0][start : start + EXTRA, :]
    for part in parts[1:]:
        total = total + part[start : start + EXTRA, :]
    return total


def whole(value):
    return jnp.sum(value, axis=(0, 1), keepdims=True)


def columns(value):
    return jnp.sum(value, axis=0, keepdims=True)


def pack_rows(rows, width):
    filled = list(rows)
    while len(filled) < EXTRA:
        filled.append(jnp.zeros((1, width), F32))
    return jnp.concatenate(filled, axis=0)


def products(tile_of, picked):
    tiles, width = picked.shape
    index = lax.broadcasted_iota(jnp.int32, (GROUP, width), 0)
    pieces = []
    for first in range(0, tiles, GROUP):
        rows = picked[first : first + GROUP, :]
        total = None
        for i in range(GROUP):
            tile, turn = tile_of(first + i)
            dims = (((1,), (1 if turn else 0,)), ((), ()))
            value = lax.dot_general(rows, tile, dims, preferred_element_type=F32)
            total = value if total is None else jnp.where(index == i, value, total)
        pieces.append(total)
    return jnp.concatenate(pieces, axis=0)


def kept_tiles(low, high):
    count = low.shape[0]
    return lambda k: (low[k], False) if k < count else (high[k - count], False)


def pick(table, values):
    return jnp.dot(table, values, preferred_element_type=F32).astype(BF16)


def gather(table, scale, terms):
    scaled = scale * terms
    upper = scaled.astype(BF16)
    lower = (scaled - upper.astype(F32)).astype(BF16)
    both = jnp.concatenate([upper, lower], axis=0)
    return jnp.dot(table, both, preferred_element_type=F32)


def tables(index, values, picks, pairs):
    tiles = index.shape[1]
    hits = lax.broadcasted_iota(jnp.int32, (values, tiles), 0) == index
    ones = jnp.where(hits, 1.0, 0.0)
    picks[...] = ones.T.astype(BF16)
    pairs[...] = jnp.concatenate([ones, ones], axis=1).astype(BF16)


def chunk_copies(codes, first, kept, done):
    copies = []
    for chunk in range(kept.shape[0] // CHUNK):
        source = codes.at[pl.ds(first + chunk * CHUNK, CHUNK)]
        target = kept.at[pl.ds(chunk * CHUNK, CHUNK)]
        copies.append(pltpu.make_async_copy(source, target, done.at[chunk]))
        copies[-1].start()
    return copies


def loading_kernel(far_codes, opening, far_scale, far_row, *refs):
    low, rows_pick, rows_pair, wide_scale, scale, row, done, small = refs
    near = [
        pltpu.make_async_copy(far_scale, scale, small.at[0]),
        pltpu.make_async_copy(far_row, row, small.at[1]),
    ]
    for copy in near:
        copy.start()
    tiles, width = wide_scale.shape
    copies = chunk_copies(far_codes, 0, low, done)
    for copy in near:
        copy.wait()
    tables(row[...], rows_pick.shape[1], rows_pick, rows_pair)
    square = (tiles, tiles)
    same = lax.broadcasted_iota(jnp.int32, square, 0) == lax.broadcasted_iota(jnp.int32, square, 1)
    wide_scale[...] = jnp.dot(
        jnp.where(same, scale[...], 0.0),
        jnp.ones((tiles, width), F32),
        precision=HIGH,
        preferred_element_type=F32,
    )
    for copy in copies:
        copy.wait()


def turning_kernel(first, low, high, part, turned):
    tile_of = kept_tiles(low, high)
    for k in range(turned.shape[0]):
        tile, _ = tile_of(first + k)
        turned[k] = tile.T


def opening_kernel(start, weight, named, out, sources, weights, names, done):
    copies = [
        pltpu.make_async_copy(start, sources, done.at[0]),
        pltpu.make_async_copy(weight, weights, done.at[1]),
        pltpu.make_async_copy(named, names, done.at[2]),
    ]
    for copy in copies:
        copy.start()
    blocks, width = sources.shape
    slots, count = names.shape
    rest = out.shape[0] - 2 * blocks
    out[2 * blocks :, :] = jnp.zeros((rest, width), F32)
    for copy in copies:
        copy.wait()
    out[:blocks, :] = sources[...]
    out[blocks : 2 * blocks, :] = weights[...]
    out[2 * blocks : 2 * blocks + slots, :count] = names[...].astype(F32)


def first_kernel(blocks, slots, order, *refs):
    far_codes, low, scale, rows_pair, column, place = refs[:6]
    count = len(order)
    parts = by_shift(order, refs[6 : 6 + count])
    out, high, source_pick, source_pair, start, weight, done = refs[6 + count :]
    loaded = low.shape[0]
    copies = chunk_copies(far_codes, loaded, high, done)
    width = out.shape[1]
    here = place[0]
    columns_of = column[...]
    source = jnp.where(columns_of < blocks, columns_of, 0)
    lane = lax.broadcasted_iota(jnp.int32, (1, width), 1)
    for shift in range(count):
        other = jnp.bitwise_xor(here, shift)
        for slot in range(slots):
            named = parts[shift][2 * blocks + slot : 2 * blocks + slot + 1, :]
            mine = jnp.where(lane == here, named, 0.0)
            block = jnp.sum(mine, axis=1, keepdims=True).astype(jnp.int32) + shift * blocks
            source = jnp.where(columns_of == blocks + other * slots + slot, block, source)
    tables(source, count * blocks, source_pick, source_pair)
    field = jnp.concatenate([part[:blocks, :] for part in parts], axis=0)
    start[...] = field
    weight[...] = jnp.concatenate([part[blocks : 2 * blocks, :] for part in parts], axis=0)


    def tile_of(k):
        if k < loaded:
            return low[k], True
        if (k - loaded) % CHUNK == 0:
            copies[(k - loaded) // CHUNK].wait()
        return high[k - loaded], True

    terms = products(tile_of, pick(source_pick[...], field.astype(BF16)))
    out[...] = gather(rows_pair[...], scale[...], terms)


def start_data_kernel(count, *refs):
    low, high, rows_pick, source_pair, scale, observed, data_weight, turned = refs[:8]
    parts = refs[8 : 8 + count]
    out = refs[8 + count]
    total = total_rows(parts)
    data = (data_weight[...] * (observed[...] - total)).astype(BF16)
    terms = products(kept_tiles(low, high), pick(rows_pick[...], data))
    out[...] = gather(source_pair[...], scale[...], terms)


def start_residual_kernel(blocks, order, *refs):
    count = len(order)
    early, late, source_pick, rows_pair, scale, start, weight = refs[:7]
    parts = by_shift(order, refs[7 : 7 + count])
    out, residual = refs[7 + count :]
    weights = weight[...]
    value = total_blocks(parts, blocks) - weights * start[...]
    residual[...] = value
    terms = products(kept_tiles(early, late), pick(source_pick[...], value.astype(BF16)))
    data_rows = rows_pair.shape[0]
    out[:data_rows, :] = gather(rows_pair[...], scale[...], terms)
    out[data_rows:, :] = pack_rows(
        [columns(value * value), columns(value * weights * value)], value.shape[1]
    )


def image_data_kernel(count, *refs):
    low, high, rows_pick, source_pair, scale, data_weight = refs[:6]
    parts = refs[6 : 6 + count]
    out, predicted, sums = refs[6 + count :]
    data_rows = data_weight.shape[0]
    whole_part = total_rows(parts)
    total = whole_part[:data_rows, :]
    predicted[...] = total
    sums[...] = whole_part[data_rows:, :]
    data = (data_weight[...] * (0.0 - total)).astype(BF16)
    terms = products(kept_tiles(low, high), pick(rows_pick[...], data))
    cells = source_pair.shape[0]
    out[:cells, :] = gather(source_pair[...], scale[...], terms)
    out[cells:, :] = pack_rows([columns(total * data.astype(F32))], total.shape[1])


def residual_kernel(blocks, order, *refs):
    count = len(order)
    early, late, source_pick, rows_pair, scale, weight, direction, sums = refs[:8]
    parts = by_shift(order, refs[8 : 8 + count])
    out, residual, step = refs[8 + count :]
    cells = source_pick.shape[1]
    weights = weight[...]
    along = direction[...]
    image = weights * along - total_blocks(parts, blocks)
    curve = whole(sums[1:2, :]) - whole(extra_rows(parts, cells)[0:1, :])
    alpha = whole(sums[0:1, :]) / curve
    step[...] = jnp.broadcast_to(alpha, step.shape)
    value = residual_of(along, alpha, image)
    residual[...] = value
    terms = products(kept_tiles(early, late), pick(source_pick[...], value.astype(BF16)))
    data_rows = rows_pair.shape[0]
    out[:data_rows, :] = gather(rows_pair[...], scale[...], terms)
    weighted = value * weights
    out[data_rows:, :] = pack_rows(
        [columns(value * value), columns(weighted * value), columns(weighted * along)],
        value.shape[1],
    )


def residual_of(residual, alpha, image):
    return residual - alpha * image


def second_data_kernel(blocks, count, *refs):
    low, high, rows_pick, source_pair, scale, data_weight, predicted, sums = refs[:8]
    parts = refs[8 : 8 + count]
    outs, scalars = refs[8 + count : -1], refs[-1]
    data_rows = data_weight.shape[0]
    whole_part = total_rows(parts)
    norm = whole(whole_part[data_rows : data_rows + 1, :])
    beta = norm / whole(sums[0:1, :])
    curve = whole(
        whole_part[data_rows + 1 : data_rows + 2, :]
        + 2.0 * beta * whole_part[data_rows + 2 : data_rows + 3, :]
        + beta * beta * sums[1:2, :]
    )
    total = whole_part[:data_rows, :] + beta * predicted[...]
    data = (data_weight[...] * (0.0 - total)).astype(BF16)
    terms = products(kept_tiles(low, high), pick(rows_pick[...], data))
    cells = gather(source_pair[...], scale[...], terms)
    curved = columns(total * data.astype(F32))
    for group, out in enumerate(outs):
        out[:blocks, :] = cells[group * blocks : (group + 1) * blocks, :]
        out[blocks:, :] = jnp.broadcast_to(curved, (out.shape[0] - blocks, total.shape[1]))
    wide = (1, scalars.shape[1])
    scalars[...] = pack_rows(
        [jnp.broadcast_to(value, wide) for value in (norm, beta, curve)], scalars.shape[1]
    )


def last_kernel(blocks, count, *refs):
    weight, start, first, second, step, scalars = refs[:6]
    parts = refs[6 : 6 + count]
    model, residual = refs[6 + count :]
    norm = scalars[0:1, 0:1]
    beta = scalars[1:2, 0:1]
    curve = scalars[2:3, 0:1]
    along = first[:blocks, :]
    left = second[:blocks, :]
    direction = left + beta * along
    whole_part = total_rows(parts)
    image = weight[:blocks, :] * direction - whole_part[:blocks, :]
    alpha = norm / (curve - whole(whole_part[blocks : blocks + 1, :]))
    model[...] = start[:blocks, :] + step[0:1, 0:1] * along + alpha * direction
    residual[...] = left - alpha * image


def call(body, outs, *args, scratch=()):
    specs = []
    for arg in args:
        far = getattr(jax.typeof(arg), "memory_space", None) == pltpu.HBM
        space = pl.ANY if far else pltpu.SMEM if arg.ndim == 1 else pltpu.VMEM
        specs.append(pl.BlockSpec(memory_space=space))
    return pl.pallas_call(
        body,
        out_shape=[jax.ShapeDtypeStruct(shape, dtype) for shape, dtype in outs],
        in_specs=specs,
        out_specs=[pl.BlockSpec(memory_space=pltpu.VMEM)] * len(outs),
        scratch_shapes=list(scratch),
        compiler_params=pltpu.CompilerParams(vmem_limit_bytes=LIMIT),
    )(*args)


def shards(
    tile_codes,
    tile_scale,
    tile_row,
    tile_column,
    send_index,
    model_start,
    reg_weight,
    observed,
    data_weight,
):
    blocks, width = model_start.shape
    slots = send_index.shape[2]
    data_rows = observed.shape[0]
    tiles = tile_codes.shape[0]
    count = lax.axis_size("tiles")
    sharing = lax.axis_size(("split", "depth"))
    cells = count * blocks
    half = tiles // 2
    loaded = tiles * 5 // 8
    codes = pltpu.with_memory_space_constraint(tile_codes, pltpu.HBM)
    place = lax.axis_index("tiles").astype(jnp.int32).reshape(1)

    order = [0] + sorted(range(1, count), key=lambda shift: (shift != 1, -abs(2 * shift - count)))

    def across(values):
        parts = exchange(values, "tiles", count)
        return [parts[shift] for shift in order]

    def within(value):
        return exchange([value] * sharing, ("split", "depth"), sharing)

    named = jnp.transpose(send_index, (0, 2, 1)).reshape(slots, count)
    (opening,) = call(
        opening_kernel,
        [((2 * blocks + EXTRA, width), F32)],
        pltpu.with_memory_space_constraint(model_start, pltpu.HBM),
        pltpu.with_memory_space_constraint(reg_weight, pltpu.HBM),
        pltpu.with_memory_space_constraint(named, pltpu.HBM),
        scratch=[
            pltpu.VMEM((blocks, width), F32),
            pltpu.VMEM((blocks, width), F32),
            pltpu.VMEM((slots, count), jnp.int32),
            pltpu.SemaphoreType.DMA((3,)),
        ],
    )
    begin = across([opening] * count)
    low, rows_pick, rows_pair, scale = call(
        loading_kernel,
        [
            ((loaded, width, width), BF16),
            ((tiles, data_rows), BF16),
            ((data_rows, 2 * tiles), BF16),
            ((tiles, width), F32),
        ],
        codes,
        opening,
        pltpu.with_memory_space_constraint(tile_scale.reshape(1, -1), pltpu.HBM),
        pltpu.with_memory_space_constraint(tile_row.reshape(1, -1), pltpu.HBM),
        scratch=[
            pltpu.VMEM((1, tiles), F32),
            pltpu.VMEM((1, tiles), jnp.int32),
            pltpu.SemaphoreType.DMA((loaded // CHUNK,)),
            pltpu.SemaphoreType.DMA((2,)),
        ],
    )
    part, high, source_pick, source_pair, start, weight = call(
        functools.partial(first_kernel, blocks, slots, order),
        [
            ((data_rows, width), F32),
            ((tiles - loaded, width, width), BF16),
            ((tiles, cells), BF16),
            ((cells, 2 * tiles), BF16),
            ((cells, width), F32),
            ((cells, width), F32),
        ],
        codes,
        low,
        scale,
        rows_pair,
        tile_column.reshape(1, -1),
        place,
        *begin,
        scratch=[pltpu.SemaphoreType.DMA(((tiles - loaded) // CHUNK,))],
    )
    parts = within(part)

    def turned_half(first, part):
        (turned,) = call(
            functools.partial(turning_kernel, first),
            [((half, width, width), BF16)],
            low,
            high,
            part,
        )
        return turned

    early = turned_half(0, part)
    (part,) = call(
        functools.partial(start_data_kernel, sharing),
        [((cells, width), F32)],
        low,
        high,
        rows_pick,
        source_pair,
        scale,
        observed,
        data_weight,
        early,
        *parts,
    )
    parts = across([part] * count)
    late = turned_half(half, part)
    part, first = call(
        functools.partial(start_residual_kernel, blocks, order),
        [((data_rows + EXTRA, width), F32), ((cells, width), F32)],
        early,
        late,
        source_pick,
        rows_pair,
        scale,
        start,
        weight,
        *parts,
    )
    part, predicted, sums = call(
        functools.partial(image_data_kernel, sharing),
        [((cells + EXTRA, width), F32), ((data_rows, width), F32), ((EXTRA, width), F32)],
        low,
        high,
        rows_pick,
        source_pair,
        scale,
        data_weight,
        *within(part),
    )
    part, second, step = call(
        functools.partial(residual_kernel, blocks, order),
        [((data_rows + EXTRA, width), F32), ((cells, width), F32), ((8, 128), F32)],
        early,
        late,
        source_pick,
        rows_pair,
        scale,
        weight,
        first,
        sums,
        *across([part] * count),
    )
    *part, scalars = call(
        functools.partial(second_data_kernel, blocks, sharing),
        [((blocks + 4, width), F32)] * count + [((EXTRA, width), F32)],
        low,
        high,
        rows_pick,
        source_pair,
        scale,
        data_weight,
        predicted,
        sums,
        *within(part),
    )
    model, residual = call(
        functools.partial(last_kernel, blocks, count),
        [((blocks, width), F32), ((blocks, width), F32)],
        weight,
        start,
        first,
        second,
        step,
        scalars,
        *[part[0]] + across(part)[:0:-1],
    )
    return (model, residual)


def solution(mesh):
    both = P(("groups", "tiles", "split", "depth"))
    owned = P(("groups", "tiles", "split", "depth"), None)
    wide = P(("groups", "tiles", "split", "depth"), None, None)
    data = P(("groups", "tiles"), None)
    in_specs = (wide, both, both, both, wide, owned, owned, data, data)
    return jax.shard_map(
        shards, mesh=mesh, in_specs=in_specs, out_specs=(owned, owned), check_vma=False
    )
```

```python
import functools

import jax
import jax.numpy as jnp
from jax import lax
from jax.experimental import pallas as pl
from jax.experimental.pallas import tpu as pltpu
from jax.sharding import PartitionSpec as P

HIGH = lax.Precision.HIGHEST
EXTRA = 8
LIMIT = 16 * 1024 * 1024
GROUP = 16
CHUNK = 8
F32 = jnp.float32
BF16 = jnp.bfloat16


def exchange(values, axes, size):
    parts = [values[0]] + [None] * (size - 1)
    for shift in range(size - 1, 0, -1):
        perm = [(i, i ^ shift) for i in range(size)]
        parts[shift] = lax.ppermute(values[shift], axes, perm)
    return parts


def by_shift(order, parts):
    return [part for _, part in sorted(zip(order, parts), key=lambda pair: pair[0])]


def total_rows(parts):
    total = parts[0][...]
    for part in parts[1:]:
        total = total + part[...]
    return total


def total_blocks(parts, blocks):
    count = len(parts)
    groups = []
    for group in range(count):
        total = None
        for shift in range(count):
            start = (group ^ shift) * blocks
            piece = parts[shift][start : start + blocks, :]
            total = piece if total is None else total + piece
        groups.append(total)
    return jnp.concatenate(groups, axis=0)


def extra_rows(parts, start):
    total = parts[0][start : start + EXTRA, :]
    for part in parts[1:]:
        total = total + part[start : start + EXTRA, :]
    return total


def whole(value):
    return jnp.sum(value, axis=(0, 1), keepdims=True)


def columns(value):
    return jnp.sum(value, axis=0, keepdims=True)


def pack_rows(rows, width):
    filled = list(rows)
    while len(filled) < EXTRA:
        filled.append(jnp.zeros((1, width), F32))
    return jnp.concatenate(filled, axis=0)


def products(tile_of, picked):
    tiles, width = picked.shape
    index = lax.broadcasted_iota(jnp.int32, (GROUP, width), 0)
    pieces = []
    for first in range(0, tiles, GROUP):
        rows = picked[first : first + GROUP, :]
        total = None
        for i in range(GROUP):
            tile, turn = tile_of(first + i)
            dims = (((1,), (1 if turn else 0,)), ((), ()))
            value = lax.dot_general(rows, tile, dims, preferred_element_type=F32)
            total = value if total is None else jnp.where(index == i, value, total)
        pieces.append(total)
    return jnp.concatenate(pieces, axis=0)


def kept_tiles(low, high):
    count = low.shape[0]
    return lambda k: (low[k], False) if k < count else (high[k - count], False)


def pick(table, values):
    return jnp.dot(table, values, preferred_element_type=F32).astype(BF16)


def gather(table, scale, terms):
    scaled = scale * terms
    upper = scaled.astype(BF16)
    lower = (scaled - upper.astype(F32)).astype(BF16)
    both = jnp.concatenate([upper, lower], axis=0)
    return jnp.dot(table, both, preferred_element_type=F32)


def tables(index, values, picks, pairs):
    tiles = index.shape[1]
    hits = lax.broadcasted_iota(jnp.int32, (values, tiles), 0) == index
    ones = jnp.where(hits, 1.0, 0.0)
    picks[...] = ones.T.astype(BF16)
    pairs[...] = jnp.concatenate([ones, ones], axis=1).astype(BF16)


def chunk_copies(codes, first, kept, done):
    copies = []
    for chunk in range(kept.shape[0] // CHUNK):
        source = codes.at[pl.ds(first + chunk * CHUNK, CHUNK)]
        target = kept.at[pl.ds(chunk * CHUNK, CHUNK)]
        copies.append(pltpu.make_async_copy(source, target, done.at[chunk]))
        copies[-1].start()
    return copies


def loading_kernel(far_codes, opening, far_scale, far_row, *refs):
    low, rows_pick, rows_pair, wide_scale, scale, row, done, small = refs
    near = [
        pltpu.make_async_copy(far_scale, scale, small.at[0]),
        pltpu.make_async_copy(far_row, row, small.at[1]),
    ]
    for copy in near:
        copy.start()
    tiles, width = wide_scale.shape
    copies = chunk_copies(far_codes, 0, low, done)
    for copy in near:
        copy.wait()
    tables(row[...], rows_pick.shape[1], rows_pick, rows_pair)
    square = (tiles, tiles)
    same = lax.broadcasted_iota(jnp.int32, square, 0) == lax.broadcasted_iota(jnp.int32, square, 1)
    wide_scale[...] = jnp.dot(
        jnp.where(same, scale[...], 0.0),
        jnp.ones((tiles, width), F32),
        precision=HIGH,
        preferred_element_type=F32,
    )
    for copy in copies:
        copy.wait()


def turning_kernel(first, low, high, part, turned):
    tile_of = kept_tiles(low, high)
    for k in range(turned.shape[0]):
        tile, _ = tile_of(first + k)
        turned[k] = tile.T


def opening_kernel(start, weight, named, out, sources, weights, names, done):
    copies = [
        pltpu.make_async_copy(start, sources, done.at[0]),
        pltpu.make_async_copy(weight, weights, done.at[1]),
        pltpu.make_async_copy(named, names, done.at[2]),
    ]
    for copy in copies:
        copy.start()
    blocks, width = sources.shape
    slots, count = names.shape
    rest = out.shape[0] - 2 * blocks
    out[2 * blocks :, :] = jnp.zeros((rest, width), F32)
    for copy in copies:
        copy.wait()
    out[:blocks, :] = sources[...]
    out[blocks : 2 * blocks, :] = weights[...]
    out[2 * blocks : 2 * blocks + slots, :count] = names[...].astype(F32)


def first_kernel(blocks, slots, order, *refs):
    far_codes, low, scale, rows_pair, column, place = refs[:6]
    count = len(order)
    parts = by_shift(order, refs[6 : 6 + count])
    out, high, source_pick, source_pair, start, weight, done = refs[6 + count :]
    loaded = low.shape[0]
    copies = chunk_copies(far_codes, loaded, high, done)
    width = out.shape[1]
    here = place[0]
    columns_of = column[...]
    source = jnp.where(columns_of < blocks, columns_of, 0)
    lane = lax.broadcasted_iota(jnp.int32, (1, width), 1)
    for shift in range(count):
        other = jnp.bitwise_xor(here, shift)
        for slot in range(slots):
            named = parts[shift][2 * blocks + slot : 2 * blocks + slot + 1, :]
            mine = jnp.where(lane == here, named, 0.0)
            block = jnp.sum(mine, axis=1, keepdims=True).astype(jnp.int32) + shift * blocks
            source = jnp.where(columns_of == blocks + other * slots + slot, block, source)
    tables(source, count * blocks, source_pick, source_pair)
    field = jnp.concatenate([part[:blocks, :] for part in parts], axis=0)
    start[...] = field
    weight[...] = jnp.concatenate([part[blocks : 2 * blocks, :] for part in parts], axis=0)


    def tile_of(k):
        if k < loaded:
            return low[k], True
        if (k - loaded) % CHUNK == 0:
            copies[(k - loaded) // CHUNK].wait()
        return high[k - loaded], True

    terms = products(tile_of, pick(source_pick[...], field.astype(BF16)))
    out[...] = gather(rows_pair[...], scale[...], terms)


def start_data_kernel(count, *refs):
    low, high, rows_pick, source_pair, scale, observed, data_weight, turned = refs[:8]
    parts = refs[8 : 8 + count]
    out = refs[8 + count]
    total = total_rows(parts)
    data = (data_weight[...] * (observed[...] - total)).astype(BF16)
    terms = products(kept_tiles(low, high), pick(rows_pick[...], data))
    out[...] = gather(source_pair[...], scale[...], terms)


def start_residual_kernel(blocks, order, *refs):
    count = len(order)
    early, late, source_pick, rows_pair, scale, start, weight = refs[:7]
    parts = by_shift(order, refs[7 : 7 + count])
    out, residual = refs[7 + count :]
    weights = weight[...]
    value = total_blocks(parts, blocks) - weights * start[...]
    residual[...] = value
    terms = products(kept_tiles(early, late), pick(source_pick[...], value.astype(BF16)))
    data_rows = rows_pair.shape[0]
    out[:data_rows, :] = gather(rows_pair[...], scale[...], terms)
    out[data_rows:, :] = pack_rows(
        [columns(value * value), columns(value * weights * value)], value.shape[1]
    )


def image_data_kernel(count, *refs):
    low, high, rows_pick, source_pair, scale, data_weight = refs[:6]
    parts = refs[6 : 6 + count]
    out, predicted, sums = refs[6 + count :]
    data_rows = data_weight.shape[0]
    whole_part = total_rows(parts)
    total = whole_part[:data_rows, :]
    predicted[...] = total
    sums[...] = whole_part[data_rows:, :]
    data = (data_weight[...] * (0.0 - total)).astype(BF16)
    terms = products(kept_tiles(low, high), pick(rows_pick[...], data))
    cells = source_pair.shape[0]
    out[:cells, :] = gather(source_pair[...], scale[...], terms)
    out[cells:, :] = pack_rows([columns(total * data.astype(F32))], total.shape[1])


def residual_kernel(blocks, order, *refs):
    count = len(order)
    early, late, source_pick, rows_pair, scale, weight, direction, sums = refs[:8]
    parts = by_shift(order, refs[8 : 8 + count])
    out, residual, step = refs[8 + count :]
    cells = source_pick.shape[1]
    weights = weight[...]
    along = direction[...]
    image = weights * along - total_blocks(parts, blocks)
    curve = whole(sums[1:2, :]) - whole(extra_rows(parts, cells)[0:1, :])
    alpha = whole(sums[0:1, :]) / curve
    step[...] = jnp.broadcast_to(alpha, step.shape)
    value = residual_of(along, alpha, image)
    residual[...] = value
    terms = products(kept_tiles(early, late), pick(source_pick[...], value.astype(BF16)))
    data_rows = rows_pair.shape[0]
    out[:data_rows, :] = gather(rows_pair[...], scale[...], terms)
    weighted = value * weights
    out[data_rows:, :] = pack_rows(
        [columns(value * value), columns(weighted * value), columns(weighted * along)],
        value.shape[1],
    )


def residual_of(residual, alpha, image):
    return residual - alpha * image


def second_data_kernel(blocks, count, *refs):
    low, high, rows_pick, source_pair, scale, data_weight, predicted, sums = refs[:8]
    parts = refs[8 : 8 + count]
    outs, scalars = refs[8 + count : -1], refs[-1]
    data_rows = data_weight.shape[0]
    whole_part = total_rows(parts)
    norm = whole(whole_part[data_rows : data_rows + 1, :])
    beta = norm / whole(sums[0:1, :])
    curve = whole(
        whole_part[data_rows + 1 : data_rows + 2, :]
        + 2.0 * beta * whole_part[data_rows + 2 : data_rows + 3, :]
        + beta * beta * sums[1:2, :]
    )
    total = whole_part[:data_rows, :] + beta * predicted[...]
    data = (data_weight[...] * (0.0 - total)).astype(BF16)
    terms = products(kept_tiles(low, high), pick(rows_pick[...], data))
    cells = gather(source_pair[...], scale[...], terms)
    curved = columns(total * data.astype(F32))
    for group, out in enumerate(outs):
        out[:blocks, :] = cells[group * blocks : (group + 1) * blocks, :]
        out[blocks:, :] = jnp.broadcast_to(curved, (out.shape[0] - blocks, total.shape[1]))
    wide = (1, scalars.shape[1])
    scalars[...] = pack_rows(
        [jnp.broadcast_to(value, wide) for value in (norm, beta, curve)], scalars.shape[1]
    )


def last_kernel(blocks, count, *refs):
    weight, start, first, second, step, scalars = refs[:6]
    parts = refs[6 : 6 + count]
    model, residual = refs[6 + count :]
    norm = scalars[0:1, 0:1]
    beta = scalars[1:2, 0:1]
    curve = scalars[2:3, 0:1]
    along = first[:blocks, :]
    left = second[:blocks, :]
    direction = left + beta * along
    whole_part = total_rows(parts)
    image = weight[:blocks, :] * direction - whole_part[:blocks, :]
    alpha = norm / (curve - whole(whole_part[blocks : blocks + 1, :]))
    model[...] = start[:blocks, :] + step[0:1, 0:1] * along + alpha * direction
    residual[...] = left - alpha * image


def call(body, outs, *args, scratch=()):
    specs = []
    for arg in args:
        far = getattr(jax.typeof(arg), "memory_space", None) == pltpu.HBM
        space = pl.ANY if far else pltpu.SMEM if arg.ndim == 1 else pltpu.VMEM
        specs.append(pl.BlockSpec(memory_space=space))
    return pl.pallas_call(
        body,
        out_shape=[jax.ShapeDtypeStruct(shape, dtype) for shape, dtype in outs],
        in_specs=specs,
        out_specs=[pl.BlockSpec(memory_space=pltpu.VMEM)] * len(outs),
        scratch_shapes=list(scratch),
        compiler_params=pltpu.CompilerParams(vmem_limit_bytes=LIMIT),
    )(*args)


def shards(
    tile_codes,
    tile_scale,
    tile_row,
    tile_column,
    send_index,
    model_start,
    reg_weight,
    observed,
    data_weight,
):
    blocks, width = model_start.shape
    slots = send_index.shape[2]
    data_rows = observed.shape[0]
    tiles = tile_codes.shape[0]
    count = lax.axis_size("tiles")
    sharing = lax.axis_size(("split", "depth"))
    cells = count * blocks
    half = tiles // 2
    loaded = tiles * 3 // 4
    codes = pltpu.with_memory_space_constraint(tile_codes, pltpu.HBM)
    place = lax.axis_index("tiles").astype(jnp.int32).reshape(1)

    order = [0] + sorted(range(1, count), key=lambda shift: (shift != 1, -abs(2 * shift - count)))

    def across(values):
        parts = exchange(values, "tiles", count)
        return [parts[shift] for shift in order]

    def within(value):
        return exchange([value] * sharing, ("split", "depth"), sharing)

    named = jnp.transpose(send_index, (0, 2, 1)).reshape(slots, count)
    (opening,) = call(
        opening_kernel,
        [((2 * blocks + EXTRA, width), F32)],
        pltpu.with_memory_space_constraint(model_start, pltpu.HBM),
        pltpu.with_memory_space_constraint(reg_weight, pltpu.HBM),
        pltpu.with_memory_space_constraint(named, pltpu.HBM),
        scratch=[
            pltpu.VMEM((blocks, width), F32),
            pltpu.VMEM((blocks, width), F32),
            pltpu.VMEM((slots, count), jnp.int32),
            pltpu.SemaphoreType.DMA((3,)),
        ],
    )
    begin = across([opening] * count)
    low, rows_pick, rows_pair, scale = call(
        loading_kernel,
        [
            ((loaded, width, width), BF16),
            ((tiles, data_rows), BF16),
            ((data_rows, 2 * tiles), BF16),
            ((tiles, width), F32),
        ],
        codes,
        opening,
        pltpu.with_memory_space_constraint(tile_scale.reshape(1, -1), pltpu.HBM),
        pltpu.with_memory_space_constraint(tile_row.reshape(1, -1), pltpu.HBM),
        scratch=[
            pltpu.VMEM((1, tiles), F32),
            pltpu.VMEM((1, tiles), jnp.int32),
            pltpu.SemaphoreType.DMA((loaded // CHUNK,)),
            pltpu.SemaphoreType.DMA((2,)),
        ],
    )
    part, high, source_pick, source_pair, start, weight = call(
        functools.partial(first_kernel, blocks, slots, order),
        [
            ((data_rows, width), F32),
            ((tiles - loaded, width, width), BF16),
            ((tiles, cells), BF16),
            ((cells, 2 * tiles), BF16),
            ((cells, width), F32),
            ((cells, width), F32),
        ],
        codes,
        low,
        scale,
        rows_pair,
        tile_column.reshape(1, -1),
        place,
        *begin,
        scratch=[pltpu.SemaphoreType.DMA(((tiles - loaded) // CHUNK,))],
    )
    parts = within(part)

    def turned_half(first, part):
        (turned,) = call(
            functools.partial(turning_kernel, first),
            [((half, width, width), BF16)],
            low,
            high,
            part,
        )
        return turned

    early = turned_half(0, part)
    (part,) = call(
        functools.partial(start_data_kernel, sharing),
        [((cells, width), F32)],
        low,
        high,
        rows_pick,
        source_pair,
        scale,
        observed,
        data_weight,
        early,
        *parts,
    )
    parts = across([part] * count)
    late = turned_half(half, part)
    part, first = call(
        functools.partial(start_residual_kernel, blocks, order),
        [((data_rows + EXTRA, width), F32), ((cells, width), F32)],
        early,
        late,
        source_pick,
        rows_pair,
        scale,
        start,
        weight,
        *parts,
    )
    part, predicted, sums = call(
        functools.partial(image_data_kernel, sharing),
        [((cells + EXTRA, width), F32), ((data_rows, width), F32), ((EXTRA, width), F32)],
        low,
        high,
        rows_pick,
        source_pair,
        scale,
        data_weight,
        *within(part),
    )
    part, second, step = call(
        functools.partial(residual_kernel, blocks, order),
        [((data_rows + EXTRA, width), F32), ((cells, width), F32), ((8, 128), F32)],
        early,
        late,
        source_pick,
        rows_pair,
        scale,
        weight,
        first,
        sums,
        *across([part] * count),
    )
    *part, scalars = call(
        functools.partial(second_data_kernel, blocks, sharing),
        [((blocks + 4, width), F32)] * count + [((EXTRA, width), F32)],
        low,
        high,
        rows_pick,
        source_pair,
        scale,
        data_weight,
        predicted,
        sums,
        *within(part),
    )
    model, residual = call(
        functools.partial(last_kernel, blocks, count),
        [((blocks, width), F32), ((blocks, width), F32)],
        weight,
        start,
        first,
        second,
        step,
        scalars,
        *[part[0]] + across(part)[:0:-1],
    )
    return (model, residual)


def solution(mesh):
    both = P(("groups", "tiles", "split", "depth"))
    owned = P(("groups", "tiles", "split", "depth"), None)
    wide = P(("groups", "tiles", "split", "depth"), None, None)
    data = P(("groups", "tiles"), None)
    in_specs = (wide, both, both, both, wide, owned, owned, data, data)
    return jax.shard_map(
        shards, mesh=mesh, in_specs=in_specs, out_specs=(owned, owned), check_vma=False
    )
```

```python
import functools

import jax
import jax.numpy as jnp
from jax import lax
from jax.experimental import pallas as pl
from jax.experimental.pallas import tpu as pltpu
from jax.sharding import PartitionSpec as P

HIGH = lax.Precision.HIGHEST
EXTRA = 8
LIMIT = 16 * 1024 * 1024
GROUP = 16
CHUNK = 16
F32 = jnp.float32
BF16 = jnp.bfloat16


def exchange(values, axes, size):
    parts = [values[0]] + [None] * (size - 1)
    for shift in range(size - 1, 0, -1):
        perm = [(i, i ^ shift) for i in range(size)]
        parts[shift] = lax.ppermute(values[shift], axes, perm)
    return parts


def by_shift(order, parts):
    return [part for _, part in sorted(zip(order, parts), key=lambda pair: pair[0])]


def total_rows(parts):
    total = parts[0][...]
    for part in parts[1:]:
        total = total + part[...]
    return total


def total_blocks(parts, blocks):
    count = len(parts)
    groups = []
    for group in range(count):
        total = None
        for shift in range(count):
            start = (group ^ shift) * blocks
            piece = parts[shift][start : start + blocks, :]
            total = piece if total is None else total + piece
        groups.append(total)
    return jnp.concatenate(groups, axis=0)


def extra_rows(parts, start):
    total = parts[0][start : start + EXTRA, :]
    for part in parts[1:]:
        total = total + part[start : start + EXTRA, :]
    return total


def whole(value):
    return jnp.sum(value, axis=(0, 1), keepdims=True)


def columns(value):
    return jnp.sum(value, axis=0, keepdims=True)


def pack_rows(rows, width):
    filled = list(rows)
    while len(filled) < EXTRA:
        filled.append(jnp.zeros((1, width), F32))
    return jnp.concatenate(filled, axis=0)


def products(tile_of, picked):
    tiles, width = picked.shape
    index = lax.broadcasted_iota(jnp.int32, (GROUP, width), 0)
    pieces = []
    for first in range(0, tiles, GROUP):
        rows = picked[first : first + GROUP, :]
        total = None
        for i in range(GROUP):
            tile, turn = tile_of(first + i)
            dims = (((1,), (1 if turn else 0,)), ((), ()))
            value = lax.dot_general(rows, tile, dims, preferred_element_type=F32)
            total = value if total is None else jnp.where(index == i, value, total)
        pieces.append(total)
    return jnp.concatenate(pieces, axis=0)


def kept_tiles(low, high):
    count = low.shape[0]
    return lambda k: (low[k], False) if k < count else (high[k - count], False)


def pick(table, values):
    return jnp.dot(table, values, preferred_element_type=F32).astype(BF16)


def gather(table, scale, terms):
    scaled = scale * terms
    upper = scaled.astype(BF16)
    lower = (scaled - upper.astype(F32)).astype(BF16)
    both = jnp.concatenate([upper, lower], axis=0)
    return jnp.dot(table, both, preferred_element_type=F32)


def tables(index, values, picks, pairs):
    tiles = index.shape[1]
    hits = lax.broadcasted_iota(jnp.int32, (values, tiles), 0) == index
    ones = jnp.where(hits, 1.0, 0.0)
    picks[...] = ones.T.astype(BF16)
    pairs[...] = jnp.concatenate([ones, ones], axis=1).astype(BF16)


def chunk_copies(codes, first, kept, done):
    copies = []
    for chunk in range(kept.shape[0] // CHUNK):
        source = codes.at[pl.ds(first + chunk * CHUNK, CHUNK)]
        target = kept.at[pl.ds(chunk * CHUNK, CHUNK)]
        copies.append(pltpu.make_async_copy(source, target, done.at[chunk]))
        copies[-1].start()
    return copies


def loading_kernel(far_codes, opening, far_scale, far_row, *refs):
    low, rows_pick, rows_pair, wide_scale, scale, row, done, small = refs
    near = [
        pltpu.make_async_copy(far_scale, scale, small.at[0]),
        pltpu.make_async_copy(far_row, row, small.at[1]),
    ]
    for copy in near:
        copy.start()
    tiles, width = wide_scale.shape
    copies = chunk_copies(far_codes, 0, low, done)
    for copy in near:
        copy.wait()
    tables(row[...], rows_pick.shape[1], rows_pick, rows_pair)
    square = (tiles, tiles)
    same = lax.broadcasted_iota(jnp.int32, square, 0) == lax.broadcasted_iota(jnp.int32, square, 1)
    wide_scale[...] = jnp.dot(
        jnp.where(same, scale[...], 0.0),
        jnp.ones((tiles, width), F32),
        precision=HIGH,
        preferred_element_type=F32,
    )
    for copy in copies:
        copy.wait()


def turning_kernel(first, low, high, part, turned):
    tile_of = kept_tiles(low, high)
    for k in range(turned.shape[0]):
        tile, _ = tile_of(first + k)
        turned[k] = tile.T


def opening_kernel(start, weight, named, out, sources, weights, names, done):
    copies = [
        pltpu.make_async_copy(start, sources, done.at[0]),
        pltpu.make_async_copy(weight, weights, done.at[1]),
        pltpu.make_async_copy(named, names, done.at[2]),
    ]
    for copy in copies:
        copy.start()
    blocks, width = sources.shape
    slots, count = names.shape
    rest = out.shape[0] - 2 * blocks
    out[2 * blocks :, :] = jnp.zeros((rest, width), F32)
    for copy in copies:
        copy.wait()
    out[:blocks, :] = sources[...]
    out[blocks : 2 * blocks, :] = weights[...]
    out[2 * blocks : 2 * blocks + slots, :count] = names[...].astype(F32)


def first_kernel(blocks, slots, order, *refs):
    far_codes, low, scale, rows_pair, column, place = refs[:6]
    count = len(order)
    parts = by_shift(order, refs[6 : 6 + count])
    out, high, source_pick, source_pair, start, weight, done = refs[6 + count :]
    loaded = low.shape[0]
    copies = chunk_copies(far_codes, loaded, high, done)
    width = out.shape[1]
    here = place[0]
    columns_of = column[...]
    source = jnp.where(columns_of < blocks, columns_of, 0)
    lane = lax.broadcasted_iota(jnp.int32, (1, width), 1)
    for shift in range(count):
        other = jnp.bitwise_xor(here, shift)
        for slot in range(slots):
            named = parts[shift][2 * blocks + slot : 2 * blocks + slot + 1, :]
            mine = jnp.where(lane == here, named, 0.0)
            block = jnp.sum(mine, axis=1, keepdims=True).astype(jnp.int32) + shift * blocks
            source = jnp.where(columns_of == blocks + other * slots + slot, block, source)
    tables(source, count * blocks, source_pick, source_pair)
    field = jnp.concatenate([part[:blocks, :] for part in parts], axis=0)
    start[...] = field
    weight[...] = jnp.concatenate([part[blocks : 2 * blocks, :] for part in parts], axis=0)


    def tile_of(k):
        if k < loaded:
            return low[k], True
        if (k - loaded) % CHUNK == 0:
            copies[(k - loaded) // CHUNK].wait()
        return high[k - loaded], True

    terms = products(tile_of, pick(source_pick[...], field.astype(BF16)))
    out[...] = gather(rows_pair[...], scale[...], terms)


def start_data_kernel(count, *refs):
    low, high, rows_pick, source_pair, scale, observed, data_weight, turned = refs[:8]
    parts = refs[8 : 8 + count]
    out = refs[8 + count]
    total = total_rows(parts)
    data = (data_weight[...] * (observed[...] - total)).astype(BF16)
    terms = products(kept_tiles(low, high), pick(rows_pick[...], data))
    out[...] = gather(source_pair[...], scale[...], terms)


def start_residual_kernel(blocks, order, *refs):
    count = len(order)
    early, late, source_pick, rows_pair, scale, start, weight = refs[:7]
    parts = by_shift(order, refs[7 : 7 + count])
    out, residual = refs[7 + count :]
    weights = weight[...]
    value = total_blocks(parts, blocks) - weights * start[...]
    residual[...] = value
    terms = products(kept_tiles(early, late), pick(source_pick[...], value.astype(BF16)))
    data_rows = rows_pair.shape[0]
    out[:data_rows, :] = gather(rows_pair[...], scale[...], terms)
    out[data_rows:, :] = pack_rows(
        [columns(value * value), columns(value * weights * value)], value.shape[1]
    )


def image_data_kernel(count, *refs):
    low, high, rows_pick, source_pair, scale, data_weight = refs[:6]
    parts = refs[6 : 6 + count]
    out, predicted, sums = refs[6 + count :]
    data_rows = data_weight.shape[0]
    whole_part = total_rows(parts)
    total = whole_part[:data_rows, :]
    predicted[...] = total
    sums[...] = whole_part[data_rows:, :]
    data = (data_weight[...] * (0.0 - total)).astype(BF16)
    terms = products(kept_tiles(low, high), pick(rows_pick[...], data))
    cells = source_pair.shape[0]
    out[:cells, :] = gather(source_pair[...], scale[...], terms)
    out[cells:, :] = pack_rows([columns(total * data.astype(F32))], total.shape[1])


def residual_kernel(blocks, order, *refs):
    count = len(order)
    early, late, source_pick, rows_pair, scale, weight, direction, sums = refs[:8]
    parts = by_shift(order, refs[8 : 8 + count])
    out, residual, step = refs[8 + count :]
    cells = source_pick.shape[1]
    weights = weight[...]
    along = direction[...]
    image = weights * along - total_blocks(parts, blocks)
    curve = whole(sums[1:2, :]) - whole(extra_rows(parts, cells)[0:1, :])
    alpha = whole(sums[0:1, :]) / curve
    step[...] = jnp.broadcast_to(alpha, step.shape)
    value = residual_of(along, alpha, image)
    residual[...] = value
    terms = products(kept_tiles(early, late), pick(source_pick[...], value.astype(BF16)))
    data_rows = rows_pair.shape[0]
    out[:data_rows, :] = gather(rows_pair[...], scale[...], terms)
    weighted = value * weights
    out[data_rows:, :] = pack_rows(
        [columns(value * value), columns(weighted * value), columns(weighted * along)],
        value.shape[1],
    )


def residual_of(residual, alpha, image):
    return residual - alpha * image


def second_data_kernel(blocks, count, *refs):
    low, high, rows_pick, source_pair, scale, data_weight, predicted, sums = refs[:8]
    parts = refs[8 : 8 + count]
    outs, scalars = refs[8 + count : -1], refs[-1]
    data_rows = data_weight.shape[0]
    whole_part = total_rows(parts)
    norm = whole(whole_part[data_rows : data_rows + 1, :])
    beta = norm / whole(sums[0:1, :])
    curve = whole(
        whole_part[data_rows + 1 : data_rows + 2, :]
        + 2.0 * beta * whole_part[data_rows + 2 : data_rows + 3, :]
        + beta * beta * sums[1:2, :]
    )
    total = whole_part[:data_rows, :] + beta * predicted[...]
    data = (data_weight[...] * (0.0 - total)).astype(BF16)
    terms = products(kept_tiles(low, high), pick(rows_pick[...], data))
    cells = gather(source_pair[...], scale[...], terms)
    curved = columns(total * data.astype(F32))
    for group, out in enumerate(outs):
        out[:blocks, :] = cells[group * blocks : (group + 1) * blocks, :]
        out[blocks:, :] = jnp.broadcast_to(curved, (out.shape[0] - blocks, total.shape[1]))
    wide = (1, scalars.shape[1])
    scalars[...] = pack_rows(
        [jnp.broadcast_to(value, wide) for value in (norm, beta, curve)], scalars.shape[1]
    )


def last_kernel(blocks, count, *refs):
    weight, start, first, second, step, scalars = refs[:6]
    parts = refs[6 : 6 + count]
    model, residual = refs[6 + count :]
    norm = scalars[0:1, 0:1]
    beta = scalars[1:2, 0:1]
    curve = scalars[2:3, 0:1]
    along = first[:blocks, :]
    left = second[:blocks, :]
    direction = left + beta * along
    whole_part = total_rows(parts)
    image = weight[:blocks, :] * direction - whole_part[:blocks, :]
    alpha = norm / (curve - whole(whole_part[blocks : blocks + 1, :]))
    model[...] = start[:blocks, :] + step[0:1, 0:1] * along + alpha * direction
    residual[...] = left - alpha * image


def call(body, outs, *args, scratch=()):
    specs = []
    for arg in args:
        far = getattr(jax.typeof(arg), "memory_space", None) == pltpu.HBM
        space = pl.ANY if far else pltpu.SMEM if arg.ndim == 1 else pltpu.VMEM
        specs.append(pl.BlockSpec(memory_space=space))
    return pl.pallas_call(
        body,
        out_shape=[jax.ShapeDtypeStruct(shape, dtype) for shape, dtype in outs],
        in_specs=specs,
        out_specs=[pl.BlockSpec(memory_space=pltpu.VMEM)] * len(outs),
        scratch_shapes=list(scratch),
        compiler_params=pltpu.CompilerParams(vmem_limit_bytes=LIMIT),
    )(*args)


def shards(
    tile_codes,
    tile_scale,
    tile_row,
    tile_column,
    send_index,
    model_start,
    reg_weight,
    observed,
    data_weight,
):
    blocks, width = model_start.shape
    slots = send_index.shape[2]
    data_rows = observed.shape[0]
    tiles = tile_codes.shape[0]
    count = lax.axis_size("tiles")
    sharing = lax.axis_size(("split", "depth"))
    cells = count * blocks
    half = tiles // 2
    loaded = tiles * 3 // 4
    codes = pltpu.with_memory_space_constraint(tile_codes, pltpu.HBM)
    place = lax.axis_index("tiles").astype(jnp.int32).reshape(1)

    order = [0] + sorted(range(1, count), key=lambda shift: (shift != 1, -abs(2 * shift - count)))

    def across(values):
        parts = exchange(values, "tiles", count)
        return [parts[shift] for shift in order]

    def within(value):
        return exchange([value] * sharing, ("split", "depth"), sharing)

    named = jnp.transpose(send_index, (0, 2, 1)).reshape(slots, count)
    (opening,) = call(
        opening_kernel,
        [((2 * blocks + EXTRA, width), F32)],
        pltpu.with_memory_space_constraint(model_start, pltpu.HBM),
        pltpu.with_memory_space_constraint(reg_weight, pltpu.HBM),
        pltpu.with_memory_space_constraint(named, pltpu.HBM),
        scratch=[
            pltpu.VMEM((blocks, width), F32),
            pltpu.VMEM((blocks, width), F32),
            pltpu.VMEM((slots, count), jnp.int32),
            pltpu.SemaphoreType.DMA((3,)),
        ],
    )
    begin = across([opening] * count)
    low, rows_pick, rows_pair, scale = call(
        loading_kernel,
        [
            ((loaded, width, width), BF16),
            ((tiles, data_rows), BF16),
            ((data_rows, 2 * tiles), BF16),
            ((tiles, width), F32),
        ],
        codes,
        opening,
        pltpu.with_memory_space_constraint(tile_scale.reshape(1, -1), pltpu.HBM),
        pltpu.with_memory_space_constraint(tile_row.reshape(1, -1), pltpu.HBM),
        scratch=[
            pltpu.VMEM((1, tiles), F32),
            pltpu.VMEM((1, tiles), jnp.int32),
            pltpu.SemaphoreType.DMA((loaded // CHUNK,)),
            pltpu.SemaphoreType.DMA((2,)),
        ],
    )
    part, high, source_pick, source_pair, start, weight = call(
        functools.partial(first_kernel, blocks, slots, order),
        [
            ((data_rows, width), F32),
            ((tiles - loaded, width, width), BF16),
            ((tiles, cells), BF16),
            ((cells, 2 * tiles), BF16),
            ((cells, width), F32),
            ((cells, width), F32),
        ],
        codes,
        low,
        scale,
        rows_pair,
        tile_column.reshape(1, -1),
        place,
        *begin,
        scratch=[pltpu.SemaphoreType.DMA(((tiles - loaded) // CHUNK,))],
    )
    parts = within(part)

    def turned_half(first, part):
        (turned,) = call(
            functools.partial(turning_kernel, first),
            [((half, width, width), BF16)],
            low,
            high,
            part,
        )
        return turned

    early = turned_half(0, part)
    (part,) = call(
        functools.partial(start_data_kernel, sharing),
        [((cells, width), F32)],
        low,
        high,
        rows_pick,
        source_pair,
        scale,
        observed,
        data_weight,
        early,
        *parts,
    )
    parts = across([part] * count)
    late = turned_half(half, part)
    part, first = call(
        functools.partial(start_residual_kernel, blocks, order),
        [((data_rows + EXTRA, width), F32), ((cells, width), F32)],
        early,
        late,
        source_pick,
        rows_pair,
        scale,
        start,
        weight,
        *parts,
    )
    part, predicted, sums = call(
        functools.partial(image_data_kernel, sharing),
        [((cells + EXTRA, width), F32), ((data_rows, width), F32), ((EXTRA, width), F32)],
        low,
        high,
        rows_pick,
        source_pair,
        scale,
        data_weight,
        *within(part),
    )
    part, second, step = call(
        functools.partial(residual_kernel, blocks, order),
        [((data_rows + EXTRA, width), F32), ((cells, width), F32), ((8, 128), F32)],
        early,
        late,
        source_pick,
        rows_pair,
        scale,
        weight,
        first,
        sums,
        *across([part] * count),
    )
    *part, scalars = call(
        functools.partial(second_data_kernel, blocks, sharing),
        [((blocks + 4, width), F32)] * count + [((EXTRA, width), F32)],
        low,
        high,
        rows_pick,
        source_pair,
        scale,
        data_weight,
        predicted,
        sums,
        *within(part),
    )
    model, residual = call(
        functools.partial(last_kernel, blocks, count),
        [((blocks, width), F32), ((blocks, width), F32)],
        weight,
        start,
        first,
        second,
        step,
        scalars,
        *[part[0]] + across(part)[:0:-1],
    )
    return (model, residual)


def solution(mesh):
    both = P(("groups", "tiles", "split", "depth"))
    owned = P(("groups", "tiles", "split", "depth"), None)
    wide = P(("groups", "tiles", "split", "depth"), None, None)
    data = P(("groups", "tiles"), None)
    in_specs = (wide, both, both, both, wide, owned, owned, data, data)
    return jax.shard_map(
        shards, mesh=mesh, in_specs=in_specs, out_specs=(owned, owned), check_vma=False
    )
```

```python
import functools

import jax
import jax.numpy as jnp
from jax import lax
from jax.experimental import pallas as pl
from jax.experimental.pallas import tpu as pltpu
from jax.sharding import PartitionSpec as P

HIGH = lax.Precision.HIGHEST
EXTRA = 8
LIMIT = 16 * 1024 * 1024
GROUP = 16
CHUNK = 8
F32 = jnp.float32
BF16 = jnp.bfloat16


def exchange(values, axes, size):
    parts = [values[0]] + [None] * (size - 1)
    for shift in range(size - 1, 0, -1):
        perm = [(i, i ^ shift) for i in range(size)]
        parts[shift] = lax.ppermute(values[shift], axes, perm)
    return parts


def by_shift(order, parts):
    return [part for _, part in sorted(zip(order, parts), key=lambda pair: pair[0])]


def total_rows(parts):
    total = parts[0][...]
    for part in parts[1:]:
        total = total + part[...]
    return total


def total_blocks(parts, blocks):
    count = len(parts)
    groups = []
    for group in range(count):
        total = None
        for shift in range(count):
            start = (group ^ shift) * blocks
            piece = parts[shift][start : start + blocks, :]
            total = piece if total is None else total + piece
        groups.append(total)
    return jnp.concatenate(groups, axis=0)


def extra_rows(parts, start):
    total = parts[0][start : start + EXTRA, :]
    for part in parts[1:]:
        total = total + part[start : start + EXTRA, :]
    return total


def whole(value):
    return jnp.sum(value, axis=(0, 1), keepdims=True)


def columns(value):
    return jnp.sum(value, axis=0, keepdims=True)


def pack_rows(rows, width):
    filled = list(rows)
    while len(filled) < EXTRA:
        filled.append(jnp.zeros((1, width), F32))
    return jnp.concatenate(filled, axis=0)


def products(tile_of, picked):
    tiles, width = picked.shape
    index = lax.broadcasted_iota(jnp.int32, (GROUP, width), 0)
    pieces = []
    for first in range(0, tiles, GROUP):
        rows = picked[first : first + GROUP, :]
        total = None
        for i in range(GROUP):
            tile, turn = tile_of(first + i)
            dims = (((1,), (1 if turn else 0,)), ((), ()))
            value = lax.dot_general(rows, tile, dims, preferred_element_type=F32)
            total = value if total is None else jnp.where(index == i, value, total)
        pieces.append(total)
    return jnp.concatenate(pieces, axis=0)


def kept_tiles(low, high):
    count = low.shape[0]
    return lambda k: (low[k], False) if k < count else (high[k - count], False)


def pick(table, values):
    return jnp.dot(table, values, preferred_element_type=F32).astype(BF16)


def gather(table, scale, terms):
    scaled = scale * terms
    upper = scaled.astype(BF16)
    lower = (scaled - upper.astype(F32)).astype(BF16)
    both = jnp.concatenate([upper, lower], axis=0)
    return jnp.dot(table, both, preferred_element_type=F32)


def tables(index, values, picks, pairs):
    tiles = index.shape[1]
    hits = lax.broadcasted_iota(jnp.int32, (values, tiles), 0) == index
    ones = jnp.where(hits, 1.0, 0.0)
    picks[...] = ones.T.astype(BF16)
    pairs[...] = jnp.concatenate([ones, ones], axis=1).astype(BF16)


def chunk_copies(codes, first, kept, done):
    copies = []
    for chunk in range(kept.shape[0] // CHUNK):
        source = codes.at[pl.ds(first + chunk * CHUNK, CHUNK)]
        target = kept.at[pl.ds(chunk * CHUNK, CHUNK)]
        copies.append(pltpu.make_async_copy(source, target, done.at[chunk]))
        copies[-1].start()
    return copies


def loading_kernel(far_codes, opening, far_scale, far_row, *refs):
    low, rows_pick, rows_pair, wide_scale, scale, row, done, small = refs
    near = [
        pltpu.make_async_copy(far_scale, scale, small.at[0]),
        pltpu.make_async_copy(far_row, row, small.at[1]),
    ]
    for copy in near:
        copy.start()
    tiles, width = wide_scale.shape
    copies = chunk_copies(far_codes, 0, low, done)
    for copy in near:
        copy.wait()
    tables(row[...], rows_pick.shape[1], rows_pick, rows_pair)
    square = (tiles, tiles)
    same = lax.broadcasted_iota(jnp.int32, square, 0) == lax.broadcasted_iota(jnp.int32, square, 1)
    wide_scale[...] = jnp.dot(
        jnp.where(same, scale[...], 0.0),
        jnp.ones((tiles, width), F32),
        precision=HIGH,
        preferred_element_type=F32,
    )
    for copy in copies:
        copy.wait()


def turning_kernel(first, low, high, part, turned):
    tile_of = kept_tiles(low, high)
    for k in range(turned.shape[0]):
        tile, _ = tile_of(first + k)
        turned[k] = tile.T


def opening_kernel(start, weight, named, out, sources, weights, names, done):
    copies = [
        pltpu.make_async_copy(start, sources, done.at[0]),
        pltpu.make_async_copy(weight, weights, done.at[1]),
        pltpu.make_async_copy(named, names, done.at[2]),
    ]
    for copy in copies:
        copy.start()
    blocks, width = sources.shape
    slots, count = names.shape
    rest = out.shape[0] - 2 * blocks
    out[2 * blocks :, :] = jnp.zeros((rest, width), F32)
    for copy in copies:
        copy.wait()
    out[:blocks, :] = sources[...]
    out[blocks : 2 * blocks, :] = weights[...]
    out[2 * blocks : 2 * blocks + slots, :count] = names[...].astype(F32)


def first_kernel(blocks, slots, order, *refs):
    far_codes, low, scale, rows_pair, column, place = refs[:6]
    count = len(order)
    parts = by_shift(order, refs[6 : 6 + count])
    out, high, source_pick, source_pair, start, weight, done = refs[6 + count :]
    loaded = low.shape[0]
    copies = chunk_copies(far_codes, loaded, high, done)
    width = out.shape[1]
    here = place[0]
    columns_of = column[...]
    source = jnp.where(columns_of < blocks, columns_of, 0)
    lane = lax.broadcasted_iota(jnp.int32, (1, width), 1)
    for shift in range(count):
        other = jnp.bitwise_xor(here, shift)
        for slot in range(slots):
            named = parts[shift][2 * blocks + slot : 2 * blocks + slot + 1, :]
            mine = jnp.where(lane == here, named, 0.0)
            block = jnp.sum(mine, axis=1, keepdims=True).astype(jnp.int32) + shift * blocks
            source = jnp.where(columns_of == blocks + other * slots + slot, block, source)
    tables(source, count * blocks, source_pick, source_pair)
    field = jnp.concatenate([part[:blocks, :] for part in parts], axis=0)
    start[...] = field
    weight[...] = jnp.concatenate([part[blocks : 2 * blocks, :] for part in parts], axis=0)


    def tile_of(k):
        if k < loaded:
            return low[k], True
        if (k - loaded) % CHUNK == 0:
            copies[(k - loaded) // CHUNK].wait()
        return high[k - loaded], True

    terms = products(tile_of, pick(source_pick[...], field.astype(BF16)))
    out[...] = gather(rows_pair[...], scale[...], terms)


def start_data_kernel(count, *refs):
    low, high, rows_pick, source_pair, scale, observed, data_weight, turned = refs[:8]
    parts = refs[8 : 8 + count]
    out = refs[8 + count]
    total = total_rows(parts)
    data = (data_weight[...] * (observed[...] - total)).astype(BF16)
    terms = products(kept_tiles(low, high), pick(rows_pick[...], data))
    out[...] = gather(source_pair[...], scale[...], terms)


def start_residual_kernel(blocks, order, *refs):
    count = len(order)
    early, late, source_pick, rows_pair, scale, start, weight = refs[:7]
    parts = by_shift(order, refs[7 : 7 + count])
    out, residual = refs[7 + count :]
    weights = weight[...]
    value = total_blocks(parts, blocks) - weights * start[...]
    residual[...] = value
    terms = products(kept_tiles(early, late), pick(source_pick[...], value.astype(BF16)))
    data_rows = rows_pair.shape[0]
    out[:data_rows, :] = gather(rows_pair[...], scale[...], terms)
    out[data_rows:, :] = pack_rows(
        [columns(value * value), columns(value * weights * value)], value.shape[1]
    )


def image_data_kernel(count, *refs):
    low, high, rows_pick, source_pair, scale, data_weight = refs[:6]
    parts = refs[6 : 6 + count]
    out, predicted, sums = refs[6 + count :]
    data_rows = data_weight.shape[0]
    whole_part = total_rows(parts)
    total = whole_part[:data_rows, :]
    predicted[...] = total
    sums[...] = whole_part[data_rows:, :]
    data = (data_weight[...] * (0.0 - total)).astype(BF16)
    terms = products(kept_tiles(low, high), pick(rows_pick[...], data))
    cells = source_pair.shape[0]
    out[:cells, :] = gather(source_pair[...], scale[...], terms)
    out[cells:, :] = pack_rows([columns(total * data.astype(F32))], total.shape[1])


def residual_kernel(blocks, order, *refs):
    count = len(order)
    early, late, source_pick, rows_pair, scale, weight, direction, sums = refs[:8]
    parts = by_shift(order, refs[8 : 8 + count])
    out, residual, step = refs[8 + count :]
    cells = source_pick.shape[1]
    weights = weight[...]
    along = direction[...]
    image = weights * along - total_blocks(parts, blocks)
    curve = whole(sums[1:2, :]) - whole(extra_rows(parts, cells)[0:1, :])
    alpha = whole(sums[0:1, :]) / curve
    step[...] = jnp.broadcast_to(alpha, step.shape)
    value = residual_of(along, alpha, image)
    residual[...] = value
    terms = products(kept_tiles(early, late), pick(source_pick[...], value.astype(BF16)))
    data_rows = rows_pair.shape[0]
    out[:data_rows, :] = gather(rows_pair[...], scale[...], terms)
    weighted = value * weights
    out[data_rows:, :] = pack_rows(
        [columns(value * value), columns(weighted * value), columns(weighted * along)],
        value.shape[1],
    )


def residual_of(residual, alpha, image):
    return residual - alpha * image


def second_data_kernel(blocks, count, *refs):
    low, high, rows_pick, source_pair, scale, data_weight, predicted, sums = refs[:8]
    parts = refs[8 : 8 + count]
    outs, scalars = refs[8 + count : -1], refs[-1]
    data_rows = data_weight.shape[0]
    whole_part = total_rows(parts)
    norm = whole(whole_part[data_rows : data_rows + 1, :])
    beta = norm / whole(sums[0:1, :])
    curve = whole(
        whole_part[data_rows + 1 : data_rows + 2, :]
        + 2.0 * beta * whole_part[data_rows + 2 : data_rows + 3, :]
        + beta * beta * sums[1:2, :]
    )
    total = whole_part[:data_rows, :] + beta * predicted[...]
    data = (data_weight[...] * (0.0 - total)).astype(BF16)
    terms = products(kept_tiles(low, high), pick(rows_pick[...], data))
    cells = gather(source_pair[...], scale[...], terms)
    curved = columns(total * data.astype(F32))
    for group, out in enumerate(outs):
        out[:blocks, :] = cells[group * blocks : (group + 1) * blocks, :]
        out[blocks:, :] = jnp.broadcast_to(curved, (out.shape[0] - blocks, total.shape[1]))
    wide = (1, scalars.shape[1])
    scalars[...] = pack_rows(
        [jnp.broadcast_to(value, wide) for value in (norm, beta, curve)], scalars.shape[1]
    )


def last_kernel(blocks, count, *refs):
    weight, start, first, second, step, scalars = refs[:6]
    parts = refs[6 : 6 + count]
    model, residual = refs[6 + count :]
    norm = scalars[0:1, 0:1]
    beta = scalars[1:2, 0:1]
    curve = scalars[2:3, 0:1]
    along = first[:blocks, :]
    left = second[:blocks, :]
    direction = left + beta * along
    whole_part = total_rows(parts)
    image = weight[:blocks, :] * direction - whole_part[:blocks, :]
    alpha = norm / (curve - whole(whole_part[blocks : blocks + 1, :]))
    model[...] = start[:blocks, :] + step[0:1, 0:1] * along + alpha * direction
    residual[...] = left - alpha * image


def call(body, outs, *args, scratch=()):
    specs = []
    for arg in args:
        far = getattr(jax.typeof(arg), "memory_space", None) == pltpu.HBM
        space = pl.ANY if far else pltpu.SMEM if arg.ndim == 1 else pltpu.VMEM
        specs.append(pl.BlockSpec(memory_space=space))
    return pl.pallas_call(
        body,
        out_shape=[jax.ShapeDtypeStruct(shape, dtype) for shape, dtype in outs],
        in_specs=specs,
        out_specs=[pl.BlockSpec(memory_space=pltpu.VMEM)] * len(outs),
        scratch_shapes=list(scratch),
        compiler_params=pltpu.CompilerParams(vmem_limit_bytes=LIMIT),
    )(*args)


def shards(
    tile_codes,
    tile_scale,
    tile_row,
    tile_column,
    send_index,
    model_start,
    reg_weight,
    observed,
    data_weight,
):
    blocks, width = model_start.shape
    slots = send_index.shape[2]
    data_rows = observed.shape[0]
    tiles = tile_codes.shape[0]
    count = lax.axis_size("tiles")
    sharing = lax.axis_size(("split", "depth"))
    cells = count * blocks
    half = tiles // 2
    loaded = tiles * 3 // 4
    codes = pltpu.with_memory_space_constraint(tile_codes, pltpu.HBM)
    place = lax.axis_index("tiles").astype(jnp.int32).reshape(1)

    order = [0] + sorted(range(1, count), key=lambda shift: (shift != 1, -abs(2 * shift - count)))

    far = list(range(count))

    def across(values, order):
        parts = exchange(values, "tiles", count)
        return [parts[shift] for shift in order]

    def within(value):
        return exchange([value] * sharing, ("split", "depth"), sharing)

    named = jnp.transpose(send_index, (0, 2, 1)).reshape(slots, count)
    (opening,) = call(
        opening_kernel,
        [((2 * blocks + EXTRA, width), F32)],
        pltpu.with_memory_space_constraint(model_start, pltpu.HBM),
        pltpu.with_memory_space_constraint(reg_weight, pltpu.HBM),
        pltpu.with_memory_space_constraint(named, pltpu.HBM),
        scratch=[
            pltpu.VMEM((blocks, width), F32),
            pltpu.VMEM((blocks, width), F32),
            pltpu.VMEM((slots, count), jnp.int32),
            pltpu.SemaphoreType.DMA((3,)),
        ],
    )
    begin = across([opening] * count, order)
    low, rows_pick, rows_pair, scale = call(
        loading_kernel,
        [
            ((loaded, width, width), BF16),
            ((tiles, data_rows), BF16),
            ((data_rows, 2 * tiles), BF16),
            ((tiles, width), F32),
        ],
        codes,
        opening,
        pltpu.with_memory_space_constraint(tile_scale.reshape(1, -1), pltpu.HBM),
        pltpu.with_memory_space_constraint(tile_row.reshape(1, -1), pltpu.HBM),
        scratch=[
            pltpu.VMEM((1, tiles), F32),
            pltpu.VMEM((1, tiles), jnp.int32),
            pltpu.SemaphoreType.DMA((loaded // CHUNK,)),
            pltpu.SemaphoreType.DMA((2,)),
        ],
    )
    part, high, source_pick, source_pair, start, weight = call(
        functools.partial(first_kernel, blocks, slots, order),
        [
            ((data_rows, width), F32),
            ((tiles - loaded, width, width), BF16),
            ((tiles, cells), BF16),
            ((cells, 2 * tiles), BF16),
            ((cells, width), F32),
            ((cells, width), F32),
        ],
        codes,
        low,
        scale,
        rows_pair,
        tile_column.reshape(1, -1),
        place,
        *begin,
        scratch=[pltpu.SemaphoreType.DMA(((tiles - loaded) // CHUNK,))],
    )
    parts = within(part)

    def turned_half(first, part):
        (turned,) = call(
            functools.partial(turning_kernel, first),
            [((half, width, width), BF16)],
            low,
            high,
            part,
        )
        return turned

    early = turned_half(0, part)
    (part,) = call(
        functools.partial(start_data_kernel, sharing),
        [((cells, width), F32)],
        low,
        high,
        rows_pick,
        source_pair,
        scale,
        observed,
        data_weight,
        early,
        *parts,
    )
    parts = across([part] * count, far)
    late = turned_half(half, part)
    part, first = call(
        functools.partial(start_residual_kernel, blocks, far),
        [((data_rows + EXTRA, width), F32), ((cells, width), F32)],
        early,
        late,
        source_pick,
        rows_pair,
        scale,
        start,
        weight,
        *parts,
    )
    part, predicted, sums = call(
        functools.partial(image_data_kernel, sharing),
        [((cells + EXTRA, width), F32), ((data_rows, width), F32), ((EXTRA, width), F32)],
        low,
        high,
        rows_pick,
        source_pair,
        scale,
        data_weight,
        *within(part),
    )
    part, second, step = call(
        functools.partial(residual_kernel, blocks, far),
        [((data_rows + EXTRA, width), F32), ((cells, width), F32), ((8, 128), F32)],
        early,
        late,
        source_pick,
        rows_pair,
        scale,
        weight,
        first,
        sums,
        *across([part] * count, far),
    )
    *part, scalars = call(
        functools.partial(second_data_kernel, blocks, sharing),
        [((blocks + 4, width), F32)] * count + [((EXTRA, width), F32)],
        low,
        high,
        rows_pick,
        source_pair,
        scale,
        data_weight,
        predicted,
        sums,
        *within(part),
    )
    model, residual = call(
        functools.partial(last_kernel, blocks, count),
        [((blocks, width), F32), ((blocks, width), F32)],
        weight,
        start,
        first,
        second,
        step,
        scalars,
        *[part[0]] + across(part, order)[:0:-1],
    )
    return (model, residual)


def solution(mesh):
    both = P(("groups", "tiles", "split", "depth"))
    owned = P(("groups", "tiles", "split", "depth"), None)
    wide = P(("groups", "tiles", "split", "depth"), None, None)
    data = P(("groups", "tiles"), None)
    in_specs = (wide, both, both, both, wide, owned, owned, data, data)
    return jax.shard_map(
        shards, mesh=mesh, in_specs=in_specs, out_specs=(owned, owned), check_vma=False
    )
```
